32 devices in a mesh: dp: 8 (over z, x), blk: 4 (over y, core).
Axes of the slice: x: 2, y: 2, z: 4, core: 2. Of those that a mesh axis runs over, the one named last changes fastest.
Arguments:
- tokens: bfloat16 [8192, 768], P(('dp', 'blk')), may hold values from -6 to 6
- cotangent: bfloat16 [8192, 768], P(('dp', 'blk')), may hold values from -6 to 6
- doc_lengths: int32 [8, 1], P('dp'), may hold values from 0 to 1024, as said below
- w_qkv: bfloat16 [768, 2304], P(('dp', 'blk')), may hold values from -0.21875 to 0.21875
- w_out: bfloat16 [768, 768], P(('dp', 'blk')), may hold values from -0.21875 to 0.21875
- w_up: bfloat16 [768, 3072], P(('dp', 'blk')), may hold values from -0.21875 to 0.21875
- w_down: bfloat16 [3072, 768], P(('dp', 'blk')), may hold values from -0.109375 to 0.109375
- ln1_gain: bfloat16 [768], P(('dp', 'blk')), may hold values from 0.099609375 to 1.8984375
- ln1_bias: bfloat16 [768], P(('dp', 'blk')), may hold values from -1.5 to 1.5
- ln2_gain: bfloat16 [768], P(('dp', 'blk')), may hold values from 0.099609375 to 1.8984375
- ln2_bias: bfloat16 [768], P(('dp', 'blk')), may hold values from -1.5 to 1.5
- ln3_gain: bfloat16 [768], P(('dp', 'blk')), may hold values from 0.099609375 to 1.8984375
- ln3_bias: bfloat16 [768], P(('dp', 'blk')), may hold values from -1.5 to 1.5
- ln4_gain: bfloat16 [3072], P(('dp', 'blk')), may hold values from 0.099609375 to 1.8984375
- ln4_bias: bfloat16 [3072], P(('dp', 'blk')), may hold values from -1.5 to 1.5
Outputs:
- output: bfloat16 [8192, 768], P(('dp', 'blk'))
- input_grad: bfloat16 [8192, 768], P(('dp', 'blk'))
- grad_w_qkv: float32 [768, 2304], P(('dp', 'blk'))
- grad_w_out: float32 [768, 768], P(('dp', 'blk'))
- grad_w_up: float32 [768, 3072], P(('dp', 'blk'))
- grad_w_down: float32 [3072, 768], P(('dp', 'blk'))
- grad_ln1_gain: float32 [768], P(('dp', 'blk'))
- grad_ln1_bias: float32 [768], P(('dp', 'blk'))
- grad_ln2_gain: float32 [768], P(('dp', 'blk'))
- grad_ln2_bias: float32 [768], P(('dp', 'blk'))
- grad_ln3_gain: float32 [768], P(('dp', 'blk'))
- grad_ln3_bias: float32 [768], P(('dp', 'blk'))
- grad_ln4_gain: float32 [3072], P(('dp', 'blk'))
- grad_ln4_bias: float32 [3072], P(('dp', 'blk'))
The draws below stay inside these ranges and needn't reach their ends.
Inputs may be any that keep to these rules, and one draw needn't show every extreme that they name: `doc_lengths`: each row sums to 1024. A row either holds documents of min(2048, 1024) tokens followed by zeros, or documents of min(1024, 1024) tokens followed by zeros; 4 rows are of the first kind, which ones varies.
All inputs are finite; a program needn't handle non-finite values.
Results may differ from the reference program's by a relative error of at most 0.018.
Values may be sent and summed in bfloat16 or wider, within the bound.
No kernel may reach another device: no remote copies, remote signals or barrier semaphores. Data moves between devices by JAX's collectives and lax.ppermute only.
A program may use at most 128 MiB of HBM per device.

```python
import math
import jax
import jax.numpy as jnp
from jax import lax

D = 768
HEADS = 12
HEAD_DIM = 64
FF = 3072
TOK_DEV = 256
SHORT_LEN = 1024
LONG_LEN = 2048
GROUP_TOK = 1024
DOCS_MAX = 1
TOKENS = 8192
N_DP = 8
N_BLK = 4


def draw_doc_lengths(key, part):
    key = jax.random.fold_in(key, 7)
    long_len = min(LONG_LEN, GROUP_TOK)
    short_len = min(SHORT_LEN, GROUP_TOK)
    order = jax.random.permutation(key, N_DP)
    is_long = order < N_DP // 2
    column = jnp.arange(DOCS_MAX, dtype=jnp.int32)
    long_row = jnp.where(column < GROUP_TOK // long_len, long_len, 0)
    short_row = jnp.where(column < GROUP_TOK // short_len, short_len, 0)
    return jnp.where(is_long[:, None], long_row[None, :], short_row[None, :]).astype(jnp.int32)


def level_of(key, dims, split, smallest, top_value):
    loudness = 1.0
    for dim, blocks in split:
        draws = jax.random.uniform(jax.random.fold_in(jax.random.fold_in(key, 6), dim), (blocks,), jnp.float32, smallest / len(split), top_value / len(split))
        loudness = loudness * jnp.repeat(jnp.exp(draws), dims[dim] // blocks).reshape((-1,) + (1,) * (len(dims) - 1 - dim))
    return loudness


def scatter_about(own_key, shape, scale, reach, split=(), kind=jnp.bfloat16):
    values = scale * jax.random.normal(own_key, shape, jnp.float32)
    if split:
        values = values * level_of(own_key, shape, split, -0.22, 0.18)
    return jnp.clip(values, -reach, reach).astype(kind)


def setup_inputs(seed: int = 0) -> dict:
    keys = jax.random.split(jax.random.key(seed), 16)
    tokens = scatter_about(keys[0], (TOKENS, D), 1.0, 6.0, ((0, 32),))
    cotangent = scatter_about(keys[1], (TOKENS, D), 1.0, 6.0, ((0, 32),))
    doc_lengths = draw_doc_lengths(jax.random.fold_in(keys[15], 71), 0)
    w_qkv = scatter_about(keys[3], (D, 3 * D), D ** -0.5, 0.21875, ((0, 32),))
    w_out = scatter_about(keys[4], (D, D), D ** -0.5, 0.21875, ((0, 32),))
    w_up = scatter_about(keys[5], (D, FF), D ** -0.5, 0.21875, ((0, 32),))
    w_down = scatter_about(keys[6], (FF, D), FF ** -0.5, 0.109375, ((0, 32),))
    ln1_gain = jnp.clip(1.0 + 0.18 * jax.random.normal(keys[7], (D,), jnp.float32), 0.099609375, 1.8984375).astype(jnp.bfloat16)
    ln1_bias = scatter_about(keys[8], (D,), 0.3, 1.5, ((0, 32),))
    ln2_gain = jnp.clip(1.0 + 0.18 * jax.random.normal(keys[9], (D,), jnp.float32), 0.099609375, 1.8984375).astype(jnp.bfloat16)
    ln2_bias = scatter_about(keys[10], (D,), 0.3, 1.5, ((0, 32),))
    ln3_gain = jnp.clip(1.0 + 0.18 * jax.random.normal(keys[11], (D,), jnp.float32), 0.099609375, 1.8984375).astype(jnp.bfloat16)
    ln3_bias = scatter_about(keys[12], (D,), 0.3, 1.5, ((0, 32),))
    ln4_gain = jnp.clip(1.0 + 0.18 * jax.random.normal(keys[13], (FF,), jnp.float32), 0.099609375, 1.8984375).astype(jnp.bfloat16)
    ln4_bias = scatter_about(keys[14], (FF,), 0.3, 1.5, ((0, 32),))
    return dict(tokens=tokens, cotangent=cotangent, doc_lengths=doc_lengths, w_qkv=w_qkv, w_out=w_out, w_up=w_up, w_down=w_down, ln1_gain=ln1_gain, ln1_bias=ln1_bias, ln2_gain=ln2_gain, ln2_bias=ln2_bias, ln3_gain=ln3_gain, ln3_bias=ln3_bias, ln4_gain=ln4_gain, ln4_bias=ln4_bias)


epsilon = 1e-05
masked_score = -1000000000.0

@jax.custom_vjp
def low(v):
    return lax.optimization_barrier(v.astype(jnp.bfloat16)).astype(jnp.float32)

@jax.custom_vjp
def low_back(v):
    return v

def low_keep(v):
    return (low(v), None)

def low_pass(kept, grad):
    return (grad,)

def back_keep(v):
    return (v, None)

def back_low(kept, grad):
    return (low(grad),)
low.defvjp(low_keep, low_pass)
low_back.defvjp(back_keep, back_low)

def product(first_operand, second_operand):
    return jnp.dot(first_operand, second_operand, precision=lax.Precision.HIGHEST, preferred_element_type=jnp.float32)

def layer_norm(values, norm_gain, norm_bias):
    centre = lax.optimization_barrier(jnp.mean(values, -1, keepdims=True))
    centred = values - centre
    spread = lax.optimization_barrier(jnp.mean(centred * centred, -1, keepdims=True))
    return centred * lax.rsqrt(spread + epsilon) * norm_gain + norm_bias

def doc_place(row_ids, doc_row, row_count, blocks):
    device = row_ids // row_count
    local = row_ids % row_count
    shares = doc_row // blocks
    ends = jnp.cumsum(shares, dtype=jnp.int32)
    starts = ends - shares
    doc = lax.optimization_barrier(jnp.sum((local[:, None] >= ends[None, :]).astype(jnp.int32), -1, dtype=jnp.int32))
    pick = (doc[:, None] == jnp.arange(doc_row.shape[0], dtype=jnp.int32)[None, :]).astype(jnp.int32)
    share_of = lax.optimization_barrier(jnp.sum(pick * shares[None, :], -1, dtype=jnp.int32))
    start_of = lax.optimization_barrier(jnp.sum(pick * starts[None, :], -1, dtype=jnp.int32))
    return (doc, device * share_of + local - start_of)

def attend(queries, keys_all, values_all, doc, place):
    block_rows = math.gcd(GROUP_TOK, 512)
    blocks = GROUP_TOK // block_rows
    key_heads = keys_all.reshape(GROUP_TOK, HEADS, HEAD_DIM)
    value_heads = values_all.reshape(GROUP_TOK, HEADS, HEAD_DIM)

    def one_block(element):
        query_block, block_doc, block_place = element
        query_heads = query_block.reshape(block_rows, HEADS, HEAD_DIM)
        scores = jnp.einsum('qhd,khd->hqk', query_heads, key_heads, precision=lax.Precision.HIGHEST) * HEAD_DIM ** (-0.5)
        scores = low_back(scores)
        allowed = (block_doc[:, None] == doc[None, :]) & (place[None, :] <= block_place[:, None])
        scores = jnp.where(allowed[None], scores, masked_score)
        weights = jnp.exp(scores - lax.optimization_barrier(jnp.max(scores, -1, keepdims=True)))
        weights = low(weights / lax.optimization_barrier(jnp.sum(weights, -1, keepdims=True)))
        mixed_heads = jnp.einsum('hqk,khd->qhd', weights, value_heads, precision=lax.Precision.HIGHEST)
        return mixed_heads.reshape(block_rows, D)
    result = lax.map(jax.checkpoint(one_block), (queries.reshape(blocks, block_rows, D), doc.reshape(blocks, block_rows), place.reshape(blocks, block_rows)))
    return result.reshape(GROUP_TOK, D)

def group_forward(group_tokens, doc_row, params):
    qkv_weight, out_weight, up_weight, down_weight, gain_one, bias_one, gain_two, bias_two, gain_three, bias_three, gain_four, bias_four = params
    row_ids = jnp.arange(GROUP_TOK, dtype=jnp.int32)
    doc, place = doc_place(row_ids, doc_row, TOK_DEV, N_BLK)
    normed = low(layer_norm(group_tokens, gain_one, bias_one))
    projected = low_back(low(product(normed, qkv_weight)))
    attended = attend(projected[:, :D], projected[:, D:2 * D], projected[:, 2 * D:], doc, place)
    attended = low_back(attended)
    inner = low(layer_norm(attended, gain_two, bias_two))
    middle = group_tokens + low_back(product(inner, out_weight))
    normed_two = low(layer_norm(middle, gain_three, bias_three))
    up_value = low_back(product(normed_two, up_weight))
    hidden = low(layer_norm(jax.nn.gelu(up_value, approximate=False), gain_four, bias_four))
    return middle + low_back(product(hidden, down_weight))

def reference(tokens, cotangent, doc_lengths, w_qkv, w_out, w_up, w_down, ln1_gain, ln1_bias, ln2_gain, ln2_bias, ln3_gain, ln3_bias, ln4_gain, ln4_bias):
    params = tuple((value.astype(jnp.float32) for value in (w_qkv, w_out, w_up, w_down, ln1_gain, ln1_bias, ln2_gain, ln2_bias, ln3_gain, ln3_bias, ln4_gain, ln4_bias)))
    grouped = tokens.astype(jnp.float32).reshape(N_DP, GROUP_TOK, D)

    def forward(grouped_in, *weights):

        def one_group(unused_state, element):
            group_tokens, doc_row = element
            return (unused_state, group_forward(group_tokens, doc_row, weights))
        _, results = lax.scan(one_group, jnp.zeros((), jnp.float32), (grouped_in, doc_lengths))
        return results
    result, pullback = jax.vjp(forward, grouped, *params)
    grads = pullback(cotangent.astype(jnp.float32).reshape(N_DP, GROUP_TOK, D))
    return (result.reshape(TOKENS, D).astype(jnp.bfloat16), grads[0].reshape(TOKENS, D).astype(jnp.bfloat16), grads[1], grads[2], grads[3], grads[4], grads[5], grads[6], grads[7], grads[8], grads[9], grads[10], grads[11], grads[12])
```

```python
import functools
import math

import jax
import jax.numpy as jnp
from jax import lax
from jax.experimental import pallas as pl
from jax.experimental.pallas import tpu as pltpu
from jax.sharding import PartitionSpec as P

HEADS = 12


epsilon = 1e-05
masked_score = -1000000000.0


def shifted(shard, axis, by):
    devices = lax.axis_size(axis)
    pairs = [(i, i + by) for i in range(devices) if 0 <= i + by < devices]
    return lax.ppermute(shard, axis, pairs)


def shifted_2(value, axis, steps):
    count = lax.axis_size(axis)
    pairs = [(source, (source + steps) % count) for source in range(count)]
    return lax.ppermute(value, axis, pairs)


def layer_norm(values, norm_gain, norm_bias):
    centre = jnp.mean(values, -1, keepdims=True)
    centred = values - centre
    spread = jnp.mean(centred * centred, -1, keepdims=True)
    return centred * lax.rsqrt(spread + epsilon) * norm_gain + norm_bias


def ffn_norm(up_value, norm_gain, norm_bias):
    return layer_norm(jax.nn.gelu(up_value, approximate=False), norm_gain, norm_bias)


def doc_place(row_ids, doc_row, row_count, blocks):
    device = row_ids // row_count
    local = row_ids % row_count
    shares = doc_row // blocks
    ends = jnp.cumsum(shares, dtype=jnp.int32)
    starts = ends - shares
    doc = jnp.sum((local[:, None] >= ends[None, :]).astype(jnp.int32), -1, dtype=jnp.int32)
    pick = (doc[:, None] == jnp.arange(doc_row.shape[0], dtype=jnp.int32)[None, :]).astype(
        jnp.int32
    )
    share_of = jnp.sum(pick * shares[None, :], -1, dtype=jnp.int32)
    start_of = jnp.sum(pick * starts[None, :], -1, dtype=jnp.int32)
    return (doc, device * share_of + local - start_of)


def visible(query_doc, query_place, key_doc, key_place):
    return (query_doc[:, None] == key_doc[None, :]) & (key_place[None, :] <= query_place[:, None])


def outer_sum(first_operand, second_operand):
    return lax.dot_general(
        first_operand, second_operand, (((0,), (0,)), ((), ())), preferred_element_type=jnp.float32
    )


def back_product(gradient, weight):
    return lax.dot_general(
        gradient, weight, (((1,), (1,)), ((), ())), preferred_element_type=jnp.float32
    )


def score_grads(
    query_heads, dout_heads, lse_heads, delta_heads, allowed, key_heads, value_heads, score_scale
):
    scores = (
        jnp.einsum("qhd,khd->hqk", query_heads, key_heads, preferred_element_type=jnp.float32)
        * score_scale
    )
    probabilities = jnp.where(allowed[None], jnp.exp(scores - lse_heads[:, :, None]), 0.0)
    weight_grad = jnp.einsum(
        "qhd,khd->hqk", dout_heads, value_heads, preferred_element_type=jnp.float32
    )
    score_grad = (probabilities * (weight_grad - delta_heads[:, :, None])).astype(jnp.bfloat16)
    return (probabilities.astype(jnp.bfloat16), score_grad)


def general_body(
    tokens,
    cotangent,
    doc_lengths,
    w_qkv,
    w_out,
    w_up,
    w_down,
    ln1_gain,
    ln1_bias,
    ln2_gain,
    ln2_bias,
    ln3_gain,
    ln3_bias,
    ln4_gain,
    ln4_bias,
):
    gathered = (
        lax.all_gather(w_qkv, ("dp", "blk"), axis=0, tiled=True),
        lax.all_gather(w_out, ("dp", "blk"), axis=0, tiled=True),
        lax.all_gather(w_up, ("dp", "blk"), axis=0, tiled=True),
        lax.all_gather(w_down, ("dp", "blk"), axis=0, tiled=True),
        lax.all_gather(ln1_gain, ("dp", "blk"), axis=0, tiled=True),
        lax.all_gather(ln1_bias, ("dp", "blk"), axis=0, tiled=True),
        lax.all_gather(ln2_gain, ("dp", "blk"), axis=0, tiled=True),
        lax.all_gather(ln2_bias, ("dp", "blk"), axis=0, tiled=True),
        lax.all_gather(ln3_gain, ("dp", "blk"), axis=0, tiled=True),
        lax.all_gather(ln3_bias, ("dp", "blk"), axis=0, tiled=True),
        lax.all_gather(ln4_gain, ("dp", "blk"), axis=0, tiled=True),
        lax.all_gather(ln4_bias, ("dp", "blk"), axis=0, tiled=True),
    )
    qkv_full, out_full, up_full, down_full = (gathered[0], gathered[1], gathered[2], gathered[3])
    norm_params = [value.astype(jnp.float32) for value in gathered[4:]]
    gain_one, bias_one, gain_two, bias_two, gain_three, bias_three, gain_four, bias_four = (
        norm_params
    )
    row_count, model_width = tokens.shape
    head_dim = model_width // HEADS
    score_scale = head_dim ** (-0.5)
    doc_row = doc_lengths[0]
    blocks = lax.axis_size("blk")
    place_index = lax.axis_index("blk")
    query_doc, query_place = doc_place(
        place_index * row_count + jnp.arange(row_count, dtype=jnp.int32), doc_row, row_count, blocks
    )

    def key_meta(first_row, count):
        return doc_place(first_row + jnp.arange(count, dtype=jnp.int32), doc_row, row_count, blocks)

    residual_in = tokens.astype(jnp.float32)
    normed = layer_norm(residual_in, gain_one, bias_one).astype(jnp.bfloat16)
    projected = jnp.dot(normed, qkv_full, preferred_element_type=jnp.float32).astype(jnp.bfloat16)
    queries = projected[:, :model_width]
    keys_own = projected[:, model_width : 2 * model_width]
    values_own = projected[:, 2 * model_width :]
    query_heads = queries.reshape(row_count, HEADS, head_dim)
    start_state = (
        jnp.full((HEADS, row_count), masked_score, jnp.float32),
        jnp.zeros((HEADS, row_count), jnp.float32),
        jnp.zeros((HEADS, row_count, head_dim), jnp.float32),
    )
    running = start_state
    key_part = lax.all_gather(keys_own, "blk", axis=0, tiled=True)
    value_part = lax.all_gather(values_own, "blk", axis=0, tiled=True)
    part_rows = key_part.shape[0]
    step_rows = math.gcd(part_rows, 512)
    count = part_rows // step_rows

    def one_step(state, element):
        key_block, value_block, block_start = element
        key_doc, key_place = key_meta(block_start, step_rows)
        allowed = visible(query_doc, query_place, key_doc, key_place)
        scores = (
            jnp.einsum(
                "qhd,khd->hqk",
                query_heads,
                key_block.reshape(step_rows, HEADS, head_dim),
                preferred_element_type=jnp.float32,
            )
            * score_scale
        )
        scores = jnp.where(allowed[None], scores, masked_score)
        peak_old, total_old, weighted_old = state
        peak_new = jnp.maximum(peak_old, jnp.max(scores, -1))
        weights = jnp.where(allowed[None], jnp.exp(scores - peak_new[:, :, None]), 0.0)
        factor = jnp.exp(peak_old - peak_new)
        total_new = total_old * factor + jnp.sum(weights, -1)
        weighted_new = weighted_old * factor[:, :, None] + jnp.einsum(
            "hqk,khd->hqd",
            weights.astype(jnp.bfloat16),
            value_block.reshape(step_rows, HEADS, head_dim),
            preferred_element_type=jnp.float32,
        )
        return ((peak_new, total_new, weighted_new), None)

    starts = jnp.arange(count, dtype=jnp.int32) * step_rows
    running, _ = lax.scan(
        one_step,
        running,
        (
            key_part.reshape(count, step_rows, model_width),
            value_part.reshape(count, step_rows, model_width),
            starts,
        ),
    )
    peak_score, total_weight, weighted_sum = running
    log_total = peak_score + jnp.log(total_weight)
    attended = (
        (weighted_sum / total_weight[:, :, None]).transpose(1, 0, 2).reshape(row_count, model_width)
    )
    inner = layer_norm(attended, gain_two, bias_two).astype(jnp.bfloat16)
    middle = residual_in + jnp.dot(inner, out_full, preferred_element_type=jnp.float32)
    normed_two = layer_norm(middle, gain_three, bias_three).astype(jnp.bfloat16)
    up_value = jnp.dot(normed_two, up_full, preferred_element_type=jnp.float32)
    hidden = ffn_norm(up_value, gain_four, bias_four).astype(jnp.bfloat16)
    output = (middle + jnp.dot(hidden, down_full, preferred_element_type=jnp.float32)).astype(
        jnp.bfloat16
    )
    grad_down = outer_sum(hidden, cotangent)
    d_hidden = back_product(cotangent, down_full)
    _, ffn_pullback = jax.vjp(ffn_norm, up_value, gain_four, bias_four)
    d_up, grad_gain_four, grad_bias_four = ffn_pullback(d_hidden)
    d_up_low = d_up.astype(jnp.bfloat16)
    grad_up = outer_sum(normed_two, d_up_low)
    _, third_pullback = jax.vjp(layer_norm, middle, gain_three, bias_three)
    d_middle_norm, grad_gain_three, grad_bias_three = third_pullback(
        back_product(d_up_low, up_full)
    )
    d_middle = cotangent.astype(jnp.float32) + d_middle_norm
    d_middle_low = d_middle.astype(jnp.bfloat16)
    grad_out = outer_sum(inner, d_middle_low)
    _, second_pullback = jax.vjp(layer_norm, attended, gain_two, bias_two)
    d_attended, grad_gain_two, grad_bias_two = second_pullback(back_product(d_middle_low, out_full))
    d_attended_low = d_attended.astype(jnp.bfloat16)
    dout_heads = d_attended_low.reshape(row_count, HEADS, head_dim)
    delta = jnp.einsum(
        "qhd,qhd->hq",
        d_attended_low.astype(jnp.float32).reshape(row_count, HEADS, head_dim),
        attended.reshape(row_count, HEADS, head_dim),
    )

    def turn(turn_index, loop_state):
        kv_now, grads_now, query_grad = loop_state
        source = (place_index - turn_index) % blocks
        key_doc, key_place = key_meta(source * row_count, row_count)
        allowed = visible(query_doc, query_place, key_doc, key_place)
        key_heads = kv_now[0].reshape(row_count, HEADS, head_dim)
        value_heads = kv_now[1].reshape(row_count, HEADS, head_dim)
        probabilities, score_grad = score_grads(
            query_heads, dout_heads, log_total, delta, allowed, key_heads, value_heads, score_scale
        )
        query_grad = (
            query_grad
            + jnp.einsum("hqk,khd->qhd", score_grad, key_heads, preferred_element_type=jnp.float32)
            * score_scale
        )
        key_grad = (
            jnp.einsum("hqk,qhd->khd", score_grad, query_heads, preferred_element_type=jnp.float32)
            * score_scale
        )
        value_grad = jnp.einsum(
            "hqk,qhd->khd", probabilities, dout_heads, preferred_element_type=jnp.float32
        )
        grads_now = grads_now + jnp.stack(
            [key_grad.reshape(row_count, model_width), value_grad.reshape(row_count, model_width)]
        )
        kv_now = shifted(kv_now, "blk", 1)
        grads_now = shifted_2(grads_now.astype(jnp.bfloat16), "blk", 1).astype(grads_now.dtype)
        return (kv_now, grads_now, query_grad)

    loop_start = (
        jnp.stack([keys_own, values_own]),
        jnp.zeros((2, row_count, model_width), jnp.float32),
        jnp.zeros((row_count, HEADS, head_dim), jnp.float32),
    )
    _, kv_grads, query_grad = lax.fori_loop(0, blocks, turn, loop_start)
    key_grad_all = kv_grads[0]
    value_grad_all = kv_grads[1]
    d_projected = jnp.concatenate(
        [query_grad.reshape(row_count, model_width), key_grad_all, value_grad_all], axis=1
    ).astype(jnp.bfloat16)
    grad_qkv = outer_sum(normed, d_projected)
    _, first_pullback = jax.vjp(layer_norm, residual_in, gain_one, bias_one)
    d_input_norm, grad_gain_one, grad_bias_one = first_pullback(back_product(d_projected, qkv_full))
    input_grad = (d_middle + d_input_norm).astype(jnp.bfloat16)
    summed = (
        lax.psum_scatter(grad_qkv, ("dp", "blk"), scatter_dimension=0, tiled=True),
        lax.psum_scatter(grad_out, ("dp", "blk"), scatter_dimension=0, tiled=True),
        lax.psum_scatter(grad_up, ("dp", "blk"), scatter_dimension=0, tiled=True),
        lax.psum_scatter(grad_down, ("dp", "blk"), scatter_dimension=0, tiled=True),
        lax.psum_scatter(grad_gain_one, ("dp", "blk"), scatter_dimension=0, tiled=True),
        lax.psum_scatter(grad_bias_one, ("dp", "blk"), scatter_dimension=0, tiled=True),
        lax.psum_scatter(grad_gain_two, ("dp", "blk"), scatter_dimension=0, tiled=True),
        lax.psum_scatter(grad_bias_two, ("dp", "blk"), scatter_dimension=0, tiled=True),
        lax.psum_scatter(grad_gain_three, ("dp", "blk"), scatter_dimension=0, tiled=True),
        lax.psum_scatter(grad_bias_three, ("dp", "blk"), scatter_dimension=0, tiled=True),
        lax.psum_scatter(grad_gain_four, ("dp", "blk"), scatter_dimension=0, tiled=True),
        lax.psum_scatter(grad_bias_four, ("dp", "blk"), scatter_dimension=0, tiled=True),
    )
    return (output, input_grad) + tuple(summed)


F32 = jnp.float32
BF16 = jnp.bfloat16
VMEM_BYTES = 56 * 1024 * 1024
CORE, Y_LINK, X_LINK, Z_LINK = 1, 2, 4, 8
Z_MASKS = (0, 8, 16, 24)
PLANE_MASKS = (0, Y_LINK, X_LINK, X_LINK + Y_LINK)


def swap(value, mask):
    devices = lax.axis_size("dp") * lax.axis_size("blk")
    return lax.ppermute(value, ("dp", "blk"), [(i, i ^ mask) for i in range(devices)])


def dot_rows(a, b):
    return lax.dot_general(a, b, (((1,), (0,)), ((), ())), preferred_element_type=F32)


def dot_back(a, b):
    return lax.dot_general(a, b, (((1,), (1,)), ((), ())), preferred_element_type=F32)


def dot_outer(a, b):
    return lax.dot_general(a, b, (((0,), (0,)), ((), ())), preferred_element_type=F32)


def row_stats(values):
    centre = jnp.mean(values, -1, keepdims=True)
    centred = values - centre
    spread = jnp.mean(centred * centred, -1, keepdims=True)
    scale = lax.rsqrt(spread + epsilon)
    return centred * scale, scale


def norm_back(grad_unit, unit, scale):
    first = jnp.mean(grad_unit, -1, keepdims=True)
    second = jnp.mean(grad_unit * unit, -1, keepdims=True)
    return scale * (grad_unit - first - unit * second)


def run_copies(copies):
    for copy in copies:
        copy.start()


def wait_copies(copies):
    for copy in copies:
        copy.wait()


def attention_forward(
    pos, t0, t1, t2, t3, s0, s1, normed, proj, weight, vectors, a0, a1, a2, a3, sems
):
    rows, width = t0.shape
    slot_rows = s0.shape[1]
    heads = a0.shape[1] // (width // HEADS)
    head_dim = width // HEADS
    span = heads * head_dim
    dp, blk = pos[0], pos[1]
    copies = []
    for x, source in enumerate((s0, s1)):
        for z in range(4):
            slot = dp ^ (2 * z + x)
            copies.append(
                pltpu.make_async_copy(
                    source.at[z],
                    weight.at[pl.ds(pl.multiple_of(slot * slot_rows, slot_rows), slot_rows)],
                    sems.at[x * 4 + z],
                )
            )
    run_copies(copies)
    wait_copies(copies)
    tail = (3 * span // 128) * 128
    turned = jnp.transpose(weight[:, tail:].astype(F32))
    vectors[...] = turned[3 * span - tail : 3 * span - tail + 16, :]
    gain, bias = vectors[0:1, :], vectors[1:2, :]
    for k, source in enumerate((t0, t1, t2, t3)):
        unit, _ = row_stats(source[...].astype(F32))
        at = pl.ds(pl.multiple_of((blk ^ k) * rows, rows), rows)
        value = (unit * gain + bias).astype(BF16)
        normed[at, :] = value
        proj[at, :] = dot_rows(value, weight[...]).astype(BF16)
    scale = head_dim ** (-0.5)
    below = lax.broadcasted_iota(jnp.int32, (rows, rows), 1) <= lax.broadcasted_iota(
        jnp.int32, (rows, rows), 0
    )
    for block in range(4):
        mixed = []
        low, high = block * rows, (block + 1) * rows
        for head in range(heads):
            q = proj[low:high, head * head_dim : (head + 1) * head_dim] * BF16(scale)
            k = proj[:high, span + head * head_dim : span + (head + 1) * head_dim]
            v = proj[:high, 2 * span + head * head_dim : 2 * span + (head + 1) * head_dim]
            own = jnp.where(below, dot_back(q, k[low:]), masked_score)
            peak = jnp.max(own, -1, keepdims=True)
            if block:
                past = dot_back(q, k[:low])
                peak = jnp.maximum(peak, jnp.max(past, -1, keepdims=True))
            own = jnp.exp(own - peak)
            total = jnp.sum(own, -1, keepdims=True)
            mix = dot_rows(own.astype(BF16), v[low:])
            if block:
                past = jnp.exp(past - peak)
                total = total + jnp.sum(past, -1, keepdims=True)
                mix = mix + dot_rows(past.astype(BF16), v[:low])
            mixed.append(mix / total)
        value = jnp.concatenate(mixed, axis=1).astype(BF16)
        for k, target in enumerate((a0, a1, a2, a3)):

            @pl.when((blk ^ k) == block)
            def _(target=target, value=value):
                target[...] = value


def merge_heads(blk, parts, merged):
    for k, part in enumerate(parts):
        merged[blk ^ k] = part[...]
    return jnp.concatenate([merged[j] for j in range(4)], axis=1)


def stacked_copies(pos, stacks, target, sems):
    rows = stacks[0].shape[1]
    chip = pos[0] * 2 + pos[1] // 2
    core = pos[1] % 2
    copies = []
    for other in range(2):
        for plane in range(4):
            source = stacks[other * 4 + plane]
            for z in range(4):
                slot = chip ^ (4 * z + plane)
                copies.append(
                    pltpu.make_async_copy(
                        source.at[z],
                        target.at[core ^ other, pl.ds(pl.multiple_of(slot * rows, rows), rows)],
                        sems.at[other * 16 + plane * 4 + z],
                    )
                )
    return copies


def ffn_forward(
    pos, a0, a1, a2, a3, tokens, vectors, wide, u0, u1, u2, u3, u4, u5, u6, u7,
    inner, middle, normed_two, hidden, unit_four, slope, scale_four,
    weights, merged, up, sems,
):
    copies = stacked_copies(pos, (u0, u1, u2, u3, u4, u5, u6, u7), weights, sems)
    run_copies(copies)
    rows, width = tokens.shape
    attended = merge_heads(pos[1], (a0, a1, a2, a3), merged).astype(F32)
    unit, _ = row_stats(attended)
    inner_low = (unit * vectors[2:3, :] + vectors[3:4, :]).astype(BF16)
    inner[...] = inner_low
    wait_copies(copies)
    half = width // 2
    mid = tokens[...].astype(F32) + jnp.concatenate(
        [dot_rows(inner_low, weights[h, :, :half]) for h in range(2)], axis=1
    )
    middle[...] = mid
    unit, _ = row_stats(mid)
    low = (unit * vectors[4:5, :] + vectors[5:6, :]).astype(BF16)
    normed_two[...] = low
    up_half = weights.shape[2] - half
    for h in range(2):
        up[:, h * up_half : (h + 1) * up_half] = dot_rows(low, weights[h, :, half:])
    step = 16

    def chunk(i, carry):
        at = pl.ds(pl.multiple_of(i * step, step), step)
        value = up[at, :]
        gate = 0.5 * (1.0 + lax.erf(value * (2.0**-0.5)))
        slope[at, :] = (gate + value * jnp.exp(-0.5 * value * value) * (0.5 / math.pi) ** 0.5).astype(
            BF16
        )
        unit, scale = row_stats(value * gate)
        unit_four[at, :] = unit.astype(BF16)
        hidden[at, :] = (unit * wide[0:1, :] + wide[1:2, :]).astype(BF16)
        scale_four[at, :] = jnp.broadcast_to(scale, (step, 128))
        return carry

    lax.fori_loop(0, rows // step, chunk, 0)


def ffn_backward(
    pos, a0, a1, a2, a3, cot, vectors, wide, middle, hidden, unit_four, slope, scale_four, w_down,
    u0, u1, u2, u3, u4, u5, u6, u7,
    output, d_up, d_middle, d_middle_low, d0, d1, d2, d3, vector_grads, wide_grads,
    weights, merged, d_hidden, sums, sems,
):
    copies = stacked_copies(pos, (u0, u1, u2, u3, u4, u5, u6, u7), weights, sems)
    run_copies(copies)
    rows, width = cot.shape
    output[...] = (middle[...] + dot_rows(hidden[...], w_down[...])).astype(BF16)
    d_hidden[...] = dot_back(cot[...], w_down[...])
    step = 16
    sums[...] = jnp.zeros_like(sums)

    def chunk(i, carry):
        at = pl.ds(pl.multiple_of(i * step, step), step)
        grad = d_hidden[at, :]
        unit = unit_four[at, :].astype(F32)
        part = grad * unit
        sums[0] += part[:8] + part[8:]
        sums[1] += grad[:8] + grad[8:]
        d_gelu = norm_back(grad * wide[0:1, :], unit, scale_four[at, 0:1])
        d_up[at, :] = (d_gelu * slope[at, :].astype(F32)).astype(BF16)
        return carry

    lax.fori_loop(0, rows // step, chunk, 0)
    wide_grads[...] = jnp.concatenate(
        [jnp.sum(sums[0], 0, keepdims=True), jnp.sum(sums[1], 0, keepdims=True)], axis=0
    )
    wait_copies(copies)
    half = width // 2
    up_half = weights.shape[2] - half
    d_normed = dot_back(d_up[:, :up_half], weights[0, :, half:]) + dot_back(
        d_up[:, up_half:], weights[1, :, half:]
    )
    unit, scale = row_stats(middle[...])
    gain_three = jnp.sum(d_normed * unit, 0, keepdims=True)
    bias_three = jnp.sum(d_normed, 0, keepdims=True)
    d_mid = cot[...].astype(F32) + norm_back(d_normed * vectors[4:5, :], unit, scale)
    d_middle[...] = d_mid
    d_mid_low = d_mid.astype(BF16)
    d_middle_low[...] = d_mid_low
    d_inner = dot_back(d_mid_low[:, :half], weights[0, :, :half]) + dot_back(
        d_mid_low[:, half:], weights[1, :, :half]
    )
    attended = merge_heads(pos[1], (a0, a1, a2, a3), merged).astype(F32)
    unit, scale = row_stats(attended)
    gain_two = jnp.sum(d_inner * unit, 0, keepdims=True)
    bias_two = jnp.sum(d_inner, 0, keepdims=True)
    vector_grads[...] = jnp.concatenate(
        [gain_two, bias_two, gain_three, bias_three, jnp.zeros((4, width), F32)], axis=0
    )
    d_att = norm_back(d_inner * vectors[2:3, :], unit, scale).astype(BF16)
    span = width // 4
    for j in range(4):
        merged[j] = d_att[:, j * span : (j + 1) * span]
    for k, target in enumerate((d0, d1, d2, d3)):
        target[...] = merged[pos[1] ^ k]


def send_pieces(pos, held, targets, sems):
    chip = pos[0] * 2 + pos[1] // 2
    copies = []
    for plane, target in enumerate(targets):
        for z in range(4):
            slot = ((chip ^ plane) & 3) + 4 * z
            copies.append(
                pltpu.make_async_copy(held.at[slot], target.at[z], sems.at[plane * 4 + z])
            )
    run_copies(copies)
    wait_copies(copies)


def down_grads(pos, h0, h1, c0, c1, p0, p1, p2, p3, held, sems):
    rows = held.shape[1]
    half = c0.shape[1] // 2
    first = pos[1] % 2 == 0
    cots = [jnp.where(first, c[:, :half], c[:, half:]) for c in (c0, c1)]
    tile = 2 * rows
    for t in range(h0.shape[1] // tile):
        at = slice(t * tile, (t + 1) * tile)
        value = dot_outer(h0[:, at], cots[0]) + dot_outer(h1[:, at], cots[1])
        value = value.astype(BF16)
        held[2 * t] = value[:rows]
        held[2 * t + 1] = value[rows:]
    send_pieces(pos, held, (p0, p1, p2, p3), sems)


def up_grads(pos, i0, i1, m0, m1, n0, n1, g0, g1, p0, p1, p2, p3, held, sems):
    rows = held.shape[1]
    first = pos[1] % 2 == 0

    def mine(ref):
        half = ref.shape[1] // 2
        return jnp.where(first, ref[:, :half], ref[:, half:])

    def fill(lefts, rights, start):
        columns = rights[0].shape[1]
        tile = 384
        for r in range(0, 768, tile):
            for c in range(0, columns, 384):
                value = dot_outer(lefts[0][:, r : r + tile], rights[0][:, c : c + 384])
                value = value + dot_outer(lefts[1][:, r : r + tile], rights[1][:, c : c + 384])
                value = value.astype(BF16)
                for s in range(tile // rows):
                    held[r // rows + s, :, start + c : start + c + 384] = value[
                        s * rows : (s + 1) * rows
                    ]

    fill((i0, i1), (mine(m0), mine(m1)), 0)
    fill((n0, n1), (mine(g0), mine(g1)), m0.shape[1] // 2)
    send_pieces(pos, held, (p0, p1, p2, p3), sems)


def attention_backward(
    pos, t0, t1, t2, t3, d0, d1, d2, d3, normed, proj, weight, vector_grads,
    own, other, p0, p1, d_proj, d_out, total, held, d_normed, sems,
):
    rows, width = t0.shape
    head_dim = width // HEADS
    span = d0.shape[1]
    heads = span // head_dim
    dp, blk = pos[0], pos[1]
    for k, source in enumerate((d0, d1, d2, d3)):
        d_out[pl.ds(pl.multiple_of((blk ^ k) * rows, rows), rows), :] = source[...]
    scale = head_dim ** (-0.5)
    below = lax.broadcasted_iota(jnp.int32, (rows, rows), 1) <= lax.broadcasted_iota(
        jnp.int32, (rows, rows), 0
    )
    for head in range(heads):
        at_q = slice(head * head_dim, (head + 1) * head_dim)
        at_k = slice(span + head * head_dim, span + (head + 1) * head_dim)
        at_v = slice(2 * span + head * head_dim, 2 * span + (head + 1) * head_dim)
        total[...] = jnp.zeros_like(total)
        for block in range(4):
            low, high = block * rows, (block + 1) * rows
            q = proj[low:high, at_q] * BF16(scale)
            d = d_out[low:high, at_q]
            parts = [(low, high)] + ([(0, low)] if block else [])
            scores = []
            for part, (start, end) in enumerate(parts):
                score = dot_back(q, proj[start:end, at_k])
                scores.append(score if part else jnp.where(below, score, masked_score))
            peak = functools.reduce(
                jnp.maximum, [jnp.max(score, -1, keepdims=True) for score in scores]
            )
            scores = [jnp.exp(score - peak) for score in scores]
            inverse = 1.0 / sum(jnp.sum(score, -1, keepdims=True) for score in scores)
            scores = [score * inverse for score in scores]
            d_weights = [dot_back(d, proj[start:end, at_v]) for start, end in parts]
            delta = sum(
                jnp.sum(score * grad, -1, keepdims=True) for score, grad in zip(scores, d_weights)
            )
            d_query = 0.0
            for (start, end), score, grad in zip(parts, scores, d_weights):
                d_score = (score * (grad - delta)).astype(BF16)
                d_query = d_query + dot_rows(d_score, proj[start:end, at_k])
                total[0, start:end] += dot_outer(d_score, q)
                total[1, start:end] += dot_outer(score.astype(BF16), d)
            d_proj[low:high, at_q] = (d_query * scale).astype(BF16)
        d_proj[:, at_k] = total[0].astype(BF16)
        d_proj[:, at_v] = total[1].astype(BF16)
    columns = weight.shape[1]
    vector_sums = []
    for k, source in enumerate((t0, t1, t2, t3)):
        at = pl.ds(pl.multiple_of((blk ^ k) * rows, rows), rows)
        grad = dot_back(d_proj[at, :], weight[:, : 3 * span])
        unit, _ = row_stats(source[...].astype(F32))
        vector_sums.append((jnp.sum(grad * unit, 0, keepdims=True), jnp.sum(grad, 0, keepdims=True)))
        d_normed[k] = grad.astype(BF16)
    own[0], own[1] = d_normed[0], d_normed[2]
    other[0], other[1] = d_normed[1], d_normed[3]
    sums = [sum(v[i] for v in vector_sums) for i in range(2)]
    turned = jnp.transpose(
        jnp.concatenate(
            sums + [vector_grads[0:14, :], jnp.zeros((128 - 16, width), F32)], axis=0
        )
    )
    slot_rows = held.shape[1]
    for r in range(0, width, 2 * slot_rows):
        value = dot_outer(normed[:, r : r + 2 * slot_rows], d_proj[...])
        value = jnp.concatenate(
            [value, turned[r : r + 2 * slot_rows, : columns - 3 * span]], axis=1
        ).astype(BF16)
        held[r // slot_rows] = value[:slot_rows]
        held[r // slot_rows + 1] = value[slot_rows:]
    copies = []
    for x, target in enumerate((p0, p1)):
        for z in range(4):
            slot = ((dp ^ x) & 1) + 2 * z
            copies.append(pltpu.make_async_copy(held.at[slot], target.at[z], sems.at[x * 4 + z]))
    run_copies(copies)
    wait_copies(copies)


def local_kernel(kernel, outs, ins, scratch, flops, in_any=(), out_any=()):
    here = pl.BlockSpec(memory_space=pltpu.VMEM)
    far = pl.BlockSpec(memory_space=pl.ANY)
    specs = [pl.BlockSpec(memory_space=pltpu.SMEM)]
    specs += [far if i in in_any else here for i in range(1, len(ins))]
    moved = sum(math.prod(v.shape) * v.dtype.itemsize for v in (*ins, *outs))
    return pl.pallas_call(
        kernel,
        out_shape=outs,
        in_specs=specs,
        out_specs=[far if i in out_any else here for i in range(len(outs))],
        scratch_shapes=scratch,
        compiler_params=pltpu.CompilerParams(vmem_limit_bytes=VMEM_BYTES),
        cost_estimate=pl.CostEstimate(flops=flops, bytes_accessed=moved, transcendentals=0),
    )(*ins)


def shape_of(dtype, *shape):
    return jax.ShapeDtypeStruct(shape, dtype)


def pick(value, index):
    return lax.dynamic_index_in_dim(value, index, 0, keepdims=False)


def z_exchange(own):
    return [own] + [swap(own, mask) for mask in Z_MASKS[1:]]


def fast_body(
    tokens, cotangent, doc_lengths, w_qkv, w_out, w_up, w_down,
    ln1_gain, ln1_bias, ln2_gain, ln2_bias, ln3_gain, ln3_bias, ln4_gain, ln4_bias,
):
    rows, width = tokens.shape
    shard = w_qkv.shape[0]
    ff = w_up.shape[1]
    head_dim = width // HEADS
    heads = HEADS // 4
    span = heads * head_dim
    group = rows * 4
    columns = -(-(3 * span + 16) // 128) * 128
    dp, blk = lax.axis_index("dp"), lax.axis_index("blk")
    core, plane_x, plane_z = blk % 2, dp % 2, dp // 2
    pos = jnp.stack([dp, blk]).astype(jnp.int32)
    down_full = lax.all_gather(w_down, ("dp", "blk"), axis=0, tiled=True)

    small = jnp.stack(
        [ln1_gain, ln1_bias, ln2_gain, ln2_bias, ln3_gain, ln3_bias], axis=1
    )
    small = jnp.concatenate(
        [
            small,
            ln4_gain.reshape(4, shard).T,
            ln4_bias.reshape(4, shard).T,
            jnp.zeros((shard, columns - 3 * span - 14), BF16),
        ],
        axis=1,
    )
    slices = jnp.stack(
        [
            jnp.concatenate(
                [w_qkv[:, p * width + j * span : p * width + (j + 1) * span] for p in range(3)]
                + [small],
                axis=1,
            )
            for j in range(4)
        ]
    )
    from_blk = [pick(slices, blk)] + [swap(pick(slices, blk ^ k), k) for k in range(1, 4)]
    from_blk = jnp.stack(from_blk)
    own_slice = jnp.concatenate([pick(from_blk, blk ^ j) for j in range(4)], axis=0)
    token_y = swap(tokens, Y_LINK)
    token_core, token_both = swap(tokens, CORE), swap(token_y, CORE)
    stack_own = jnp.stack(z_exchange(own_slice))
    stack_x = swap(stack_own, X_LINK)

    def halves(weight):
        half = weight.shape[1] // 2
        return weight[:, :half], weight[:, half:]

    out_halves, up_halves = halves(w_out), halves(w_up)
    both = [jnp.concatenate([out_halves[h], up_halves[h]], axis=1) for h in range(2)]
    mine = jnp.where(core == 0, both[0], both[1])
    theirs = swap(jnp.where(core == 0, both[1], both[0]), CORE)
    pair = jnp.where(
        core == 0, jnp.concatenate([mine, theirs], 0), jnp.concatenate([theirs, mine], 0)
    )
    up_own = jnp.stack(z_exchange(pair))
    up_stacks = [up_own] + [swap(up_own, mask) for mask in PLANE_MASKS[1:]]
    up_stacks = up_stacks + [swap(stack, CORE) for stack in up_stacks]

    tokens_group = [tokens, token_core, token_y, token_both]
    normed, proj, weight, vectors, *att = local_kernel(
        attention_forward,
        [
            shape_of(BF16, group, width),
            shape_of(BF16, group, columns),
            shape_of(BF16, width, columns),
            shape_of(F32, 16, width),
        ]
        + [shape_of(BF16, rows, span)] * 4,
        [pos, *tokens_group, stack_own, stack_x],
        [pltpu.SemaphoreType.DMA((8,))],
        2 * group * width * columns + 4 * group * group * span,
        in_any=(5, 6),
    )
    wide = vectors[6:14].reshape(2, 4, 32, shard).transpose(0, 2, 1, 3).reshape(2, ff)
    att = [att[0]] + [swap(att[k], k) for k in range(1, 4)]

    up_columns = (width + ff) // 2
    inner, middle, normed_two, hidden, unit_four, slope, scale_four = local_kernel(
        ffn_forward,
        [
            shape_of(BF16, rows, width),
            shape_of(F32, rows, width),
            shape_of(BF16, rows, width),
            shape_of(BF16, rows, ff),
            shape_of(BF16, rows, ff),
            shape_of(BF16, rows, ff),
            shape_of(F32, rows, 128),
        ],
        [pos, *att, tokens, vectors, wide, *up_stacks],
        [
            pltpu.VMEM((2, width, up_columns), BF16),
            pltpu.VMEM((4, rows, span), BF16),
            pltpu.VMEM((rows, ff), F32),
            pltpu.SemaphoreType.DMA((32,)),
        ],
        2 * rows * width * (width + ff),
        in_any=range(8, 16),
    )
    cot_other = swap(cotangent, CORE)
    hidden_other = swap(hidden, CORE)
    normed_two_other, inner_other = swap(normed_two, CORE), swap(inner, CORE)
    down_rows = ff // 16
    down_parts = local_kernel(
        down_grads,
        [shape_of(BF16, 4, down_rows, width // 2)] * 4,
        [pos, hidden, hidden_other, cotangent, cot_other],
        [pltpu.VMEM((16, down_rows, width // 2), BF16), pltpu.SemaphoreType.DMA((16,))],
        2 * rows * width * ff,
        out_any=range(4),
    )

    (
        output, d_up, d_middle, d_middle_low, d0, d1, d2, d3, vector_grads, wide_grads,
    ) = local_kernel(
        ffn_backward,
        [
            shape_of(BF16, rows, width),
            shape_of(BF16, rows, ff),
            shape_of(F32, rows, width),
            shape_of(BF16, rows, width),
        ]
        + [shape_of(BF16, rows, span)] * 4
        + [shape_of(F32, 8, width), shape_of(F32, 2, ff)],
        [
            pos, *att, cotangent, vectors, wide, middle, hidden, unit_four, slope, scale_four,
            down_full, *up_stacks,
        ],
        [
            pltpu.VMEM((2, width, up_columns), BF16),
            pltpu.VMEM((4, rows, span), BF16),
            pltpu.VMEM((rows, ff), F32),
            pltpu.VMEM((2, 8, ff), F32),
            pltpu.SemaphoreType.DMA((32,)),
        ],
        2 * rows * width * (width + 3 * ff),
        in_any=range(14, 22),
    )
    d_att = [d0] + [swap(value, k) for k, value in ((1, d1), (2, d2), (3, d3))]
    d_up_other, d_middle_other = swap(d_up, CORE), swap(d_middle_low, CORE)
    up_rows = width // 16
    up_parts = local_kernel(
        up_grads,
        [shape_of(BF16, 4, up_rows, up_columns)] * 4,
        [
            pos, inner, inner_other, d_middle_low, d_middle_other,
            normed_two, normed_two_other, d_up, d_up_other,
        ],
        [pltpu.VMEM((16, up_rows, up_columns), BF16), pltpu.SemaphoreType.DMA((16,))],
        2 * rows * width * (width + ff),
        out_any=range(4),
    )

    wide_rows = wide_grads.reshape(2, 32, 4, shard).transpose(0, 2, 1, 3).reshape(8, width)
    all_vectors = jnp.concatenate(
        [vector_grads[:4], wide_rows, jnp.zeros((4, width), F32)], axis=0
    )
    slot_rows = 4 * shard
    own_part, other_part, p0, p1 = local_kernel(
        attention_backward,
        [shape_of(BF16, 2, rows, width)] * 2 + [shape_of(BF16, 4, slot_rows, columns)] * 2,
        [pos, *tokens_group, *d_att, normed, proj, weight, all_vectors],
        [
            pltpu.VMEM((group, 3 * span), BF16),
            pltpu.VMEM((group, span), BF16),
            pltpu.VMEM((2, group, head_dim), F32),
            pltpu.VMEM((8, slot_rows, columns), BF16),
            pltpu.VMEM((4, rows, width), BF16),
            pltpu.SemaphoreType.DMA((8,)),
        ],
        4 * group * width * columns + 10 * group * group * span,
        out_any=(2, 3),
    )

    pair_part = own_part.astype(F32) + swap(other_part, CORE).astype(F32)
    far_part = swap(pair_part[1].astype(BF16), Y_LINK)
    d_first = pair_part[0] + far_part.astype(F32)
    unit, scale = row_stats(tokens.astype(F32))
    input_grad = (d_middle + norm_back(d_first * vectors[0:1, :], unit, scale)).astype(BF16)

    def z_sum(whole):
        parts = [pick(whole, plane_z ^ z) for z in range(4)]
        return parts[0] + sum(
            swap(parts[z].astype(BF16), Z_MASKS[z]).astype(F32) for z in range(1, 4)
        )

    def chip_sum(parts):
        whole = parts[0].astype(F32) + sum(
            swap(parts[p], PLANE_MASKS[p]).astype(F32) for p in range(1, 4)
        )
        whole = z_sum(whole)
        half_rows = whole.shape[0] // 2
        by_core = whole.reshape(2, half_rows, -1)
        kept, given = pick(by_core, core), pick(by_core, 1 - core)
        got = swap(given, CORE)
        return jnp.where(core == 0, kept, got), jnp.where(core == 0, got, kept)

    grad_down = jnp.concatenate(chip_sum(down_parts), axis=1)
    low_half, high_half = chip_sum(up_parts)
    cut = width // 2
    grad_out = jnp.concatenate([low_half[:, :cut], high_half[:, :cut]], axis=1)
    grad_up = jnp.concatenate([low_half[:, cut:], high_half[:, cut:]], axis=1)

    head_sum = z_sum(p0.astype(F32) + swap(p1, X_LINK).astype(F32)).reshape(4, shard, columns)
    head_parts = [pick(head_sum, blk)] + [swap(pick(head_sum, blk ^ k), k) for k in range(1, 4)]
    head_parts = jnp.stack(head_parts)
    by_block = [pick(head_parts, blk ^ j) for j in range(4)]
    grad_qkv = jnp.concatenate(
        [by_block[j][:, p * span : (p + 1) * span] for p in range(3) for j in range(4)], axis=1
    )
    ends = sum(by_block)[:, 3 * span :].T
    return (
        output, input_grad, grad_qkv, grad_out, grad_up, grad_down,
        ends[0], ends[1], ends[2], ends[3], ends[4], ends[5],
        ends[6:10].reshape(-1), ends[10:14].reshape(-1),
    )


def layer(*arrays):
    one_document = arrays[2].shape[1] == 1
    if lax.axis_size("dp") == 8 and lax.axis_size("blk") == 4 and one_document:
        return fast_body(*arrays)
    return general_body(*arrays)


def solution(mesh):
    placed = (
        P(("dp", "blk"), None),
        P(("dp", "blk"), None),
        P("dp", None),
        P(("dp", "blk"), None),
        P(("dp", "blk"), None),
        P(("dp", "blk"), None),
        P(("dp", "blk"), None),
        P(("dp", "blk")),
        P(("dp", "blk")),
        P(("dp", "blk")),
        P(("dp", "blk")),
        P(("dp", "blk")),
        P(("dp", "blk")),
        P(("dp", "blk")),
        P(("dp", "blk")),
    )
    return jax.shard_map(
        layer,
        mesh=mesh,
        in_specs=placed,
        out_specs=(
            P(("dp", "blk"), None),
            P(("dp", "blk"), None),
            P(("dp", "blk"), None),
            P(("dp", "blk"), None),
            P(("dp", "blk"), None),
            P(("dp", "blk"), None),
            P(("dp", "blk")),
            P(("dp", "blk")),
            P(("dp", "blk")),
            P(("dp", "blk")),
            P(("dp", "blk")),
            P(("dp", "blk")),
            P(("dp", "blk")),
            P(("dp", "blk")),
        ),
        check_vma=False,
    )
```

```python
import functools
import math

import jax
import jax.numpy as jnp
from jax import lax
from jax.experimental import pallas as pl
from jax.experimental.pallas import tpu as pltpu
from jax.sharding import PartitionSpec as P

HEADS = 12


epsilon = 1e-05
masked_score = -1000000000.0


def shifted(shard, axis, by):
    devices = lax.axis_size(axis)
    pairs = [(i, i + by) for i in range(devices) if 0 <= i + by < devices]
    return lax.ppermute(shard, axis, pairs)


def shifted_2(value, axis, steps):
    count = lax.axis_size(axis)
    pairs = [(source, (source + steps) % count) for source in range(count)]
    return lax.ppermute(value, axis, pairs)


def layer_norm(values, norm_gain, norm_bias):
    centre = jnp.mean(values, -1, keepdims=True)
    centred = values - centre
    spread = jnp.mean(centred * centred, -1, keepdims=True)
    return centred * lax.rsqrt(spread + epsilon) * norm_gain + norm_bias


def ffn_norm(up_value, norm_gain, norm_bias):
    return layer_norm(jax.nn.gelu(up_value, approximate=False), norm_gain, norm_bias)


def doc_place(row_ids, doc_row, row_count, blocks):
    device = row_ids // row_count
    local = row_ids % row_count
    shares = doc_row // blocks
    ends = jnp.cumsum(shares, dtype=jnp.int32)
    starts = ends - shares
    doc = jnp.sum((local[:, None] >= ends[None, :]).astype(jnp.int32), -1, dtype=jnp.int32)
    pick = (doc[:, None] == jnp.arange(doc_row.shape[0], dtype=jnp.int32)[None, :]).astype(
        jnp.int32
    )
    share_of = jnp.sum(pick * shares[None, :], -1, dtype=jnp.int32)
    start_of = jnp.sum(pick * starts[None, :], -1, dtype=jnp.int32)
    return (doc, device * share_of + local - start_of)


def visible(query_doc, query_place, key_doc, key_place):
    return (query_doc[:, None] == key_doc[None, :]) & (key_place[None, :] <= query_place[:, None])


def outer_sum(first_operand, second_operand):
    return lax.dot_general(
        first_operand, second_operand, (((0,), (0,)), ((), ())), preferred_element_type=jnp.float32
    )


def back_product(gradient, weight):
    return lax.dot_general(
        gradient, weight, (((1,), (1,)), ((), ())), preferred_element_type=jnp.float32
    )


def score_grads(
    query_heads, dout_heads, lse_heads, delta_heads, allowed, key_heads, value_heads, score_scale
):
    scores = (
        jnp.einsum("qhd,khd->hqk", query_heads, key_heads, preferred_element_type=jnp.float32)
        * score_scale
    )
    probabilities = jnp.where(allowed[None], jnp.exp(scores - lse_heads[:, :, None]), 0.0)
    weight_grad = jnp.einsum(
        "qhd,khd->hqk", dout_heads, value_heads, preferred_element_type=jnp.float32
    )
    score_grad = (probabilities * (weight_grad - delta_heads[:, :, None])).astype(jnp.bfloat16)
    return (probabilities.astype(jnp.bfloat16), score_grad)


def general_body(
    tokens,
    cotangent,
    doc_lengths,
    w_qkv,
    w_out,
    w_up,
    w_down,
    ln1_gain,
    ln1_bias,
    ln2_gain,
    ln2_bias,
    ln3_gain,
    ln3_bias,
    ln4_gain,
    ln4_bias,
):
    gathered = (
        lax.all_gather(w_qkv, ("dp", "blk"), axis=0, tiled=True),
        lax.all_gather(w_out, ("dp", "blk"), axis=0, tiled=True),
        lax.all_gather(w_up, ("dp", "blk"), axis=0, tiled=True),
        lax.all_gather(w_down, ("dp", "blk"), axis=0, tiled=True),
        lax.all_gather(ln1_gain, ("dp", "blk"), axis=0, tiled=True),
        lax.all_gather(ln1_bias, ("dp", "blk"), axis=0, tiled=True),
        lax.all_gather(ln2_gain, ("dp", "blk"), axis=0, tiled=True),
        lax.all_gather(ln2_bias, ("dp", "blk"), axis=0, tiled=True),
        lax.all_gather(ln3_gain, ("dp", "blk"), axis=0, tiled=True),
        lax.all_gather(ln3_bias, ("dp", "blk"), axis=0, tiled=True),
        lax.all_gather(ln4_gain, ("dp", "blk"), axis=0, tiled=True),
        lax.all_gather(ln4_bias, ("dp", "blk"), axis=0, tiled=True),
    )
    qkv_full, out_full, up_full, down_full = (gathered[0], gathered[1], gathered[2], gathered[3])
    norm_params = [value.astype(jnp.float32) for value in gathered[4:]]
    gain_one, bias_one, gain_two, bias_two, gain_three, bias_three, gain_four, bias_four = (
        norm_params
    )
    row_count, model_width = tokens.shape
    head_dim = model_width // HEADS
    score_scale = head_dim ** (-0.5)
    doc_row = doc_lengths[0]
    blocks = lax.axis_size("blk")
    place_index = lax.axis_index("blk")
    query_doc, query_place = doc_place(
        place_index * row_count + jnp.arange(row_count, dtype=jnp.int32), doc_row, row_count, blocks
    )

    def key_meta(first_row, count):
        return doc_place(first_row + jnp.arange(count, dtype=jnp.int32), doc_row, row_count, blocks)

    residual_in = tokens.astype(jnp.float32)
    normed = layer_norm(residual_in, gain_one, bias_one).astype(jnp.bfloat16)
    projected = jnp.dot(normed, qkv_full, preferred_element_type=jnp.float32).astype(jnp.bfloat16)
    queries = projected[:, :model_width]
    keys_own = projected[:, model_width : 2 * model_width]
    values_own = projected[:, 2 * model_width :]
    query_heads = queries.reshape(row_count, HEADS, head_dim)
    start_state = (
        jnp.full((HEADS, row_count), masked_score, jnp.float32),
        jnp.zeros((HEADS, row_count), jnp.float32),
        jnp.zeros((HEADS, row_count, head_dim), jnp.float32),
    )
    running = start_state
    key_part = lax.all_gather(keys_own, "blk", axis=0, tiled=True)
    value_part = lax.all_gather(values_own, "blk", axis=0, tiled=True)
    part_rows = key_part.shape[0]
    step_rows = math.gcd(part_rows, 512)
    count = part_rows // step_rows

    def one_step(state, element):
        key_block, value_block, block_start = element
        key_doc, key_place = key_meta(block_start, step_rows)
        allowed = visible(query_doc, query_place, key_doc, key_place)
        scores = (
            jnp.einsum(
                "qhd,khd->hqk",
                query_heads,
                key_block.reshape(step_rows, HEADS, head_dim),
                preferred_element_type=jnp.float32,
            )
            * score_scale
        )
        scores = jnp.where(allowed[None], scores, masked_score)
        peak_old, total_old, weighted_old = state
        peak_new = jnp.maximum(peak_old, jnp.max(scores, -1))
        weights = jnp.where(allowed[None], jnp.exp(scores - peak_new[:, :, None]), 0.0)
        factor = jnp.exp(peak_old - peak_new)
        total_new = total_old * factor + jnp.sum(weights, -1)
        weighted_new = weighted_old * factor[:, :, None] + jnp.einsum(
            "hqk,khd->hqd",
            weights.astype(jnp.bfloat16),
            value_block.reshape(step_rows, HEADS, head_dim),
            preferred_element_type=jnp.float32,
        )
        return ((peak_new, total_new, weighted_new), None)

    starts = jnp.arange(count, dtype=jnp.int32) * step_rows
    running, _ = lax.scan(
        one_step,
        running,
        (
            key_part.reshape(count, step_rows, model_width),
            value_part.reshape(count, step_rows, model_width),
            starts,
        ),
    )
    peak_score, total_weight, weighted_sum = running
    log_total = peak_score + jnp.log(total_weight)
    attended = (
        (weighted_sum / total_weight[:, :, None]).transpose(1, 0, 2).reshape(row_count, model_width)
    )
    inner = layer_norm(attended, gain_two, bias_two).astype(jnp.bfloat16)
    middle = residual_in + jnp.dot(inner, out_full, preferred_element_type=jnp.float32)
    normed_two = layer_norm(middle, gain_three, bias_three).astype(jnp.bfloat16)
    up_value = jnp.dot(normed_two, up_full, preferred_element_type=jnp.float32)
    hidden = ffn_norm(up_value, gain_four, bias_four).astype(jnp.bfloat16)
    output = (middle + jnp.dot(hidden, down_full, preferred_element_type=jnp.float32)).astype(
        jnp.bfloat16
    )
    grad_down = outer_sum(hidden, cotangent)
    d_hidden = back_product(cotangent, down_full)
    _, ffn_pullback = jax.vjp(ffn_norm, up_value, gain_four, bias_four)
    d_up, grad_gain_four, grad_bias_four = ffn_pullback(d_hidden)
    d_up_low = d_up.astype(jnp.bfloat16)
    grad_up = outer_sum(normed_two, d_up_low)
    _, third_pullback = jax.vjp(layer_norm, middle, gain_three, bias_three)
    d_middle_norm, grad_gain_three, grad_bias_three = third_pullback(
        back_product(d_up_low, up_full)
    )
    d_middle = cotangent.astype(jnp.float32) + d_middle_norm
    d_middle_low = d_middle.astype(jnp.bfloat16)
    grad_out = outer_sum(inner, d_middle_low)
    _, second_pullback = jax.vjp(layer_norm, attended, gain_two, bias_two)
    d_attended, grad_gain_two, grad_bias_two = second_pullback(back_product(d_middle_low, out_full))
    d_attended_low = d_attended.astype(jnp.bfloat16)
    dout_heads = d_attended_low.reshape(row_count, HEADS, head_dim)
    delta = jnp.einsum(
        "qhd,qhd->hq",
        d_attended_low.astype(jnp.float32).reshape(row_count, HEADS, head_dim),
        attended.reshape(row_count, HEADS, head_dim),
    )

    def turn(turn_index, loop_state):
        kv_now, grads_now, query_grad = loop_state
        source = (place_index - turn_index) % blocks
        key_doc, key_place = key_meta(source * row_count, row_count)
        allowed = visible(query_doc, query_place, key_doc, key_place)
        key_heads = kv_now[0].reshape(row_count, HEADS, head_dim)
        value_heads = kv_now[1].reshape(row_count, HEADS, head_dim)
        probabilities, score_grad = score_grads(
            query_heads, dout_heads, log_total, delta, allowed, key_heads, value_heads, score_scale
        )
        query_grad = (
            query_grad
            + jnp.einsum("hqk,khd->qhd", score_grad, key_heads, preferred_element_type=jnp.float32)
            * score_scale
        )
        key_grad = (
            jnp.einsum("hqk,qhd->khd", score_grad, query_heads, preferred_element_type=jnp.float32)
            * score_scale
        )
        value_grad = jnp.einsum(
            "hqk,qhd->khd", probabilities, dout_heads, preferred_element_type=jnp.float32
        )
        grads_now = grads_now + jnp.stack(
            [key_grad.reshape(row_count, model_width), value_grad.reshape(row_count, model_width)]
        )
        kv_now = shifted(kv_now, "blk", 1)
        grads_now = shifted_2(grads_now.astype(jnp.bfloat16), "blk", 1).astype(grads_now.dtype)
        return (kv_now, grads_now, query_grad)

    loop_start = (
        jnp.stack([keys_own, values_own]),
        jnp.zeros((2, row_count, model_width), jnp.float32),
        jnp.zeros((row_count, HEADS, head_dim), jnp.float32),
    )
    _, kv_grads, query_grad = lax.fori_loop(0, blocks, turn, loop_start)
    key_grad_all = kv_grads[0]
    value_grad_all = kv_grads[1]
    d_projected = jnp.concatenate(
        [query_grad.reshape(row_count, model_width), key_grad_all, value_grad_all], axis=1
    ).astype(jnp.bfloat16)
    grad_qkv = outer_sum(normed, d_projected)
    _, first_pullback = jax.vjp(layer_norm, residual_in, gain_one, bias_one)
    d_input_norm, grad_gain_one, grad_bias_one = first_pullback(back_product(d_projected, qkv_full))
    input_grad = (d_middle + d_input_norm).astype(jnp.bfloat16)
    summed = (
        lax.psum_scatter(grad_qkv, ("dp", "blk"), scatter_dimension=0, tiled=True),
        lax.psum_scatter(grad_out, ("dp", "blk"), scatter_dimension=0, tiled=True),
        lax.psum_scatter(grad_up, ("dp", "blk"), scatter_dimension=0, tiled=True),
        lax.psum_scatter(grad_down, ("dp", "blk"), scatter_dimension=0, tiled=True),
        lax.psum_scatter(grad_gain_one, ("dp", "blk"), scatter_dimension=0, tiled=True),
        lax.psum_scatter(grad_bias_one, ("dp", "blk"), scatter_dimension=0, tiled=True),
        lax.psum_scatter(grad_gain_two, ("dp", "blk"), scatter_dimension=0, tiled=True),
        lax.psum_scatter(grad_bias_two, ("dp", "blk"), scatter_dimension=0, tiled=True),
        lax.psum_scatter(grad_gain_three, ("dp", "blk"), scatter_dimension=0, tiled=True),
        lax.psum_scatter(grad_bias_three, ("dp", "blk"), scatter_dimension=0, tiled=True),
        lax.psum_scatter(grad_gain_four, ("dp", "blk"), scatter_dimension=0, tiled=True),
        lax.psum_scatter(grad_bias_four, ("dp", "blk"), scatter_dimension=0, tiled=True),
    )
    return (output, input_grad) + tuple(summed)


F32 = jnp.float32
BF16 = jnp.bfloat16
VMEM_BYTES = 56 * 1024 * 1024
CORE, Y_LINK, X_LINK, Z_LINK = 1, 2, 4, 8
Z_MASKS = (0, 8, 16, 24)
PLANE_MASKS = (0, Y_LINK, X_LINK, X_LINK + Y_LINK)


def swap(value, mask):
    devices = lax.axis_size("dp") * lax.axis_size("blk")
    return lax.ppermute(value, ("dp", "blk"), [(i, i ^ mask) for i in range(devices)])


def dot_rows(a, b):
    return lax.dot_general(a, b, (((1,), (0,)), ((), ())), preferred_element_type=F32)


def dot_back(a, b):
    return lax.dot_general(a, b, (((1,), (1,)), ((), ())), preferred_element_type=F32)


def dot_outer(a, b):
    return lax.dot_general(a, b, (((0,), (0,)), ((), ())), preferred_element_type=F32)


def row_stats(values):
    centre = jnp.mean(values, -1, keepdims=True)
    centred = values - centre
    spread = jnp.mean(centred * centred, -1, keepdims=True)
    scale = lax.rsqrt(spread + epsilon)
    return centred * scale, scale


def norm_back(grad_unit, unit, scale):
    first = jnp.mean(grad_unit, -1, keepdims=True)
    second = jnp.mean(grad_unit * unit, -1, keepdims=True)
    return scale * (grad_unit - first - unit * second)


def run_copies(copies):
    for copy in copies:
        copy.start()


def wait_copies(copies):
    for copy in copies:
        copy.wait()


def regroup(quarter):
    size = 16 * quarter
    row = lax.broadcasted_iota(jnp.int32, (size, size), 0)
    column = lax.broadcasted_iota(jnp.int32, (size, size), 1)
    device, rest = row // (4 * quarter), row % (4 * quarter)
    return column == (rest // quarter) * 4 * quarter + device * quarter + rest % quarter


def attention_forward(
    pos, t0, t1, t2, t3, source, normed, proj, weight, vectors, att, sems
):
    rows, width = t0.shape
    slot_rows = source.shape[2]
    head_dim = width // HEADS
    span = att.shape[2]
    heads = span // head_dim
    blk = pos[1]
    copies = []
    for x in range(2):
        for z in range(4):
            at = pl.ds((2 * z + x) * slot_rows, slot_rows)
            copies.append(
                pltpu.make_async_copy(source.at[x, z], weight.at[at], sems.at[x * 4 + z])
            )
    run_copies(copies)
    wait_copies(copies)
    tail = (3 * span // 128) * 128
    first = 3 * span - tail
    turned = jnp.transpose(weight[:, tail:].astype(F32))
    vectors[...] = turned[first : first + 16, :]
    gain, bias = vectors[0:1, :], vectors[1:2, :]
    for k, source in enumerate((t0, t1, t2, t3)):
        unit, _ = row_stats(source[...].astype(F32))
        at = pl.ds(pl.multiple_of((blk ^ k) * rows, rows), rows)
        value = (unit * gain + bias).astype(BF16)
        normed[at, :] = value
        proj[at, :] = dot_rows(value, weight[...]).astype(BF16)
    scale = head_dim ** (-0.5)
    below = lax.broadcasted_iota(jnp.int32, (rows, rows), 1) <= lax.broadcasted_iota(
        jnp.int32, (rows, rows), 0
    )
    for block in range(4):
        mixed = []
        low, high = block * rows, (block + 1) * rows
        for head in range(heads):
            q = proj[low:high, head * head_dim : (head + 1) * head_dim] * BF16(scale)
            k = proj[:high, span + head * head_dim : span + (head + 1) * head_dim]
            v = proj[:high, 2 * span + head * head_dim : 2 * span + (head + 1) * head_dim]
            own = jnp.where(below, dot_back(q, k[low:]), masked_score)
            peak = jnp.max(own, -1, keepdims=True)
            if block:
                past = dot_back(q, k[:low])
                peak = jnp.maximum(peak, jnp.max(past, -1, keepdims=True))
            own = jnp.exp(own - peak)
            total = jnp.sum(own, -1, keepdims=True)
            mix = dot_rows(own.astype(BF16), v[low:])
            if block:
                past = jnp.exp(past - peak)
                total = total + jnp.sum(past, -1, keepdims=True)
                mix = mix + dot_rows(past.astype(BF16), v[:low])
            mixed.append(mix / total)
        att[block] = jnp.concatenate(mixed, axis=1).astype(BF16)


def wide_vector(vectors, start):
    return jnp.concatenate([vectors[start + q : start + q + 1, :] for q in range(4)], axis=1)


def ffn_forward(
    pos, att, tokens, vectors, weights,
    acts, middle, unit_four, slope, scale_four,
    w_out, w_up, up, sems,
):
    rows, width = tokens.shape
    copies = [
        pltpu.make_async_copy(weights.at[:, pl.ds(0, width)], w_out, sems.at[0]),
        pltpu.make_async_copy(weights.at[:, pl.ds(width, w_up.shape[1])], w_up, sems.at[1]),
    ]
    run_copies(copies)
    attended = jnp.concatenate([att[j] for j in range(4)], axis=1).astype(F32)
    unit, _ = row_stats(attended)
    inner_low = (unit * vectors[2:3, :] + vectors[3:4, :]).astype(BF16)
    wide = w_up.shape[1]
    acts[:, wide + width :] = inner_low
    copies[0].wait()
    mid = tokens[...].astype(F32) + dot_rows(inner_low, w_out[...])
    middle[...] = mid
    unit, _ = row_stats(mid)
    low = (unit * vectors[4:5, :] + vectors[5:6, :]).astype(BF16)
    acts[:, wide : wide + width] = low
    copies[1].wait()
    up[...] = dot_rows(low, w_up[...])
    step = 16
    gain, bias = wide_vector(vectors, 6), wide_vector(vectors, 10)

    def chunk(i, carry):
        at = pl.ds(pl.multiple_of(i * step, step), step)
        value = up[at, :]
        gate = 0.5 * (1.0 + lax.erf(value * (2.0**-0.5)))
        slope[at, :] = (gate + value * jnp.exp(-0.5 * value * value) * (0.5 / math.pi) ** 0.5).astype(
            BF16
        )
        unit, scale = row_stats(value * gate)
        unit_four[at, :] = unit.astype(BF16)
        acts[at, :wide] = (unit * gain + bias).astype(BF16)
        scale_four[at, :] = jnp.broadcast_to(scale, (step, 128))
        return carry

    lax.fori_loop(0, rows // step, chunk, 0)


def ffn_backward(
    pos, att, cot, vectors, middle, acts, unit_four, slope, scale_four, weights,
    output, grads, d_middle, d0, d1, d2, d3, vector_grads, wide_grads,
    w_down, w_out, w_up, d_hidden, sums, sems,
):
    rows, width = cot.shape
    first = width + w_up.shape[1]
    copies = [
        pltpu.make_async_copy(
            weights.at[:, pl.ds(first + q * width, width)],
            w_down.at[pl.ds(q * width, width)],
            sems.at[q],
        )
        for q in range(4)
    ]
    later = [
        pltpu.make_async_copy(weights.at[:, pl.ds(0, width)], w_out, sems.at[4]),
        pltpu.make_async_copy(weights.at[:, pl.ds(width, w_up.shape[1])], w_up, sems.at[5]),
    ]
    run_copies(copies)
    run_copies(later)
    wait_copies(copies)
    d_hidden[...] = dot_back(cot[...], w_down[...])
    output[...] = (middle[...] + dot_rows(acts[:, : w_up.shape[1]], w_down[...])).astype(BF16)
    step = 16
    sums[...] = jnp.zeros_like(sums)
    gain = wide_vector(vectors, 6)

    def chunk(i, carry):
        at = pl.ds(pl.multiple_of(i * step, step), step)
        grad = d_hidden[at, :]
        unit = unit_four[at, :].astype(F32)
        part = grad * unit
        sums[0] += part[:8] + part[8:]
        sums[1] += grad[:8] + grad[8:]
        d_gelu = norm_back(grad * gain, unit, scale_four[at, 0:1])
        grads[at, : w_up.shape[1]] = (d_gelu * slope[at, :].astype(F32)).astype(BF16)
        return carry

    lax.fori_loop(0, rows // step, chunk, 0)
    lines = []
    for i in range(2):
        line = jnp.sum(sums[i], 0, keepdims=True)
        lines += [line[:, q * width : (q + 1) * width] for q in range(4)]
    wide_grads[...] = jnp.concatenate(lines, axis=0)
    wait_copies(later)
    d_normed = dot_back(grads[:, : w_up.shape[1]], w_up[...])
    unit, scale = row_stats(middle[...])
    gain_three = jnp.sum(d_normed * unit, 0, keepdims=True)
    bias_three = jnp.sum(d_normed, 0, keepdims=True)
    d_mid = cot[...].astype(F32) + norm_back(d_normed * vectors[4:5, :], unit, scale)
    d_middle[...] = d_mid
    d_mid_low = d_mid.astype(BF16)
    grads[:, w_up.shape[1] :] = d_mid_low
    d_inner = dot_back(d_mid_low, w_out[...])
    attended = jnp.concatenate([att[j] for j in range(4)], axis=1).astype(F32)
    unit, scale = row_stats(attended)
    gain_two = jnp.sum(d_inner * unit, 0, keepdims=True)
    bias_two = jnp.sum(d_inner, 0, keepdims=True)
    vector_grads[...] = jnp.concatenate(
        [gain_two, bias_two, gain_three, bias_three, jnp.zeros((4, width), F32)], axis=0
    )
    back = norm_back(d_inner * vectors[2:3, :], unit, scale).astype(BF16)
    span = width // 4
    parts = [back[:, j * span : (j + 1) * span] for j in range(4)]
    for k, target in enumerate((d0, d1, d2, d3)):
        value = parts[k]
        for j in range(4):
            if j != k:
                value = jnp.where((pos[1] ^ k) == j, parts[j], value)
        target[...] = value


def send_pieces(pos, held, targets, sems):
    chip = pos[0] * 2 + pos[1] // 2
    copies = []
    for start, masks, target in targets:
        for i, plane in enumerate(masks):
            for z in range(4):
                slot = ((chip ^ plane) & 3) + 4 * z
                copies.append(
                    pltpu.make_async_copy(
                        held.at[slot, :, pl.ds(start, target.shape[3])],
                        target.at[i, z],
                        sems.at[len(copies)],
                    )
                )
    run_copies(copies)
    wait_copies(copies)


def down_grads(pos, a0, a1, c0, c1, held):
    rows = held.shape[2]
    width = c0.shape[1]
    half = width // 2
    plane = 2 * (pos[0] % 2) + pos[1] // 2
    first = pos[1] % 2 == 0
    cots = [jnp.where(first, c[:, :half], c[:, half:]) for c in (c0, c1)]
    for q in range(4):
        for t in range(0, width, 384):
            at = slice(q * width + t, q * width + t + 384)
            value = dot_outer(a0[:, at], cots[0]) + dot_outer(a1[:, at], cots[1])
            value = value.astype(BF16)
            for i in range(384 // rows):
                chip = t // rows + i
                held[chip // 4, (chip % 4) ^ plane, :, q * half : (q + 1) * half] = value[
                    i * rows : (i + 1) * rows
                ]


def up_grads(pos, a0, a1, g0, g1, keep_a, send_a, keep_b, send_b, held, sems):
    rows = held.shape[1]
    first = pos[1] % 2 == 0

    wide = a0.shape[1] * 2 // 3
    width = wide // 4

    def mine(ref, start, columns):
        half = columns // 2
        low, high = ref[:, start : start + half], ref[:, start + half : start + columns]
        return jnp.where(first, low, high)

    def fill(lefts, rights, start):
        columns = rights[0].shape[1]
        tile = 384
        for r in range(0, 768, tile):
            for c in range(0, columns, 384):
                value = dot_outer(lefts[0][:, r : r + tile], rights[0][:, c : c + 384])
                value = value + dot_outer(lefts[1][:, r : r + tile], rights[1][:, c : c + 384])
                value = value.astype(BF16)
                for s in range(tile // rows):
                    held[r // rows + s, :, start + c : start + c + 384] = value[
                        s * rows : (s + 1) * rows
                    ]

    acts = (a0, a1)
    inner = [ref[:, wide + width :] for ref in acts]
    fill(inner, [mine(ref, wide, width) for ref in (g0, g1)], 0)
    normed_two = [ref[:, wide : wide + width] for ref in acts]
    fill(normed_two, [mine(ref, 0, wide) for ref in (g0, g1)], width // 2)
    cut = keep_a.shape[3]
    pieces = ((0, (0, 1), keep_a), (0, (2, 3), send_a), (cut, (0, 2), keep_b), (cut, (1, 3), send_b))
    send_pieces(pos, held, pieces, sems)


def attention_backward(
    pos, t0, t1, t2, t3, d0, d1, d2, d3, normed, proj, weight, vector_grads, wide_grads,
    own, other, p0, p1, d_out, d_proj, total, held, d_normed, sems,
):
    rows, width = t0.shape
    head_dim = width // HEADS
    span = d_out.shape[1]
    heads = span // head_dim
    dp, blk = pos[0], pos[1]
    for k, source in enumerate((d0, d1, d2, d3)):
        d_out[pl.ds(pl.multiple_of((blk ^ k) * rows, rows), rows), :] = source[...]
    scale = head_dim ** (-0.5)
    below = lax.broadcasted_iota(jnp.int32, (rows, rows), 1) <= lax.broadcasted_iota(
        jnp.int32, (rows, rows), 0
    )
    for head in range(heads):
        at_q = slice(head * head_dim, (head + 1) * head_dim)
        at_k = slice(span + head * head_dim, span + (head + 1) * head_dim)
        at_v = slice(2 * span + head * head_dim, 2 * span + (head + 1) * head_dim)
        total[...] = jnp.zeros_like(total)
        for block in range(4):
            low, high = block * rows, (block + 1) * rows
            q = proj[low:high, at_q] * BF16(scale)
            d = d_out[low:high, at_q]
            parts = [(low, high)] + ([(0, low)] if block else [])
            scores = []
            for part, (start, end) in enumerate(parts):
                score = dot_back(q, proj[start:end, at_k])
                scores.append(score if part else jnp.where(below, score, masked_score))
            peak = functools.reduce(
                jnp.maximum, [jnp.max(score, -1, keepdims=True) for score in scores]
            )
            scores = [jnp.exp(score - peak) for score in scores]
            inverse = 1.0 / sum(jnp.sum(score, -1, keepdims=True) for score in scores)
            scores = [score * inverse for score in scores]
            d_weights = [dot_back(d, proj[start:end, at_v]) for start, end in parts]
            delta = sum(
                jnp.sum(score * grad, -1, keepdims=True) for score, grad in zip(scores, d_weights)
            )
            d_query = 0.0
            for (start, end), score, grad in zip(parts, scores, d_weights):
                d_score = (score * (grad - delta)).astype(BF16)
                d_query = d_query + dot_rows(d_score, proj[start:end, at_k])
                total[0, start:end] += dot_outer(d_score, q)
                total[1, start:end] += dot_outer(score.astype(BF16), d)
            d_proj[low:high, at_q] = (d_query * scale).astype(BF16)
        d_proj[:, at_k] = total[0].astype(BF16)
        d_proj[:, at_v] = total[1].astype(BF16)
    columns = weight.shape[1]
    vector_sums = []
    for k, source in enumerate((t0, t1, t2, t3)):
        at = pl.ds(pl.multiple_of((blk ^ k) * rows, rows), rows)
        grad = dot_back(d_proj[at, :], weight[:, : 3 * span])
        unit, _ = row_stats(source[...].astype(F32))
        vector_sums.append((jnp.sum(grad * unit, 0, keepdims=True), jnp.sum(grad, 0, keepdims=True)))
        d_normed[k] = grad.astype(BF16)
    own[0], own[1] = d_normed[0], d_normed[2]
    other[0], other[1] = d_normed[1], d_normed[3]
    sums = [sum(v[i] for v in vector_sums) for i in range(2)]
    turned = jnp.transpose(
        jnp.concatenate(
            sums + [vector_grads[0:4, :], wide_grads[...], jnp.zeros((128 - 14, width), F32)],
            axis=0,
        )
    )
    slot_rows = held.shape[1]
    for r in range(0, width, 2 * slot_rows):
        value = dot_outer(normed[:, r : r + 2 * slot_rows], d_proj[...])
        value = jnp.concatenate(
            [value, turned[r : r + 2 * slot_rows, : columns - 3 * span]], axis=1
        ).astype(BF16)
        held[r // slot_rows] = value[:slot_rows]
        held[r // slot_rows + 1] = value[slot_rows:]
    copies = []
    for x, target in enumerate((p0, p1)):
        for z in range(4):
            slot = ((dp ^ x) & 1) + 2 * z
            copies.append(pltpu.make_async_copy(held.at[slot], target.at[z], sems.at[x * 4 + z]))
    run_copies(copies)
    wait_copies(copies)


def local_kernel(kernel, outs, ins, scratch=(), us=2, in_any=(), out_any=(), after=(), passed=()):
    here = pl.BlockSpec(memory_space=pltpu.VMEM)
    far = pl.BlockSpec(memory_space=pl.ANY)
    specs = [pl.BlockSpec(memory_space=pltpu.SMEM)]
    specs += [far if i in in_any else here for i in range(1, len(ins))]
    specs += [far] * (len(after) + len(passed))
    unread = len(ins) + len(after) + len(passed)
    ends = unread + len(outs)

    def run(*refs):
        kernel(*refs[: len(ins)], *refs[unread:ends], *refs[ends + len(passed) :])

    return pl.pallas_call(
        run,
        out_shape=[*outs, *(shape_of(v.dtype, *v.shape) for v in passed)],
        in_specs=specs,
        out_specs=[far if i in out_any else here for i in range(len(outs))] + [far] * len(passed),
        input_output_aliases={
            len(ins) + len(after) + i: len(outs) + i for i in range(len(passed))
        },
        scratch_shapes=list(scratch),
        compiler_params=pltpu.CompilerParams(vmem_limit_bytes=VMEM_BYTES),
        cost_estimate=pl.CostEstimate(
            flops=int(us * 1.15e9) // 100, bytes_accessed=int(us * 3.6e6) // 100, transcendentals=0
        ),
    )(*ins, *after, *passed)


def shape_of(dtype, *shape):
    return jax.ShapeDtypeStruct(shape, dtype)


def z_exchange(own):
    return [own] + [swap(own, mask) for mask in Z_MASKS[1:]]


def pack_wide(pos, w_out, w_up, w_down, packed):
    shard, width = w_out.shape
    packed[:, :width] = w_out[...]
    take = regroup(shard).astype(BF16)
    size = take.shape[0]
    parts = [dot_rows(w_up[:, m : m + size], take) for m in range(0, w_up.shape[1], size)]
    piece = size // 4
    for q in range(4):
        packed[:, (1 + q) * width : (2 + q) * width] = jnp.concatenate(
            [part[:, q * piece : (q + 1) * piece] for part in parts], axis=1
        ).astype(BF16)
    down = w_down[...].astype(F32)
    for q in range(4):
        packed[:, (5 + q) * width : (6 + q) * width] = down[q * shard : (q + 1) * shard].astype(
            BF16
        )


def pack_heads(pos, w_qkv, small, slices):
    width = w_qkv.shape[1] // 3
    span = width // 4
    rows = w_qkv.shape[0]
    lines = [small[i : i + 1, :rows] for i in range(6)]
    lines += [small[i : i + 1, c * rows : (c + 1) * rows] for i in (6, 7) for c in range(4)]
    square = jnp.concatenate(lines + [jnp.zeros((128 - 14, rows), F32)], axis=0)
    square = jnp.concatenate([square, jnp.zeros((128, 128 - rows), F32)], axis=1)
    ends = jnp.transpose(square)[:rows, : slices.shape[2] - 3 * span].astype(BF16)
    for j in range(4):
        parts = [w_qkv[:, p * width + j * span : p * width + (j + 1) * span] for p in range(3)]
        slices[j] = jnp.concatenate(parts + [ends], axis=1)


def sum_first(pos, keep_a, got_a, keep_b, got_b, own_a, send_a, own_b, send_b):
    for keep, got, own, send in ((keep_a, got_a, own_a, send_a), (keep_b, got_b, own_b, send_b)):
        own[...] = keep[0].astype(F32) + got[0].astype(F32)
        send[...] = (keep[1].astype(F32) + got[1].astype(F32)).astype(BF16)


def sum_second(pos, own_a, got_a, own_b, got_b, z0, z1, z2, z3):
    for k, target in enumerate((z0, z1, z2, z3)):
        at = (pos[0] // 2) ^ k
        value = jnp.concatenate(
            [own_a[at] + got_a[at].astype(F32), own_b[at] + got_b[at].astype(F32)], axis=1
        )
        target[...] = value.astype(target.dtype)


def sum_two(pos, p0, p1, z0, z1, z2, z3):
    for k, target in enumerate((z0, z1, z2, z3)):
        at = (pos[0] // 2) ^ k
        target[...] = (p0[at].astype(F32) + p1[at].astype(F32)).astype(target.dtype)


def sum_chips(pos, z0, z1, z2, z3, total):
    total[...] = (z0[...].astype(F32) + z1[...].astype(F32)) + (
        z2[...].astype(F32) + z3[...].astype(F32)
    )


def join_halves(pos, own, got):
    first = pos[1] % 2 == 0
    rows = own.shape[0] // 2
    own_rows = jnp.where(first, own[:rows], own[rows:]).astype(F32)
    got_rows = jnp.where(first, got[:rows], got[rows:]).astype(F32)
    return jnp.where(first, own_rows, got_rows), jnp.where(first, got_rows, own_rows)


def join_down(pos, own, got, target):
    low, high = join_halves(pos, own, got)
    rows = low.shape[0]
    half = target.shape[1] // 2
    for q in range(4):
        target[q * rows : (q + 1) * rows, :half] = low[:, q * half : (q + 1) * half]
        target[q * rows : (q + 1) * rows, half:] = high[:, q * half : (q + 1) * half]


def join_up(pos, own, got, w_out, w_up):
    low, high = join_halves(pos, own, got)
    half = w_out.shape[1] // 2
    w_out[:, :half], w_out[:, half:] = low[:, :half], high[:, :half]
    wide = jnp.concatenate([low[:, half:], high[:, half:]], axis=1)
    take = regroup(w_out.shape[0]).astype(BF16)
    size = take.shape[0]
    piece = size // 4
    width = w_out.shape[1]
    for m in range(w_up.shape[1] // size):
        part = jnp.concatenate(
            [wide[:, q * width + m * piece : q * width + (m + 1) * piece] for q in range(4)], axis=1
        )
        high_part = part.astype(BF16)
        low_part = (part - high_part.astype(F32)).astype(BF16)
        w_up[:, m * size : (m + 1) * size] = dot_back(high_part, take) + dot_back(low_part, take)


def join_heads(pos, parts, grad, ends):
    width = grad.shape[1] // 3
    span = width // 4
    rows = grad.shape[0]
    for j in range(4):
        for p in range(3):
            grad[:, p * width + j * span : p * width + (j + 1) * span] = parts[
                j, :, p * span : (p + 1) * span
            ]
    tail = (3 * span // 128) * 128
    last = (parts[0] + parts[1]) + (parts[2] + parts[3])
    square = jnp.concatenate([last[:, tail:], jnp.zeros((128 - rows, 128), F32)], axis=0)
    ends[...] = jnp.transpose(square)[3 * span - tail : 3 * span - tail + 16]


def input_back(pos, own, core_part, far, tokens, d_middle, vectors, input_grad):
    grad = own[0].astype(F32) + core_part[0].astype(F32) + far[...].astype(F32)
    unit, scale = row_stats(tokens[...].astype(F32))
    input_grad[...] = (d_middle[...] + norm_back(grad * vectors[0:1, :], unit, scale)).astype(BF16)


def far_pair(pos, own, core_part, target):
    target[...] = (own[1].astype(F32) + core_part[1].astype(F32)).astype(BF16)


def groups_of(fixed):
    numbers = range(lax.axis_size("dp") * lax.axis_size("blk"))
    return [[i for i in numbers if i & fixed == j] for j in numbers if j & fixed == j]


def fast_body(
    tokens, cotangent, doc_lengths, w_qkv, w_out, w_up, w_down,
    ln1_gain, ln1_bias, ln2_gain, ln2_bias, ln3_gain, ln3_bias, ln4_gain, ln4_bias,
):
    rows, width = tokens.shape
    shard = w_qkv.shape[0]
    ff = w_up.shape[1]
    head_dim = width // HEADS
    span = width // 4
    group = rows * 4
    columns = -(-(3 * span + 16) // 128) * 128
    up_columns = (width + ff) // 2
    slot_rows = 4 * shard
    both = ("dp", "blk")
    along_z = groups_of(CORE + Y_LINK + X_LINK)
    along_x = groups_of(CORE + Y_LINK + 3 * Z_LINK)
    in_plane = groups_of(CORE + 3 * Z_LINK)
    dp, blk = lax.axis_index("dp"), lax.axis_index("blk")
    pos = jnp.stack([dp, blk]).astype(jnp.int32)

    def gather(value, groups):
        return lax.all_gather(value, both, axis=0, axis_index_groups=groups)

    def scatter(value, groups):
        return lax.psum_scatter(
            value, both, scatter_dimension=0, axis_index_groups=groups, tiled=False
        )

    (packed,) = local_kernel(
        pack_wide, [shape_of(BF16, shard, width + 2 * ff)], [pos, w_out, w_up, w_down]
    )
    weights = lax.all_gather(packed, both, axis=0, tiled=True)
    token_y = swap(tokens, Y_LINK)

    norms = [ln1_gain, ln1_bias, ln2_gain, ln2_bias, ln3_gain, ln3_bias, ln4_gain, ln4_bias]
    small = jnp.stack([jnp.pad(v.astype(F32), (0, 4 * shard - v.shape[0])) for v in norms])
    (slices,) = local_kernel(
        pack_heads, [shape_of(BF16, 4, shard, columns)], [pos, w_qkv, small]
    )
    slices = lax.all_to_all(slices, "blk", 0, 0).reshape(slot_rows, columns)
    slices = gather(slices, along_z)
    slices = gather(slices, along_x)
    token_core, token_both = swap(tokens, CORE), swap(token_y, CORE)

    tokens_group = [tokens, token_core, token_y, token_both]
    normed, proj, weight, vectors, att = local_kernel(
        attention_forward,
        [
            shape_of(BF16, group, width),
            shape_of(BF16, group, columns),
            shape_of(BF16, width, columns),
            shape_of(F32, 16, width),
            shape_of(BF16, 4, rows, span),
        ],
        [pos, *tokens_group, slices],
        [pltpu.SemaphoreType.DMA((8,))],
        in_any=(5,),
        us=11,
    )
    att = lax.all_to_all(att, "blk", 0, 0)

    acts, middle, unit_four, slope, scale_four = local_kernel(
        ffn_forward,
        [
            shape_of(BF16, rows, ff + 2 * width),
            shape_of(F32, rows, width),
            shape_of(BF16, rows, ff),
            shape_of(BF16, rows, ff),
            shape_of(F32, rows, 128),
        ],
        [pos, att, tokens, vectors, weights],
        [
            pltpu.VMEM((width, width), BF16),
            pltpu.VMEM((width, ff), BF16),
            pltpu.VMEM((rows, ff), F32),
            pltpu.SemaphoreType.DMA((2,)),
        ],
        in_any=(4,),
        us=12,
    )
    cot_other = swap(cotangent, CORE)
    acts_other = swap(acts, CORE)
    output, grads, d_middle, d0, d1, d2, d3, vector_grads, wide_grads = local_kernel(
        ffn_backward,
        [
            shape_of(BF16, rows, width),
            shape_of(BF16, rows, ff + width),
            shape_of(F32, rows, width),
            *[shape_of(BF16, rows, span)] * 4,
            shape_of(F32, 8, width),
            shape_of(F32, 8, width),
        ],
        [
            pos, att, cotangent, vectors, middle, acts, unit_four, slope, scale_four, weights,
        ],
        [
            pltpu.VMEM((ff, width), BF16),
            pltpu.VMEM((width, width), BF16),
            pltpu.VMEM((width, ff), BF16),
            pltpu.VMEM((rows, ff), F32),
            pltpu.VMEM((2, 8, ff), F32),
            pltpu.SemaphoreType.DMA((6,)),
        ],
        in_any=(9,),
        us=15,
    )
    d_att = [d0] + [swap(value, k) for k, value in ((1, d1), (2, d2), (3, d3))]
    grads_other = swap(grads, CORE)
    up_rows = width // 16
    (down_parts,) = local_kernel(
        down_grads,
        [shape_of(BF16, 4, 4, up_rows, ff // 2)],
        [pos, acts, acts_other, cotangent, cot_other],
        after=(grads,),
        us=5,
    )
    down_first = scatter(down_parts, along_z)
    down_sum = [down_first[0]] + [swap(down_first[p], PLANE_MASKS[p]) for p in range(1, 4)]
    a_columns = -(-up_columns // 256) * 128
    piece_a = (4, up_rows, a_columns)
    piece_b = (4, up_rows, up_columns - a_columns)
    keep_a, send_a, keep_b, send_b = local_kernel(
        up_grads,
        [shape_of(BF16, 2, *piece_a)] * 2 + [shape_of(BF16, 2, *piece_b)] * 2,
        [pos, acts, acts_other, grads, grads_other],
        [pltpu.VMEM((16, up_rows, up_columns), BF16), pltpu.SemaphoreType.DMA((32,))],
        out_any=range(4),
        after=(down_parts, *d_att[1:]),
    )
    got_a, got_b = swap(send_a, X_LINK), swap(send_b, Y_LINK)

    def z_pieces(summed, kernel, parts, after=()):
        pieces = local_kernel(
            kernel,
            [shape_of(F32 if z == 0 else BF16, *summed) for z in range(4)],
            [pos, *parts],
            after=after,
        )
        return [pieces[0]] + [swap(pieces[z], Z_MASKS[z]) for z in range(1, 4)]

    def total_of(pieces):
        (total,) = local_kernel(sum_chips, [shape_of(F32, *pieces[0].shape)], [pos, *pieces])
        return total

    own_part, other_part, p0, p1 = local_kernel(
        attention_backward,
        [shape_of(BF16, 2, rows, width)] * 2 + [shape_of(BF16, 4, slot_rows, columns)] * 2,
        [pos, *tokens_group, *d_att, normed, proj, weight, vector_grads, wide_grads],
        [
            pltpu.VMEM((group, span), BF16),
            pltpu.VMEM((group, 3 * span), BF16),
            pltpu.VMEM((2, group, head_dim), F32),
            pltpu.VMEM((8, slot_rows, columns), BF16),
            pltpu.VMEM((4, rows, width), BF16),
            pltpu.SemaphoreType.DMA((8,)),
        ],
        out_any=(2, 3),
        after=(keep_a,),
        us=20,
    )
    own_a, send_a, own_b, send_b, other_part, p1 = local_kernel(
        sum_first,
        [
            shape_of(F32, *piece_a),
            shape_of(BF16, *piece_a),
            shape_of(F32, *piece_b),
            shape_of(BF16, *piece_b),
        ],
        [pos, keep_a, got_a, keep_b, got_b],
        passed=(other_part, p1),
    )
    got_a, got_b = swap(send_a, Y_LINK), swap(send_b, X_LINK)
    core_part = swap(other_part, CORE)
    head_got = [p0, swap(p1, X_LINK)]
    (pair_far,) = local_kernel(
        far_pair, [shape_of(BF16, rows, width)], [pos, own_part, core_part]
    )
    far_part = swap(pair_far, Y_LINK)
    up_z = z_pieces((up_rows, up_columns), sum_second, [own_a, got_a, own_b, got_b], (pair_far, *down_sum))
    (input_grad,) = local_kernel(
        input_back,
        [shape_of(BF16, rows, width)],
        [pos, own_part, core_part, far_part, tokens, d_middle, vectors],
    )
    head_z = z_pieces((slot_rows, columns), sum_two, head_got, (up_z[0],))
    head_parts = total_of(head_z).reshape(4, shard, columns)
    head_parts = lax.all_to_all(head_parts, "blk", 0, 0)
    down_sum = total_of(down_sum)
    (grad_down,) = local_kernel(
        join_down, [shape_of(F32, *w_down.shape)], [pos, down_sum, swap(down_sum, CORE)]
    )
    up_sum = total_of(up_z)
    grad_out, grad_up = local_kernel(
        join_up,
        [shape_of(F32, *w_out.shape), shape_of(F32, *w_up.shape)],
        [pos, up_sum, swap(up_sum, CORE)],
    )
    grad_qkv, ends = local_kernel(
        join_heads,
        [shape_of(F32, shard, 3 * width), shape_of(F32, 16, 128)],
        [pos, head_parts],
    )
    ends = ends[:, :shard]
    return (
        output, input_grad, grad_qkv, grad_out, grad_up, grad_down,
        ends[0], ends[1], ends[2], ends[3], ends[4], ends[5],
        ends[6:10].reshape(-1), ends[10:14].reshape(-1),
    )


def layer(*arrays):
    one_document = arrays[2].shape[1] == 1
    if lax.axis_size("dp") == 8 and lax.axis_size("blk") == 4 and one_document:
        return fast_body(*arrays)
    return general_body(*arrays)


def solution(mesh):
    placed = (
        P(("dp", "blk"), None),
        P(("dp", "blk"), None),
        P("dp", None),
        P(("dp", "blk"), None),
        P(("dp", "blk"), None),
        P(("dp", "blk"), None),
        P(("dp", "blk"), None),
        P(("dp", "blk")),
        P(("dp", "blk")),
        P(("dp", "blk")),
        P(("dp", "blk")),
        P(("dp", "blk")),
        P(("dp", "blk")),
        P(("dp", "blk")),
        P(("dp", "blk")),
    )
    return jax.shard_map(
        layer,
        mesh=mesh,
        in_specs=placed,
        out_specs=(
            P(("dp", "blk"), None),
            P(("dp", "blk"), None),
            P(("dp", "blk"), None),
            P(("dp", "blk"), None),
            P(("dp", "blk"), None),
            P(("dp", "blk"), None),
            P(("dp", "blk")),
            P(("dp", "blk")),
            P(("dp", "blk")),
            P(("dp", "blk")),
            P(("dp", "blk")),
            P(("dp", "blk")),
            P(("dp", "blk")),
            P(("dp", "blk")),
        ),
        check_vma=False,
    )
```

```python
import functools
import math

import jax
import jax.numpy as jnp
from jax import lax
from jax.experimental import pallas as pl
from jax.experimental.pallas import tpu as pltpu
from jax.sharding import PartitionSpec as P

HEADS = 12


epsilon = 1e-05
masked_score = -1000000000.0


def shifted(shard, axis, by):
    devices = lax.axis_size(axis)
    pairs = [(i, i + by) for i in range(devices) if 0 <= i + by < devices]
    return lax.ppermute(shard, axis, pairs)


def shifted_2(value, axis, steps):
    count = lax.axis_size(axis)
    pairs = [(source, (source + steps) % count) for source in range(count)]
    return lax.ppermute(value, axis, pairs)


def layer_norm(values, norm_gain, norm_bias):
    centre = jnp.mean(values, -1, keepdims=True)
    centred = values - centre
    spread = jnp.mean(centred * centred, -1, keepdims=True)
    return centred * lax.rsqrt(spread + epsilon) * norm_gain + norm_bias


def ffn_norm(up_value, norm_gain, norm_bias):
    return layer_norm(jax.nn.gelu(up_value, approximate=False), norm_gain, norm_bias)


def doc_place(row_ids, doc_row, row_count, blocks):
    device = row_ids // row_count
    local = row_ids % row_count
    shares = doc_row // blocks
    ends = jnp.cumsum(shares, dtype=jnp.int32)
    starts = ends - shares
    doc = jnp.sum((local[:, None] >= ends[None, :]).astype(jnp.int32), -1, dtype=jnp.int32)
    pick = (doc[:, None] == jnp.arange(doc_row.shape[0], dtype=jnp.int32)[None, :]).astype(
        jnp.int32
    )
    share_of = jnp.sum(pick * shares[None, :], -1, dtype=jnp.int32)
    start_of = jnp.sum(pick * starts[None, :], -1, dtype=jnp.int32)
    return (doc, device * share_of + local - start_of)


def visible(query_doc, query_place, key_doc, key_place):
    return (query_doc[:, None] == key_doc[None, :]) & (key_place[None, :] <= query_place[:, None])


def outer_sum(first_operand, second_operand):
    return lax.dot_general(
        first_operand, second_operand, (((0,), (0,)), ((), ())), preferred_element_type=jnp.float32
    )


def back_product(gradient, weight):
    return lax.dot_general(
        gradient, weight, (((1,), (1,)), ((), ())), preferred_element_type=jnp.float32
    )


def score_grads(
    query_heads, dout_heads, lse_heads, delta_heads, allowed, key_heads, value_heads, score_scale
):
    scores = (
        jnp.einsum("qhd,khd->hqk", query_heads, key_heads, preferred_element_type=jnp.float32)
        * score_scale
    )
    probabilities = jnp.where(allowed[None], jnp.exp(scores - lse_heads[:, :, None]), 0.0)
    weight_grad = jnp.einsum(
        "qhd,khd->hqk", dout_heads, value_heads, preferred_element_type=jnp.float32
    )
    score_grad = (probabilities * (weight_grad - delta_heads[:, :, None])).astype(jnp.bfloat16)
    return (probabilities.astype(jnp.bfloat16), score_grad)


def general_body(
    tokens,
    cotangent,
    doc_lengths,
    w_qkv,
    w_out,
    w_up,
    w_down,
    ln1_gain,
    ln1_bias,
    ln2_gain,
    ln2_bias,
    ln3_gain,
    ln3_bias,
    ln4_gain,
    ln4_bias,
):
    gathered = (
        lax.all_gather(w_qkv, ("dp", "blk"), axis=0, tiled=True),
        lax.all_gather(w_out, ("dp", "blk"), axis=0, tiled=True),
        lax.all_gather(w_up, ("dp", "blk"), axis=0, tiled=True),
        lax.all_gather(w_down, ("dp", "blk"), axis=0, tiled=True),
        lax.all_gather(ln1_gain, ("dp", "blk"), axis=0, tiled=True),
        lax.all_gather(ln1_bias, ("dp", "blk"), axis=0, tiled=True),
        lax.all_gather(ln2_gain, ("dp", "blk"), axis=0, tiled=True),
        lax.all_gather(ln2_bias, ("dp", "blk"), axis=0, tiled=True),
        lax.all_gather(ln3_gain, ("dp", "blk"), axis=0, tiled=True),
        lax.all_gather(ln3_bias, ("dp", "blk"), axis=0, tiled=True),
        lax.all_gather(ln4_gain, ("dp", "blk"), axis=0, tiled=True),
        lax.all_gather(ln4_bias, ("dp", "blk"), axis=0, tiled=True),
    )
    qkv_full, out_full, up_full, down_full = (gathered[0], gathered[1], gathered[2], gathered[3])
    norm_params = [value.astype(jnp.float32) for value in gathered[4:]]
    gain_one, bias_one, gain_two, bias_two, gain_three, bias_three, gain_four, bias_four = (
        norm_params
    )
    row_count, model_width = tokens.shape
    head_dim = model_width // HEADS
    score_scale = head_dim ** (-0.5)
    doc_row = doc_lengths[0]
    blocks = lax.axis_size("blk")
    place_index = lax.axis_index("blk")
    query_doc, query_place = doc_place(
        place_index * row_count + jnp.arange(row_count, dtype=jnp.int32), doc_row, row_count, blocks
    )

    def key_meta(first_row, count):
        return doc_place(first_row + jnp.arange(count, dtype=jnp.int32), doc_row, row_count, blocks)

    residual_in = tokens.astype(jnp.float32)
    normed = layer_norm(residual_in, gain_one, bias_one).astype(jnp.bfloat16)
    projected = jnp.dot(normed, qkv_full, preferred_element_type=jnp.float32).astype(jnp.bfloat16)
    queries = projected[:, :model_width]
    keys_own = projected[:, model_width : 2 * model_width]
    values_own = projected[:, 2 * model_width :]
    query_heads = queries.reshape(row_count, HEADS, head_dim)
    start_state = (
        jnp.full((HEADS, row_count), masked_score, jnp.float32),
        jnp.zeros((HEADS, row_count), jnp.float32),
        jnp.zeros((HEADS, row_count, head_dim), jnp.float32),
    )
    running = start_state
    key_part = lax.all_gather(keys_own, "blk", axis=0, tiled=True)
    value_part = lax.all_gather(values_own, "blk", axis=0, tiled=True)
    part_rows = key_part.shape[0]
    step_rows = math.gcd(part_rows, 512)
    count = part_rows // step_rows

    def one_step(state, element):
        key_block, value_block, block_start = element
        key_doc, key_place = key_meta(block_start, step_rows)
        allowed = visible(query_doc, query_place, key_doc, key_place)
        scores = (
            jnp.einsum(
                "qhd,khd->hqk",
                query_heads,
                key_block.reshape(step_rows, HEADS, head_dim),
                preferred_element_type=jnp.float32,
            )
            * score_scale
        )
        scores = jnp.where(allowed[None], scores, masked_score)
        peak_old, total_old, weighted_old = state
        peak_new = jnp.maximum(peak_old, jnp.max(scores, -1))
        weights = jnp.where(allowed[None], jnp.exp(scores - peak_new[:, :, None]), 0.0)
        factor = jnp.exp(peak_old - peak_new)
        total_new = total_old * factor + jnp.sum(weights, -1)
        weighted_new = weighted_old * factor[:, :, None] + jnp.einsum(
            "hqk,khd->hqd",
            weights.astype(jnp.bfloat16),
            value_block.reshape(step_rows, HEADS, head_dim),
            preferred_element_type=jnp.float32,
        )
        return ((peak_new, total_new, weighted_new), None)

    starts = jnp.arange(count, dtype=jnp.int32) * step_rows
    running, _ = lax.scan(
        one_step,
        running,
        (
            key_part.reshape(count, step_rows, model_width),
            value_part.reshape(count, step_rows, model_width),
            starts,
        ),
    )
    peak_score, total_weight, weighted_sum = running
    log_total = peak_score + jnp.log(total_weight)
    attended = (
        (weighted_sum / total_weight[:, :, None]).transpose(1, 0, 2).reshape(row_count, model_width)
    )
    inner = layer_norm(attended, gain_two, bias_two).astype(jnp.bfloat16)
    middle = residual_in + jnp.dot(inner, out_full, preferred_element_type=jnp.float32)
    normed_two = layer_norm(middle, gain_three, bias_three).astype(jnp.bfloat16)
    up_value = jnp.dot(normed_two, up_full, preferred_element_type=jnp.float32)
    hidden = ffn_norm(up_value, gain_four, bias_four).astype(jnp.bfloat16)
    output = (middle + jnp.dot(hidden, down_full, preferred_element_type=jnp.float32)).astype(
        jnp.bfloat16
    )
    grad_down = outer_sum(hidden, cotangent)
    d_hidden = back_product(cotangent, down_full)
    _, ffn_pullback = jax.vjp(ffn_norm, up_value, gain_four, bias_four)
    d_up, grad_gain_four, grad_bias_four = ffn_pullback(d_hidden)
    d_up_low = d_up.astype(jnp.bfloat16)
    grad_up = outer_sum(normed_two, d_up_low)
    _, third_pullback = jax.vjp(layer_norm, middle, gain_three, bias_three)
    d_middle_norm, grad_gain_three, grad_bias_three = third_pullback(
        back_product(d_up_low, up_full)
    )
    d_middle = cotangent.astype(jnp.float32) + d_middle_norm
    d_middle_low = d_middle.astype(jnp.bfloat16)
    grad_out = outer_sum(inner, d_middle_low)
    _, second_pullback = jax.vjp(layer_norm, attended, gain_two, bias_two)
    d_attended, grad_gain_two, grad_bias_two = second_pullback(back_product(d_middle_low, out_full))
    d_attended_low = d_attended.astype(jnp.bfloat16)
    dout_heads = d_attended_low.reshape(row_count, HEADS, head_dim)
    delta = jnp.einsum(
        "qhd,qhd->hq",
        d_attended_low.astype(jnp.float32).reshape(row_count, HEADS, head_dim),
        attended.reshape(row_count, HEADS, head_dim),
    )

    def turn(turn_index, loop_state):
        kv_now, grads_now, query_grad = loop_state
        source = (place_index - turn_index) % blocks
        key_doc, key_place = key_meta(source * row_count, row_count)
        allowed = visible(query_doc, query_place, key_doc, key_place)
        key_heads = kv_now[0].reshape(row_count, HEADS, head_dim)
        value_heads = kv_now[1].reshape(row_count, HEADS, head_dim)
        probabilities, score_grad = score_grads(
            query_heads, dout_heads, log_total, delta, allowed, key_heads, value_heads, score_scale
        )
        query_grad = (
            query_grad
            + jnp.einsum("hqk,khd->qhd", score_grad, key_heads, preferred_element_type=jnp.float32)
            * score_scale
        )
        key_grad = (
            jnp.einsum("hqk,qhd->khd", score_grad, query_heads, preferred_element_type=jnp.float32)
            * score_scale
        )
        value_grad = jnp.einsum(
            "hqk,qhd->khd", probabilities, dout_heads, preferred_element_type=jnp.float32
        )
        grads_now = grads_now + jnp.stack(
            [key_grad.reshape(row_count, model_width), value_grad.reshape(row_count, model_width)]
        )
        kv_now = shifted(kv_now, "blk", 1)
        grads_now = shifted_2(grads_now.astype(jnp.bfloat16), "blk", 1).astype(grads_now.dtype)
        return (kv_now, grads_now, query_grad)

    loop_start = (
        jnp.stack([keys_own, values_own]),
        jnp.zeros((2, row_count, model_width), jnp.float32),
        jnp.zeros((row_count, HEADS, head_dim), jnp.float32),
    )
    _, kv_grads, query_grad = lax.fori_loop(0, blocks, turn, loop_start)
    key_grad_all = kv_grads[0]
    value_grad_all = kv_grads[1]
    d_projected = jnp.concatenate(
        [query_grad.reshape(row_count, model_width), key_grad_all, value_grad_all], axis=1
    ).astype(jnp.bfloat16)
    grad_qkv = outer_sum(normed, d_projected)
    _, first_pullback = jax.vjp(layer_norm, residual_in, gain_one, bias_one)
    d_input_norm, grad_gain_one, grad_bias_one = first_pullback(back_product(d_projected, qkv_full))
    input_grad = (d_middle + d_input_norm).astype(jnp.bfloat16)
    summed = (
        lax.psum_scatter(grad_qkv, ("dp", "blk"), scatter_dimension=0, tiled=True),
        lax.psum_scatter(grad_out, ("dp", "blk"), scatter_dimension=0, tiled=True),
        lax.psum_scatter(grad_up, ("dp", "blk"), scatter_dimension=0, tiled=True),
        lax.psum_scatter(grad_down, ("dp", "blk"), scatter_dimension=0, tiled=True),
        lax.psum_scatter(grad_gain_one, ("dp", "blk"), scatter_dimension=0, tiled=True),
        lax.psum_scatter(grad_bias_one, ("dp", "blk"), scatter_dimension=0, tiled=True),
        lax.psum_scatter(grad_gain_two, ("dp", "blk"), scatter_dimension=0, tiled=True),
        lax.psum_scatter(grad_bias_two, ("dp", "blk"), scatter_dimension=0, tiled=True),
        lax.psum_scatter(grad_gain_three, ("dp", "blk"), scatter_dimension=0, tiled=True),
        lax.psum_scatter(grad_bias_three, ("dp", "blk"), scatter_dimension=0, tiled=True),
        lax.psum_scatter(grad_gain_four, ("dp", "blk"), scatter_dimension=0, tiled=True),
        lax.psum_scatter(grad_bias_four, ("dp", "blk"), scatter_dimension=0, tiled=True),
    )
    return (output, input_grad) + tuple(summed)


F32 = jnp.float32
BF16 = jnp.bfloat16
VMEM_BYTES = 56 * 1024 * 1024
CORE, Y_LINK, X_LINK, Z_LINK = 1, 2, 4, 8
Z_MASKS = (0, 8, 16, 24)
PLANE_MASKS = (0, Y_LINK, X_LINK, X_LINK + Y_LINK)


def swap(value, mask):
    devices = lax.axis_size("dp") * lax.axis_size("blk")
    return lax.ppermute(value, ("dp", "blk"), [(i, i ^ mask) for i in range(devices)])


def dot_rows(a, b):
    return lax.dot_general(a, b, (((1,), (0,)), ((), ())), preferred_element_type=F32)


def dot_back(a, b):
    return lax.dot_general(a, b, (((1,), (1,)), ((), ())), preferred_element_type=F32)


def dot_outer(a, b):
    return lax.dot_general(a, b, (((0,), (0,)), ((), ())), preferred_element_type=F32)


def row_stats(values):
    centre = jnp.mean(values, -1, keepdims=True)
    centred = values - centre
    spread = jnp.mean(centred * centred, -1, keepdims=True)
    scale = lax.rsqrt(spread + epsilon)
    return centred * scale, scale


def norm_back(grad_unit, unit, scale):
    first = jnp.mean(grad_unit, -1, keepdims=True)
    second = jnp.mean(grad_unit * unit, -1, keepdims=True)
    return scale * (grad_unit - first - unit * second)


def run_copies(copies):
    for copy in copies:
        copy.start()


def wait_copies(copies):
    for copy in copies:
        copy.wait()


def spread_wide(columns, width):
    quarter = width // 32
    run = 4 * quarter
    place = lax.broadcasted_iota(jnp.int32, (run, 4 * run), 1)
    row = lax.broadcasted_iota(jnp.int32, (run, 4 * run), 0)
    lines = []
    for first in (0, 4):
        pieces = []
        for m in range(8):
            piece = 0.0
            for c in range(4):
                want = (row // quarter) * run + c * quarter + row % quarter
                put = (place == want).astype(BF16)
                got = dot_outer(columns[m * run : (m + 1) * run, first : first + 8], put)
                piece = piece + got[c : c + 1]
            pieces.append(piece)
        lines.append(jnp.concatenate(pieces, axis=1))
    return jnp.concatenate(lines, axis=0)


def fold_heads(value):
    rows = value.shape[0] // 2
    last = jnp.concatenate([value[:rows, 128:], value[rows:, 128:]], axis=1)
    return jnp.concatenate([value[:, :128], last], axis=0)


def unfold_heads(value):
    rows = value.shape[0] // 3
    last = value[2 * rows :]
    last = jnp.concatenate([last[:, :64], last[:, 64:]], axis=0)
    return jnp.concatenate([value[: 2 * rows], last], axis=1)


def attention_forward(
    pos, t0, t1, t2, t3, own, other, normed, units, proj, weight, vectors, wide, att, mixed_out, stats, sems
):
    rows, width = t0.shape
    slot_rows = own.shape[1]
    head_dim = width // HEADS
    span = mixed_out.shape[1]
    heads = span // head_dim
    blk = pos[1]
    copies = []
    for x, source in enumerate((own, other)):
        for z in range(4):
            slot = 2 * z + (pos[0] % 2 ^ x)
            at = pl.ds(pl.multiple_of(slot * slot_rows, slot_rows), slot_rows)
            copies.append(
                pltpu.make_async_copy(source.at[z], weight.at[at], sems.at[x * 4 + z])
            )
    run_copies(copies)
    wait_copies(copies)
    tail = (3 * span // 128) * 128
    first = 3 * span - tail
    turned = jnp.transpose(weight[:, tail:].astype(F32))
    vectors[...] = turned[first : first + 8, :]
    wide[...] = spread_wide(weight[:, tail + first + 6 : tail + first + 22], width)
    gain, bias = vectors[0:1, :], vectors[1:2, :]
    for k, source in enumerate((t0, t1, t2, t3)):
        unit, _ = row_stats(source[...].astype(F32))
        at = pl.ds(pl.multiple_of((blk ^ k) * rows, rows), rows)
        value = (unit * gain + bias).astype(BF16)
        normed[at, :] = value
        units[at, :] = unit.astype(BF16)
        proj[at, :] = dot_rows(value, weight[...]).astype(BF16)
    scale = head_dim ** (-0.5)
    below = lax.broadcasted_iota(jnp.int32, (rows, rows), 1) <= lax.broadcasted_iota(
        jnp.int32, (rows, rows), 0
    )
    lane = lax.broadcasted_iota(jnp.int32, (rows, 128), 1)
    for block in range(4):
        mixed = []
        low, high = block * rows, (block + 1) * rows
        stat = jnp.zeros((rows, 128), F32)
        for head in range(heads):
            q = proj[low:high, head * head_dim : (head + 1) * head_dim] * BF16(scale)
            k = proj[:high, span + head * head_dim : span + (head + 1) * head_dim]
            v = proj[:high, 2 * span + head * head_dim : 2 * span + (head + 1) * head_dim]
            own = jnp.where(below, dot_back(q, k[low:]), masked_score)
            peak = jnp.max(own, -1, keepdims=True)
            if block:
                past = dot_back(q, k[:low])
                peak = jnp.maximum(peak, jnp.max(past, -1, keepdims=True))
            own = jnp.exp(own - peak)
            total = jnp.sum(own, -1, keepdims=True)
            mix = dot_rows(own.astype(BF16), v[low:])
            if block:
                past = jnp.exp(past - peak)
                total = total + jnp.sum(past, -1, keepdims=True)
                mix = mix + dot_rows(past.astype(BF16), v[:low])
            mixed.append(mix / total)
            stat = jnp.where(lane == head, peak + jnp.log(total), stat)
        stats[low:high, :] = stat
        value = jnp.concatenate(mixed, axis=1)
        mixed_out[low:high, :] = value
        att[block] = fold_heads(value.astype(BF16))


def ffn_forward(
    pos, att, tokens, vectors, wide_gains, weights,
    hidden, acts, middle, unit_four, slope, scale_four,
    w_out, w_up, up, sems,
):
    rows, width = tokens.shape
    copies = [
        pltpu.make_async_copy(weights.at[:, pl.ds(0, width)], w_out, sems.at[0]),
        pltpu.make_async_copy(weights.at[:, pl.ds(width, w_up.shape[1])], w_up, sems.at[1]),
    ]
    run_copies(copies)
    attended = jnp.concatenate([unfold_heads(att[j]) for j in range(4)], axis=1).astype(F32)
    unit, _ = row_stats(attended)
    inner_low = (unit * vectors[2:3, :] + vectors[3:4, :]).astype(BF16)
    acts[:, width:] = inner_low
    copies[0].wait()
    mid = tokens[...].astype(F32) + dot_rows(inner_low, w_out[...])
    middle[...] = mid
    unit, _ = row_stats(mid)
    low = (unit * vectors[4:5, :] + vectors[5:6, :]).astype(BF16)
    acts[:, :width] = low
    copies[1].wait()
    up[...] = dot_rows(low, w_up[...])
    step = 16
    gain, bias = wide_gains[0:1, :], wide_gains[1:2, :]

    def chunk(i, carry):
        at = pl.ds(pl.multiple_of(i * step, step), step)
        value = up[at, :]
        gate = 0.5 * (1.0 + lax.erf(value * (2.0**-0.5)))
        slope[at, :] = (gate + value * jnp.exp(-0.5 * value * value) * (0.5 / math.pi) ** 0.5).astype(
            BF16
        )
        unit, scale = row_stats(value * gate)
        unit_four[at, :] = unit.astype(BF16)
        hidden[at, :] = (unit * gain + bias).astype(BF16)
        scale_four[at, :] = jnp.broadcast_to(scale, (step, 128))
        return carry

    lax.fori_loop(0, rows // step, chunk, 0)


def down_copies(pos, stacks, target, sems):
    rows = stacks[0].shape[1]
    plane = 2 * (pos[0] % 2) + pos[1] // 2
    copies = []
    for other in range(2):
        for mask in range(4):
            for z in range(4):
                slot = 2 * (4 * z + (plane ^ mask)) + (pos[1] % 2 ^ other)
                copies.append(
                    pltpu.make_async_copy(
                        stacks[other * 4 + mask].at[z],
                        target.at[pl.ds(pl.multiple_of(slot * rows, rows), rows)],
                        sems.at[len(copies)],
                    )
                )
    return copies


def fold(value):
    total = value[:, :128]
    for start in range(128, value.shape[1], 128):
        total = total + value[:, start : start + 128]
    return total


def ffn_backward(
    pos, att, cot, vectors, wide_gains, middle, hidden_far, unit_four, slope, scale_four, weights,
    s0, s1, s2, s3, s4, s5, s6, s7,
    output, grads, d_middle, d0, d1, d2, d3, vector_grads, wide_grads,
    w_down, w_out, w_up, hidden, units, slopes, d_hidden, sems,
):
    rows, width = cot.shape
    wide = w_up.shape[1]
    copies = down_copies(pos, (s0, s1, s2, s3, s4, s5, s6, s7), w_down, sems)
    later = []
    for source, target in (
        (unit_four, units),
        (hidden_far, hidden),
        (slope, slopes),
        (weights.at[:, pl.ds(width, wide)], w_up),
        (weights.at[:, pl.ds(0, width)], w_out),
    ):
        later.append(pltpu.make_async_copy(source, target, sems.at[len(copies) + len(later)]))
    run_copies(copies)
    run_copies(later)
    wait_copies(copies)
    wait_copies(later[:2])

    def first_grad(q):
        return dot_back(cot[...], w_down[q * width : (q + 1) * width, :])

    def fold_rows(value):
        total = value[:8]
        for start in range(8, rows, 8):
            total = total + value[start : start + 8]
        return jnp.sum(total, 0, keepdims=True)

    current = first_grad(0)
    first = jnp.zeros((rows, 128), F32)
    second = jnp.zeros((rows, 128), F32)
    out = middle[...]
    for q in range(4):
        at = slice(q * width, (q + 1) * width)
        if q < 3:
            following = first_grad(q + 1)
        out = out + dot_rows(hidden[:, at], w_down[at, :])
        d_hidden[:, at] = current
        unit = units[:, at].astype(F32)
        part = current * unit
        wide_grads[0:1, at] = fold_rows(part)
        wide_grads[1:2, at] = fold_rows(current)
        gain = wide_gains[0:1, at]
        first = first + fold(current * gain)
        second = second + fold(part * gain)
        current = following
    output[...] = out.astype(BF16)
    first = jnp.sum(first, -1, keepdims=True) * (1.0 / wide)
    second = jnp.sum(second, -1, keepdims=True) * (1.0 / wide)
    scale = scale_four[:, 0:1]
    wait_copies(later[2:])

    def second_grad(q):
        at = slice(q * width, (q + 1) * width)
        grad = d_hidden[:, at] * wide_gains[0:1, at] - first - units[:, at].astype(F32) * second
        grad = (scale * grad * slopes[:, at].astype(F32)).astype(BF16)
        grads[:, at] = grad
        return grad

    d_normed = 0.0
    for q in range(4):
        d_normed = d_normed + dot_back(second_grad(q), w_up[:, q * width : (q + 1) * width])
    unit, scale = row_stats(middle[...])
    gain_three = jnp.sum(d_normed * unit, 0, keepdims=True)
    bias_three = jnp.sum(d_normed, 0, keepdims=True)
    d_mid = cot[...].astype(F32) + norm_back(d_normed * vectors[4:5, :], unit, scale)
    d_middle[...] = d_mid
    d_mid_low = d_mid.astype(BF16)
    grads[:, wide:] = d_mid_low
    d_inner = dot_back(d_mid_low, w_out[...])
    attended = jnp.concatenate([unfold_heads(att[j]) for j in range(4)], axis=1).astype(F32)
    unit, scale = row_stats(attended)
    gain_two = jnp.sum(d_inner * unit, 0, keepdims=True)
    bias_two = jnp.sum(d_inner, 0, keepdims=True)
    vector_grads[...] = jnp.concatenate(
        [gain_two, bias_two, gain_three, bias_three, jnp.zeros((4, width), F32)], axis=0
    )
    back = norm_back(d_inner * vectors[2:3, :], unit, scale).astype(BF16)
    span = width // 4
    parts = [back[:, j * span : (j + 1) * span] for j in range(4)]
    for k, target in enumerate((d0, d1, d2, d3)):
        value = parts[k]
        for j in range(4):
            if j != k:
                value = jnp.where((pos[1] ^ k) == j, parts[j], value)
        target[...] = fold_heads(value)


def piece_copies(pos, held, targets, sems, zs):
    chip = pos[0] * 2 + pos[1] // 2
    copies = []
    for start, masks, target in targets:
        for i, plane in enumerate(masks):
            for z in zs:
                slot = ((chip ^ plane) & 3) + 4 * z
                copies.append(
                    pltpu.make_async_copy(
                        held.at[slot, :, pl.ds(start, target.shape[3])],
                        target.at[i, z],
                        sems.at[len(copies)],
                    )
                )
    return copies


def down_grads(pos, hidden, cot, mine, theirs):
    rows = mine.shape[2]
    plane = 2 * (pos[0] % 2) + pos[1] // 2
    first = pos[1] % 2 == 0
    for pair in range(hidden.shape[1] // (4 * rows)):
        value = dot_outer(hidden[:, 4 * rows * pair : 4 * rows * (pair + 1)], cot[...]).astype(BF16)
        for i in range(2):
            chip = 2 * pair + i
            low, high = value[2 * i * rows : (2 * i + 1) * rows], value[(2 * i + 1) * rows : (2 * i + 2) * rows]
            mine[chip // 4, (chip % 4) ^ plane] = jnp.where(first, low, high)
            theirs[chip // 4, (chip % 4) ^ plane] = jnp.where(first, high, low)


def up_grads(
    pos, acts, acts_other, g0, g1, down_mine, down_got,
    keep_a, send_a, keep_b, send_b, down_grad,
    held, left, right, chosen, down, out_sems, sems,
):
    rows = held.shape[1]
    core = pos[1] % 2
    width = acts.shape[1] // 2
    wide = 4 * width
    copies = []

    def load(source, target):
        copies.append(pltpu.make_async_copy(source, target, sems.at[len(copies)]))
        copies[-1].start()

    for i, source in enumerate((acts, acts_other)):
        load(source, left.at[i])
    for i, source in enumerate((g0, g1)):
        load(source, right.at[i])
    for i, source in enumerate((down_mine, down_got)):
        load(source, down.at[i])
    row = lax.broadcasted_iota(jnp.int32, (width, width // 2), 0)
    column = lax.broadcasted_iota(jnp.int32, (width, width // 2), 1)
    take = (row // rows == 2 * (column // rows) + core) & (row % rows == column % rows)
    take = take.astype(BF16)
    wait_copies(copies[:2])
    for i in range(2):
        for part in range(2):
            at = slice(part * width // 2, (part + 1) * width // 2)
            chosen[i, :, at] = dot_rows(
                left[i, :, part * width : (part + 1) * width], take
            ).astype(BF16)
    cut = keep_a.shape[3]
    pieces = ((0, (0, 1), keep_a), (0, (2, 3), send_a), (cut, (0, 2), keep_b), (cut, (1, 3), send_b))
    tile = 384
    wait_copies(copies[2:4])
    outs = []
    for c in range(0, wide + width, tile):
        from_up = c >= width
        source = c - width if from_up else wide + c
        first = 0 if from_up else width // 2
        value = 0.0
        for i in range(2):
            value = value + dot_outer(
                chosen[i, :, first : first + width // 2], right[i, :, source : source + tile]
            )
        for chip in range(16):
            held[chip, :, c : c + tile] = value[chip * rows : (chip + 1) * rows].astype(BF16)
        if c + tile == cut or c + tile == wide + width:
            part = len(outs)
            outs.append(
                piece_copies(pos, held, pieces[2 * part : 2 * part + 2], out_sems.at[part], range(4))
            )
            run_copies(outs[-1])
    wait_copies(copies[4:])
    for z in range(down.shape[1]):
        down[0, z] = down[0, z] + down[1, z]
    outs.append([pltpu.make_async_copy(down.at[0], down_grad, sems.at[0])])
    run_copies(outs[-1])
    for group in outs:
        wait_copies(group)


def gather_wide(grads, width):
    quarter = width // 32
    run = 4 * quarter
    place = lax.broadcasted_iota(jnp.int32, (run, 4 * run), 1)
    row = lax.broadcasted_iota(jnp.int32, (run, 4 * run), 0)
    lane = lax.broadcasted_iota(jnp.int32, (run, 128), 1)
    rows = jnp.concatenate([grads, jnp.zeros((126, grads.shape[1]), F32)], axis=0).astype(BF16)
    pieces = []
    for m in range(8):
        piece = jnp.zeros((run, 128), F32)
        for c in range(4):
            want = (row // quarter) * run + c * quarter + row % quarter
            put = (place == want).astype(BF16)
            got = dot_back(put, rows[:, m * 4 * run : (m + 1) * 4 * run])
            for v in range(2):
                piece = piece + jnp.where(lane == 6 + 4 * v + c, got[:, v : v + 1], 0.0)
        pieces.append(piece)
    return jnp.concatenate(pieces, axis=0)


def attention_backward(
    pos, d0, d1, d2, d3, normed_far, units_far, proj, weight_far, mixed, stats, vector_grads,
    wide_grads,
    own, own_far, other, p0, p1,
    d_out, d_proj, tt, held, d_normed, normed, units, weight, load_sems, sems,
):
    rows, width = d0.shape[0] * 2 // 3, normed.shape[1]
    loads = [
        pltpu.make_async_copy(source, target, load_sems.at[i])
        for i, (source, target) in enumerate(
            ((weight_far, weight), (units_far, units), (normed_far, normed))
        )
    ]
    run_copies(loads)
    head_dim = width // HEADS
    span = d_out.shape[1]
    heads = span // head_dim
    dp, blk = pos[0], pos[1]
    for k, source in enumerate((d0, d1, d2, d3)):
        d_out[pl.ds(pl.multiple_of((blk ^ k) * rows, rows), rows), :] = unfold_heads(source[...])
    scale = head_dim ** (-0.5)
    below = lax.broadcasted_iota(jnp.int32, (rows, rows), 1) <= lax.broadcasted_iota(
        jnp.int32, (rows, rows), 0
    )
    for head in range(heads):
        at_q = slice(head * head_dim, (head + 1) * head_dim)
        at_k = slice(span + head * head_dim, span + (head + 1) * head_dim)
        at_v = slice(2 * span + head * head_dim, 2 * span + (head + 1) * head_dim)
        tt[...] = jnp.zeros_like(tt)
        for block in range(4):
            low, high = block * rows, (block + 1) * rows
            q = proj[low:high, at_q] * BF16(scale)
            d = d_out[low:high, at_q]
            log_total = stats[low:high, head : head + 1]
            delta = jnp.sum(d.astype(F32) * mixed[low:high, at_q], -1, keepdims=True)
            d_query = 0.0
            for start, end in [(low, high)] + ([(0, low)] if block else []):
                score = dot_back(q, proj[start:end, at_k])
                if start == low:
                    score = jnp.where(below, score, masked_score)
                score = jnp.exp(score - log_total)
                grad = dot_back(d, proj[start:end, at_v])
                d_score = (score * (grad - delta)).astype(BF16)
                d_query = d_query + dot_rows(d_score, proj[start:end, at_k])
                tt[0, :, start:end] += dot_outer(q, d_score)
                tt[1, :, start:end] += dot_outer(d, score.astype(BF16))
            d_proj[low:high, at_q] = (d_query * scale).astype(BF16)
        d_proj[:, at_k] = jnp.transpose(tt[0]).astype(BF16)
        d_proj[:, at_v] = jnp.transpose(tt[1]).astype(BF16)
    columns = weight.shape[1]
    vector_sums = []
    wait_copies(loads[:2])
    for j in range(4):
        at = slice(j * rows, (j + 1) * rows)
        grad = dot_back(d_proj[at, :], weight[:, : 3 * span])
        unit = units[at, :].astype(F32)
        vector_sums.append((jnp.sum(grad * unit, 0, keepdims=True), jnp.sum(grad, 0, keepdims=True)))
        d_normed[j ^ blk] = grad.astype(BF16)
    copies = [
        pltpu.make_async_copy(d_normed.at[k], target, sems.at[8 + k])
        for k, target in enumerate((own, other.at[0], own_far, other.at[1]))
    ]
    run_copies(copies)
    loads[2].wait()
    sums = [sum(v[i] for v in vector_sums) for i in range(2)]
    turned = jnp.transpose(
        jnp.concatenate(
            sums + [vector_grads[0:4, :], jnp.zeros((128 - 6, width), F32)], axis=0
        )
    ) + gather_wide(wide_grads[...], width)
    slot_rows = held.shape[1]
    for r in range(0, width, 2 * slot_rows):
        value = dot_outer(normed[:, r : r + 2 * slot_rows], d_proj[...])
        value = jnp.concatenate(
            [value, turned[r : r + 2 * slot_rows, : columns - 3 * span]], axis=1
        ).astype(BF16)
        held[r // slot_rows] = value[:slot_rows]
        held[r // slot_rows + 1] = value[slot_rows:]
    pieces = []
    for x, target in enumerate((p0, p1)):
        for z in range(4):
            slot = ((dp ^ x) & 1) + 2 * z
            pieces.append(pltpu.make_async_copy(held.at[slot], target.at[z], sems.at[x * 4 + z]))
    run_copies(pieces)
    wait_copies(copies + pieces)


def local_kernel(kernel, outs, ins, scratch=(), us=2, in_any=(), out_any=(), after=(), passed=()):
    here = pl.BlockSpec(memory_space=pltpu.VMEM)
    far = pl.BlockSpec(memory_space=pl.ANY)
    specs = [pl.BlockSpec(memory_space=pltpu.SMEM)]
    specs += [far if i in in_any else here for i in range(1, len(ins))]
    specs += [far] * (len(after) + len(passed))
    unread = len(ins) + len(after) + len(passed)
    ends = unread + len(outs)

    def run(*refs):
        kernel(*refs[: len(ins)], *refs[unread:ends], *refs[ends + len(passed) :])

    return pl.pallas_call(
        run,
        out_shape=[*outs, *(shape_of(v.dtype, *v.shape) for v in passed)],
        in_specs=specs,
        out_specs=[far if i in out_any else here for i in range(len(outs))] + [far] * len(passed),
        input_output_aliases={
            len(ins) + len(after) + i: len(outs) + i for i in range(len(passed))
        },
        scratch_shapes=list(scratch),
        compiler_params=pltpu.CompilerParams(vmem_limit_bytes=VMEM_BYTES),
        cost_estimate=pl.CostEstimate(
            flops=int(us * 1.15e9) // 100, bytes_accessed=int(us * 3.6e6) // 100, transcendentals=0
        ),
    )(*ins, *after, *passed)


def shape_of(dtype, *shape):
    return jax.ShapeDtypeStruct(shape, dtype)


def z_exchange(own):
    return [own] + [swap(own, mask) for mask in Z_MASKS[1:]]


def pack_weights(
    pos, w_qkv, w_out, w_up, gains, wide_gains, packed, slices
):
    rows, width = w_out.shape
    span = width // 4
    packed[:, :width] = w_out[...]
    packed[:, width:] = w_up[...]
    lines = [gains[...]] + [
        wide_gains[i : i + 1, c * rows : (c + 1) * rows] for i in range(2) for c in range(4)
    ]
    square = jnp.concatenate(lines + [jnp.zeros((128 - 14, rows), F32)], axis=0)
    square = jnp.concatenate([square, jnp.zeros((128, 128 - rows), F32)], axis=1)
    ends = jnp.transpose(square)[:rows, : slices.shape[2] - 3 * span].astype(BF16)
    for j in range(4):
        parts = [w_qkv[:, p * width + j * span : p * width + (j + 1) * span] for p in range(3)]
        slices[j] = jnp.concatenate(parts + [ends], axis=1)

def stack_z(pos, b0, b1, b2, b3, target):
    for k, part in enumerate((b0, b1, b2, b3)):
        target[(pos[0] // 2) ^ k] = part[...]


def nothing(pos):
    pass


def sum_first(pos, keep_a, got_a, keep_b, got_b, own_a, send_a, own_b, send_b):
    for keep, got, own, send in ((keep_a, got_a, own_a, send_a), (keep_b, got_b, own_b, send_b)):
        own[...] = keep[0].astype(F32) + got[0].astype(F32)
        send[...] = (keep[1].astype(F32) + got[1].astype(F32)).astype(BF16)


def sum_second(pos, own_a, got_a, own_b, got_b, total):
    cut = own_a.shape[2]
    total[:, :, :cut] = (own_a[...] + got_a[...].astype(F32)).astype(BF16)
    total[:, :, cut:] = (own_b[...] + got_b[...].astype(F32)).astype(BF16)


def sum_two(pos, p0, p1, z0, z1, z2, z3, held, sems):
    copies = [pltpu.make_async_copy(ref, held.at[i], sems.at[i]) for i, ref in enumerate((p0, p1))]
    run_copies(copies)
    wait_copies(copies)
    for k, target in enumerate((z0, z1, z2, z3)):
        at = (pos[0] // 2) ^ k
        target[...] = (held[0, at].astype(F32) + held[1, at].astype(F32)).astype(target.dtype)


def join_heads(pos, parts, grad, e0, e1, e2, e3, e4, e5, e6, e7):
    width = grad.shape[1] // 3
    span = width // 4
    rows = grad.shape[0]
    for j in range(4):
        for p in range(3):
            grad[:, p * width + j * span : p * width + (j + 1) * span] = parts[
                j, :, p * span : (p + 1) * span
            ]
    tail = (3 * span // 128) * 128
    last = (parts[0] + parts[1]) + (parts[2] + parts[3])
    square = jnp.concatenate([last[:, tail:], jnp.zeros((128 - rows, 128), F32)], axis=0)
    ends = jnp.transpose(square)[3 * span - tail : 3 * span - tail + 16]
    for i, target in enumerate((e0, e1, e2, e3, e4, e5)):
        target[...] = ends[i : i + 1, :rows]
    for i, target in enumerate((e6, e7)):
        first = 6 + 4 * i
        target[...] = jnp.concatenate(
            [ends[first + c : first + c + 1, :rows] for c in range(4)], axis=1
        )


def far_pair(pos, own, core_part, target):
    target[...] = (own[...].astype(F32) + core_part[1].astype(F32)).astype(BF16)


def sum_four(pos, p0, p1, p2, p3, total):
    total[...] = (p0[...].astype(F32) + p1[...].astype(F32)) + (
        p2[...].astype(F32) + p3[...].astype(F32)
    )


def input_back(pos, own, core_part, far, tokens, d_middle, vectors, input_grad):
    grad = own[...].astype(F32) + core_part[0].astype(F32) + far[...].astype(F32)
    unit, scale = row_stats(tokens[...].astype(F32))
    input_grad[...] = (d_middle[...] + norm_back(grad * vectors[0:1, :], unit, scale)).astype(BF16)


def groups_of(fixed):
    numbers = range(lax.axis_size("dp") * lax.axis_size("blk"))
    return [[i for i in numbers if i & fixed == j] for j in numbers if j & fixed == j]


def fast_body(
    tokens, cotangent, doc_lengths, w_qkv, w_out, w_up, w_down,
    ln1_gain, ln1_bias, ln2_gain, ln2_bias, ln3_gain, ln3_bias, ln4_gain, ln4_bias,
):
    rows, width = tokens.shape
    shard = w_qkv.shape[0]
    ff = w_up.shape[1]
    head_dim = width // HEADS
    span = width // 4
    group = rows * 4
    columns = -(-(3 * span + 16) // 128) * 128
    slot_rows = 4 * shard
    both = ("dp", "blk")
    along_z = groups_of(CORE + Y_LINK + X_LINK)
    in_plane = groups_of(CORE + 3 * Z_LINK)
    dp, blk = lax.axis_index("dp"), lax.axis_index("blk")
    pos = jnp.stack([dp, blk]).astype(jnp.int32)

    def gather(value, groups):
        return lax.all_gather(value, both, axis=0, axis_index_groups=groups)

    def scatter(value, groups):
        return lax.psum_scatter(
            value, both, scatter_dimension=0, axis_index_groups=groups, tiled=False
        )

    norms = [ln1_gain, ln1_bias, ln2_gain, ln2_bias, ln3_gain, ln3_bias]
    gains = jnp.stack([v.astype(F32) for v in norms])
    wide_gains = jnp.stack([v.astype(F32) for v in (ln4_gain, ln4_bias)])
    packed, slices = local_kernel(
        pack_weights,
        [shape_of(BF16, shard, width + ff), shape_of(BF16, 4, shard, columns)],
        [pos, w_qkv, w_out, w_up, gains, wide_gains],
    )
    weights = lax.all_gather(packed, both, axis=0, tiled=True)

    token_y = swap(tokens, Y_LINK)

    slices = lax.all_to_all(slices, "blk", 0, 0).reshape(slot_rows, columns)
    down_own, slices = local_kernel(
        stack_z,
        [shape_of(BF16, 4, *w_down.shape)],
        [pos, w_down] + [swap(w_down, mask) for mask in Z_MASKS[1:]],
        after=(token_y,),
        passed=(slices,),
    )
    slices = gather(slices, along_z)
    slices, down_own, down_x = local_kernel(
        nothing, [], [pos], passed=(slices, down_own, swap(down_own, X_LINK))
    )
    down_parts = [down_own, swap(down_own, Y_LINK), down_x, swap(down_x, Y_LINK)]
    token_core, token_both = swap(tokens, CORE), swap(token_y, CORE)
    slices_x = swap(slices, X_LINK)

    tokens_group = [tokens, token_core, token_y, token_both]
    packed_rows = rows * 3 // 2
    normed, units, proj, weight, vectors, wide, att, mixed, stats = local_kernel(
        attention_forward,
        [
            shape_of(BF16, group, width),
            shape_of(BF16, group, width),
            shape_of(BF16, group, columns),
            shape_of(BF16, width, columns),
            shape_of(F32, 8, width),
            shape_of(F32, 2, ff),
            shape_of(BF16, 4, packed_rows, 128),
            shape_of(F32, group, span),
            shape_of(F32, group, 128),
        ],
        [pos, *tokens_group, slices, slices_x],
        [pltpu.SemaphoreType.DMA((8,))],
        in_any=(5, 6),
        us=11,
    )
    att, *down_parts = local_kernel(nothing, [], [pos], passed=(att, *down_parts))
    down_all = down_parts + [swap(value, CORE) for value in down_parts]
    att = lax.all_to_all(att, "blk", 0, 0)
    hidden, acts, middle, unit_four, slope, scale_four = local_kernel(
        ffn_forward,
        [
            shape_of(BF16, rows, ff),
            shape_of(BF16, rows, 2 * width),
            shape_of(F32, rows, width),
            shape_of(BF16, rows, ff),
            shape_of(BF16, rows, ff),
            shape_of(F32, rows, 128),
        ],
        [pos, att, tokens, vectors, wide, weights],
        [
            pltpu.VMEM((width, width), BF16),
            pltpu.VMEM((width, ff), BF16),
            pltpu.VMEM((rows, ff), F32),
            pltpu.SemaphoreType.DMA((2,)),
        ],
        in_any=(5,),
        after=down_all[4:],
        us=12,
    )
    down_mine, down_theirs = local_kernel(
        down_grads,
        [shape_of(BF16, 4, 4, *w_down.shape)] * 2,
        [pos, hidden, cotangent],
        us=5,
    )
    down_got = swap(down_theirs, CORE)
    acts_other = swap(acts, CORE)
    output, grads, d_middle, d0, d1, d2, d3, vector_grads, wide_grads = local_kernel(
        ffn_backward,
        [
            shape_of(BF16, rows, width),
            shape_of(BF16, rows, ff + width),
            shape_of(F32, rows, width),
            *[shape_of(BF16, packed_rows, 128)] * 4,
            shape_of(F32, 8, width),
            shape_of(F32, 2, ff),
        ],
        [
            pos, att, cotangent, vectors, wide, middle, hidden, unit_four, slope, scale_four,
            weights, *down_all,
        ],
        [
            pltpu.VMEM((ff, width), BF16),
            pltpu.VMEM((width, width), BF16),
            pltpu.VMEM((width, ff), BF16),
            pltpu.VMEM((rows, ff), BF16),
            pltpu.VMEM((rows, ff), BF16),
            pltpu.VMEM((rows, ff), BF16),
            pltpu.VMEM((rows, ff), F32),
            pltpu.SemaphoreType.DMA((37,)),
        ],
        in_any=(6, 7, 8, *range(10, 19)),
        us=15,
        after=(down_mine,),
    )
    d_att = [d0] + [swap(value, k) for k, value in ((1, d1), (2, d2), (3, d3))]
    grads_other = swap(grads, CORE)
    a_columns = -(-(width + ff) // (2 * 384)) * 384
    piece_a = (4, shard, a_columns)
    piece_b = (4, shard, width + ff - a_columns)
    keep_a, send_a, keep_b, send_b, down_grad = local_kernel(
        up_grads,
        [shape_of(BF16, 2, *piece_a)] * 2
        + [shape_of(BF16, 2, *piece_b)] * 2
        + [shape_of(BF16, *down_mine.shape)],
        [pos, acts, acts_other, grads, grads_other, down_mine, down_got],
        [
            pltpu.VMEM((16, shard, width + ff), BF16),
            pltpu.VMEM((2, rows, 2 * width), BF16),
            pltpu.VMEM((2, rows, width + ff), BF16),
            pltpu.VMEM((2, rows, width), BF16),
            pltpu.VMEM((2, *down_mine.shape), BF16),
            pltpu.SemaphoreType.DMA((2, 16)),
            pltpu.SemaphoreType.DMA((6,)),
        ],
        in_any=range(1, 7),
        out_any=range(5),
        after=d_att[1:],
    )
    down_first = scatter(down_grad, along_z)
    got_a, got_b = swap(send_a, X_LINK), swap(send_b, Y_LINK)

    def total_of(pieces):
        return sum(piece.astype(F32) for piece in pieces)

    own_part, own_far, other_part, p0, p1 = local_kernel(
        attention_backward,
        [shape_of(BF16, rows, width)] * 2
        + [shape_of(BF16, 2, rows, width)]
        + [shape_of(BF16, 4, slot_rows, columns)] * 2,
        [
            pos, *d_att, normed, units, proj, weight, mixed, stats, vector_grads, wide_grads
        ],
        [
            pltpu.VMEM((group, span), BF16),
            pltpu.VMEM((group, 3 * span), BF16),
            pltpu.VMEM((2, head_dim, group), F32),
            pltpu.VMEM((8, slot_rows, columns), BF16),
            pltpu.VMEM((4, rows, width), BF16),
            pltpu.VMEM((group, width), BF16),
            pltpu.VMEM((group, width), BF16),
            pltpu.VMEM((width, columns), BF16),
            pltpu.SemaphoreType.DMA((3,)),
            pltpu.SemaphoreType.DMA((12,)),
        ],
        in_any=(5, 6, 8),
        out_any=range(5),
        after=(keep_a,),
        us=20,
    )
    own_a, send_a, own_b, send_b, other_part = local_kernel(
        sum_first,
        [
            shape_of(F32, *piece_a),
            shape_of(BF16, *piece_a),
            shape_of(F32, *piece_b),
            shape_of(BF16, *piece_b),
        ],
        [pos, keep_a, got_a, keep_b, got_b],
        after=(own_part,),
        passed=(other_part,),
    )
    got_a, got_b = swap(send_a, Y_LINK), swap(send_b, X_LINK)
    core_part = swap(other_part, CORE)
    (pair_far,) = local_kernel(
        far_pair,
        [shape_of(BF16, rows, width)],
        [pos, own_far, core_part],
    )
    far_part = swap(pair_far, Y_LINK)
    up_total, p1 = local_kernel(
        sum_second,
        [shape_of(BF16, 4, shard, width + ff)],
        [pos, own_a, got_a, own_b, got_b],
        after=(pair_far,),
        passed=(p1,),
    )
    up_sum = scatter(up_total, along_z).astype(F32)
    grad_out, grad_up = up_sum[:, :width], up_sum[:, width:]
    *head_z, down_first = local_kernel(
        sum_two,
        [shape_of(F32 if z == 0 else BF16, slot_rows, columns) for z in range(4)],
        [pos, p0, swap(p1, X_LINK)],
        [pltpu.VMEM((2, 4, slot_rows, columns), BF16), pltpu.SemaphoreType.DMA((2,))],
        in_any=(1, 2),
        passed=(down_first,),
    )
    head_z = [head_z[0]] + [swap(head_z[z], Z_MASKS[z]) for z in range(1, 4)]
    down_plane = [down_first[0]] + [
        swap(down_first[k], PLANE_MASKS[k]) for k in range(1, 4)
    ]
    (grad_down,) = local_kernel(
        sum_four, [shape_of(F32, *w_down.shape)], [pos, *down_plane]
    )
    (input_grad,) = local_kernel(
        input_back,
        [shape_of(BF16, rows, width)],
        [pos, own_part, core_part, far_part, tokens, d_middle, vectors],
    )
    head_parts = total_of(head_z).reshape(4, shard, columns)
    head_parts = lax.all_to_all(head_parts, "blk", 0, 0)
    grad_qkv, *ends = local_kernel(
        join_heads,
        [shape_of(F32, shard, 3 * width)]
        + [shape_of(F32, 1, shard)] * 6
        + [shape_of(F32, 1, 4 * shard)] * 2,
        [pos, head_parts],
    )
    ends = [value.reshape(-1) for value in ends]
    return (output, input_grad, grad_qkv, grad_out, grad_up, grad_down, *ends)


def layer(*arrays):
    one_document = arrays[2].shape[1] == 1
    if lax.axis_size("dp") == 8 and lax.axis_size("blk") == 4 and one_document:
        return fast_body(*arrays)
    return general_body(*arrays)


def solution(mesh):
    placed = (
        P(("dp", "blk"), None),
        P(("dp", "blk"), None),
        P("dp", None),
        P(("dp", "blk"), None),
        P(("dp", "blk"), None),
        P(("dp", "blk"), None),
        P(("dp", "blk"), None),
        P(("dp", "blk")),
        P(("dp", "blk")),
        P(("dp", "blk")),
        P(("dp", "blk")),
        P(("dp", "blk")),
        P(("dp", "blk")),
        P(("dp", "blk")),
        P(("dp", "blk")),
    )
    return jax.shard_map(
        layer,
        mesh=mesh,
        in_specs=placed,
        out_specs=(
            P(("dp", "blk"), None),
            P(("dp", "blk"), None),
            P(("dp", "blk"), None),
            P(("dp", "blk"), None),
            P(("dp", "blk"), None),
            P(("dp", "blk"), None),
            P(("dp", "blk")),
            P(("dp", "blk")),
            P(("dp", "blk")),
            P(("dp", "blk")),
            P(("dp", "blk")),
            P(("dp", "blk")),
            P(("dp", "blk")),
            P(("dp", "blk")),
        ),
        check_vma=False,
    )
```

```python
import functools
import math

import jax
import jax.numpy as jnp
from jax import lax
from jax.experimental import pallas as pl
from jax.experimental.pallas import tpu as pltpu
from jax.sharding import PartitionSpec as P

HEADS = 12


epsilon = 1e-05
masked_score = -1000000000.0


def shifted(shard, axis, by):
    devices = lax.axis_size(axis)
    pairs = [(i, i + by) for i in range(devices) if 0 <= i + by < devices]
    return lax.ppermute(shard, axis, pairs)


def shifted_2(value, axis, steps):
    count = lax.axis_size(axis)
    pairs = [(source, (source + steps) % count) for source in range(count)]
    return lax.ppermute(value, axis, pairs)


def layer_norm(values, norm_gain, norm_bias):
    centre = jnp.mean(values, -1, keepdims=True)
    centred = values - centre
    spread = jnp.mean(centred * centred, -1, keepdims=True)
    return centred * lax.rsqrt(spread + epsilon) * norm_gain + norm_bias


def ffn_norm(up_value, norm_gain, norm_bias):
    return layer_norm(jax.nn.gelu(up_value, approximate=False), norm_gain, norm_bias)


def doc_place(row_ids, doc_row, row_count, blocks):
    device = row_ids // row_count
    local = row_ids % row_count
    shares = doc_row // blocks
    ends = jnp.cumsum(shares, dtype=jnp.int32)
    starts = ends - shares
    doc = jnp.sum((local[:, None] >= ends[None, :]).astype(jnp.int32), -1, dtype=jnp.int32)
    pick = (doc[:, None] == jnp.arange(doc_row.shape[0], dtype=jnp.int32)[None, :]).astype(
        jnp.int32
    )
    share_of = jnp.sum(pick * shares[None, :], -1, dtype=jnp.int32)
    start_of = jnp.sum(pick * starts[None, :], -1, dtype=jnp.int32)
    return (doc, device * share_of + local - start_of)


def visible(query_doc, query_place, key_doc, key_place):
    return (query_doc[:, None] == key_doc[None, :]) & (key_place[None, :] <= query_place[:, None])


def outer_sum(first_operand, second_operand):
    return lax.dot_general(
        first_operand, second_operand, (((0,), (0,)), ((), ())), preferred_element_type=jnp.float32
    )


def back_product(gradient, weight):
    return lax.dot_general(
        gradient, weight, (((1,), (1,)), ((), ())), preferred_element_type=jnp.float32
    )


def score_grads(
    query_heads, dout_heads, lse_heads, delta_heads, allowed, key_heads, value_heads, score_scale
):
    scores = (
        jnp.einsum("qhd,khd->hqk", query_heads, key_heads, preferred_element_type=jnp.float32)
        * score_scale
    )
    probabilities = jnp.where(allowed[None], jnp.exp(scores - lse_heads[:, :, None]), 0.0)
    weight_grad = jnp.einsum(
        "qhd,khd->hqk", dout_heads, value_heads, preferred_element_type=jnp.float32
    )
    score_grad = (probabilities * (weight_grad - delta_heads[:, :, None])).astype(jnp.bfloat16)
    return (probabilities.astype(jnp.bfloat16), score_grad)


def general_body(
    tokens,
    cotangent,
    doc_lengths,
    w_qkv,
    w_out,
    w_up,
    w_down,
    ln1_gain,
    ln1_bias,
    ln2_gain,
    ln2_bias,
    ln3_gain,
    ln3_bias,
    ln4_gain,
    ln4_bias,
):
    gathered = (
        lax.all_gather(w_qkv, ("dp", "blk"), axis=0, tiled=True),
        lax.all_gather(w_out, ("dp", "blk"), axis=0, tiled=True),
        lax.all_gather(w_up, ("dp", "blk"), axis=0, tiled=True),
        lax.all_gather(w_down, ("dp", "blk"), axis=0, tiled=True),
        lax.all_gather(ln1_gain, ("dp", "blk"), axis=0, tiled=True),
        lax.all_gather(ln1_bias, ("dp", "blk"), axis=0, tiled=True),
        lax.all_gather(ln2_gain, ("dp", "blk"), axis=0, tiled=True),
        lax.all_gather(ln2_bias, ("dp", "blk"), axis=0, tiled=True),
        lax.all_gather(ln3_gain, ("dp", "blk"), axis=0, tiled=True),
        lax.all_gather(ln3_bias, ("dp", "blk"), axis=0, tiled=True),
        lax.all_gather(ln4_gain, ("dp", "blk"), axis=0, tiled=True),
        lax.all_gather(ln4_bias, ("dp", "blk"), axis=0, tiled=True),
    )
    qkv_full, out_full, up_full, down_full = (gathered[0], gathered[1], gathered[2], gathered[3])
    norm_params = [value.astype(jnp.float32) for value in gathered[4:]]
    gain_one, bias_one, gain_two, bias_two, gain_three, bias_three, gain_four, bias_four = (
        norm_params
    )
    row_count, model_width = tokens.shape
    head_dim = model_width // HEADS
    score_scale = head_dim ** (-0.5)
    doc_row = doc_lengths[0]
    blocks = lax.axis_size("blk")
    place_index = lax.axis_index("blk")
    query_doc, query_place = doc_place(
        place_index * row_count + jnp.arange(row_count, dtype=jnp.int32), doc_row, row_count, blocks
    )

    def key_meta(first_row, count):
        return doc_place(first_row + jnp.arange(count, dtype=jnp.int32), doc_row, row_count, blocks)

    residual_in = tokens.astype(jnp.float32)
    normed = layer_norm(residual_in, gain_one, bias_one).astype(jnp.bfloat16)
    projected = jnp.dot(normed, qkv_full, preferred_element_type=jnp.float32).astype(jnp.bfloat16)
    queries = projected[:, :model_width]
    keys_own = projected[:, model_width : 2 * model_width]
    values_own = projected[:, 2 * model_width :]
    query_heads = queries.reshape(row_count, HEADS, head_dim)
    start_state = (
        jnp.full((HEADS, row_count), masked_score, jnp.float32),
        jnp.zeros((HEADS, row_count), jnp.float32),
        jnp.zeros((HEADS, row_count, head_dim), jnp.float32),
    )
    running = start_state
    key_part = lax.all_gather(keys_own, "blk", axis=0, tiled=True)
    value_part = lax.all_gather(values_own, "blk", axis=0, tiled=True)
    part_rows = key_part.shape[0]
    step_rows = math.gcd(part_rows, 512)
    count = part_rows // step_rows

    def one_step(state, element):
        key_block, value_block, block_start = element
        key_doc, key_place = key_meta(block_start, step_rows)
        allowed = visible(query_doc, query_place, key_doc, key_place)
        scores = (
            jnp.einsum(
                "qhd,khd->hqk",
                query_heads,
                key_block.reshape(step_rows, HEADS, head_dim),
                preferred_element_type=jnp.float32,
            )
            * score_scale
        )
        scores = jnp.where(allowed[None], scores, masked_score)
        peak_old, total_old, weighted_old = state
        peak_new = jnp.maximum(peak_old, jnp.max(scores, -1))
        weights = jnp.where(allowed[None], jnp.exp(scores - peak_new[:, :, None]), 0.0)
        factor = jnp.exp(peak_old - peak_new)
        total_new = total_old * factor + jnp.sum(weights, -1)
        weighted_new = weighted_old * factor[:, :, None] + jnp.einsum(
            "hqk,khd->hqd",
            weights.astype(jnp.bfloat16),
            value_block.reshape(step_rows, HEADS, head_dim),
            preferred_element_type=jnp.float32,
        )
        return ((peak_new, total_new, weighted_new), None)

    starts = jnp.arange(count, dtype=jnp.int32) * step_rows
    running, _ = lax.scan(
        one_step,
        running,
        (
            key_part.reshape(count, step_rows, model_width),
            value_part.reshape(count, step_rows, model_width),
            starts,
        ),
    )
    peak_score, total_weight, weighted_sum = running
    log_total = peak_score + jnp.log(total_weight)
    attended = (
        (weighted_sum / total_weight[:, :, None]).transpose(1, 0, 2).reshape(row_count, model_width)
    )
    inner = layer_norm(attended, gain_two, bias_two).astype(jnp.bfloat16)
    middle = residual_in + jnp.dot(inner, out_full, preferred_element_type=jnp.float32)
    normed_two = layer_norm(middle, gain_three, bias_three).astype(jnp.bfloat16)
    up_value = jnp.dot(normed_two, up_full, preferred_element_type=jnp.float32)
    hidden = ffn_norm(up_value, gain_four, bias_four).astype(jnp.bfloat16)
    output = (middle + jnp.dot(hidden, down_full, preferred_element_type=jnp.float32)).astype(
        jnp.bfloat16
    )
    grad_down = outer_sum(hidden, cotangent)
    d_hidden = back_product(cotangent, down_full)
    _, ffn_pullback = jax.vjp(ffn_norm, up_value, gain_four, bias_four)
    d_up, grad_gain_four, grad_bias_four = ffn_pullback(d_hidden)
    d_up_low = d_up.astype(jnp.bfloat16)
    grad_up = outer_sum(normed_two, d_up_low)
    _, third_pullback = jax.vjp(layer_norm, middle, gain_three, bias_three)
    d_middle_norm, grad_gain_three, grad_bias_three = third_pullback(
        back_product(d_up_low, up_full)
    )
    d_middle = cotangent.astype(jnp.float32) + d_middle_norm
    d_middle_low = d_middle.astype(jnp.bfloat16)
    grad_out = outer_sum(inner, d_middle_low)
    _, second_pullback = jax.vjp(layer_norm, attended, gain_two, bias_two)
    d_attended, grad_gain_two, grad_bias_two = second_pullback(back_product(d_middle_low, out_full))
    d_attended_low = d_attended.astype(jnp.bfloat16)
    dout_heads = d_attended_low.reshape(row_count, HEADS, head_dim)
    delta = jnp.einsum(
        "qhd,qhd->hq",
        d_attended_low.astype(jnp.float32).reshape(row_count, HEADS, head_dim),
        attended.reshape(row_count, HEADS, head_dim),
    )

    def turn(turn_index, loop_state):
        kv_now, grads_now, query_grad = loop_state
        source = (place_index - turn_index) % blocks
        key_doc, key_place = key_meta(source * row_count, row_count)
        allowed = visible(query_doc, query_place, key_doc, key_place)
        key_heads = kv_now[0].reshape(row_count, HEADS, head_dim)
        value_heads = kv_now[1].reshape(row_count, HEADS, head_dim)
        probabilities, score_grad = score_grads(
            query_heads, dout_heads, log_total, delta, allowed, key_heads, value_heads, score_scale
        )
        query_grad = (
            query_grad
            + jnp.einsum("hqk,khd->qhd", score_grad, key_heads, preferred_element_type=jnp.float32)
            * score_scale
        )
        key_grad = (
            jnp.einsum("hqk,qhd->khd", score_grad, query_heads, preferred_element_type=jnp.float32)
            * score_scale
        )
        value_grad = jnp.einsum(
            "hqk,qhd->khd", probabilities, dout_heads, preferred_element_type=jnp.float32
        )
        grads_now = grads_now + jnp.stack(
            [key_grad.reshape(row_count, model_width), value_grad.reshape(row_count, model_width)]
        )
        kv_now = shifted(kv_now, "blk", 1)
        grads_now = shifted_2(grads_now.astype(jnp.bfloat16), "blk", 1).astype(grads_now.dtype)
        return (kv_now, grads_now, query_grad)

    loop_start = (
        jnp.stack([keys_own, values_own]),
        jnp.zeros((2, row_count, model_width), jnp.float32),
        jnp.zeros((row_count, HEADS, head_dim), jnp.float32),
    )
    _, kv_grads, query_grad = lax.fori_loop(0, blocks, turn, loop_start)
    key_grad_all = kv_grads[0]
    value_grad_all = kv_grads[1]
    d_projected = jnp.concatenate(
        [query_grad.reshape(row_count, model_width), key_grad_all, value_grad_all], axis=1
    ).astype(jnp.bfloat16)
    grad_qkv = outer_sum(normed, d_projected)
    _, first_pullback = jax.vjp(layer_norm, residual_in, gain_one, bias_one)
    d_input_norm, grad_gain_one, grad_bias_one = first_pullback(back_product(d_projected, qkv_full))
    input_grad = (d_middle + d_input_norm).astype(jnp.bfloat16)
    summed = (
        lax.psum_scatter(grad_qkv, ("dp", "blk"), scatter_dimension=0, tiled=True),
        lax.psum_scatter(grad_out, ("dp", "blk"), scatter_dimension=0, tiled=True),
        lax.psum_scatter(grad_up, ("dp", "blk"), scatter_dimension=0, tiled=True),
        lax.psum_scatter(grad_down, ("dp", "blk"), scatter_dimension=0, tiled=True),
        lax.psum_scatter(grad_gain_one, ("dp", "blk"), scatter_dimension=0, tiled=True),
        lax.psum_scatter(grad_bias_one, ("dp", "blk"), scatter_dimension=0, tiled=True),
        lax.psum_scatter(grad_gain_two, ("dp", "blk"), scatter_dimension=0, tiled=True),
        lax.psum_scatter(grad_bias_two, ("dp", "blk"), scatter_dimension=0, tiled=True),
        lax.psum_scatter(grad_gain_three, ("dp", "blk"), scatter_dimension=0, tiled=True),
        lax.psum_scatter(grad_bias_three, ("dp", "blk"), scatter_dimension=0, tiled=True),
        lax.psum_scatter(grad_gain_four, ("dp", "blk"), scatter_dimension=0, tiled=True),
        lax.psum_scatter(grad_bias_four, ("dp", "blk"), scatter_dimension=0, tiled=True),
    )
    return (output, input_grad) + tuple(summed)


F32 = jnp.float32
BF16 = jnp.bfloat16
CORE, Y_LINK, X_LINK, Z_LINK = 1, 2, 4, 8
Z_MASKS = (0, 8, 16, 24)
PLANE_MASKS = (0, Y_LINK, X_LINK, X_LINK + Y_LINK)


def swap(value, mask):
    devices = lax.axis_size("dp") * lax.axis_size("blk")
    return lax.ppermute(value, ("dp", "blk"), [(i, i ^ mask) for i in range(devices)])


def dot_rows(a, b):
    return lax.dot_general(a, b, (((1,), (0,)), ((), ())), preferred_element_type=F32)


def dot_back(a, b):
    return lax.dot_general(a, b, (((1,), (1,)), ((), ())), preferred_element_type=F32)


def dot_outer(a, b):
    return lax.dot_general(a, b, (((0,), (0,)), ((), ())), preferred_element_type=F32)


def row_stats(values):
    centre = jnp.mean(values, -1, keepdims=True)
    centred = values - centre
    spread = jnp.mean(centred * centred, -1, keepdims=True)
    scale = lax.rsqrt(spread + epsilon)
    return centred * scale, scale


def norm_back(grad_unit, unit, scale):
    first = jnp.mean(grad_unit, -1, keepdims=True)
    second = jnp.mean(grad_unit * unit, -1, keepdims=True)
    return scale * (grad_unit - first - unit * second)


def run_copies(copies):
    for copy in copies:
        copy.start()


def wait_copies(copies):
    for copy in copies:
        copy.wait()


def spread_wide(columns, width):
    quarter = width // 32
    run = 4 * quarter
    place = lax.broadcasted_iota(jnp.int32, (run, 4 * run), 1)
    row = lax.broadcasted_iota(jnp.int32, (run, 4 * run), 0)
    lines = []
    for first in (0, 4):
        pieces = []
        for m in range(8):
            piece = 0.0
            for c in range(4):
                want = (row // quarter) * run + c * quarter + row % quarter
                put = (place == want).astype(BF16)
                got = dot_outer(columns[m * run : (m + 1) * run, first : first + 8], put)
                piece = piece + got[c : c + 1]
            pieces.append(piece)
        lines.append(jnp.concatenate(pieces, axis=1))
    return jnp.concatenate(lines, axis=0)


def fold_heads(value):
    rows = value.shape[0] // 2
    last = jnp.concatenate([value[:rows, 128:], value[rows:, 128:]], axis=1)
    return jnp.concatenate([value[:, :128], last], axis=0)


def unfold_heads(value):
    rows = value.shape[0] // 3
    last = value[2 * rows :]
    last = jnp.concatenate([last[:, :64], last[:, 64:]], axis=0)
    return jnp.concatenate([value[: 2 * rows], last], axis=1)


def attention_forward(
    pos, t0, t1, t2, t3, own, other, normed, units, proj, weight, vectors, wide, att, mixed_out, stats
):
    rows, width = t0.shape
    slot_rows = own.shape[1]
    head_dim = width // HEADS
    span = mixed_out.shape[1]
    heads = span // head_dim
    blk = pos[1]
    for x, source in enumerate((own, other)):
        for z in range(4):
            slot = 2 * z + (pos[0] % 2 ^ x)
            at = pl.ds(pl.multiple_of(slot * slot_rows, slot_rows), slot_rows)
            weight[at, :] = source[z]
    tail = (3 * span // 128) * 128
    first = 3 * span - tail
    turned = jnp.transpose(weight[:, tail:].astype(F32))
    vectors[...] = turned[first : first + 8, :]
    wide[...] = spread_wide(weight[:, tail + first + 6 : tail + first + 22], width)
    gain, bias = vectors[0:1, :], vectors[1:2, :]
    for k, source in enumerate((t0, t1, t2, t3)):
        unit, _ = row_stats(source[...].astype(F32))
        at = pl.ds(pl.multiple_of((blk ^ k) * rows, rows), rows)
        value = (unit * gain + bias).astype(BF16)
        normed[at, :] = value
        units[at, :] = unit.astype(BF16)
        proj[at, :] = dot_rows(value, weight[...]).astype(BF16)
    scale = head_dim ** (-0.5)
    below = lax.broadcasted_iota(jnp.int32, (rows, rows), 1) <= lax.broadcasted_iota(
        jnp.int32, (rows, rows), 0
    )
    lane = lax.broadcasted_iota(jnp.int32, (rows, 128), 1)
    for block in range(4):
        mixed = []
        low, high = block * rows, (block + 1) * rows
        stat = jnp.zeros((rows, 128), F32)
        for head in range(heads):
            q = proj[low:high, head * head_dim : (head + 1) * head_dim] * BF16(scale)
            k = proj[:high, span + head * head_dim : span + (head + 1) * head_dim]
            v = proj[:high, 2 * span + head * head_dim : 2 * span + (head + 1) * head_dim]
            own = jnp.where(below, dot_back(q, k[low:]), masked_score)
            peak = jnp.max(own, -1, keepdims=True)
            if block:
                past = dot_back(q, k[:low])
                peak = jnp.maximum(peak, jnp.max(past, -1, keepdims=True))
            own = jnp.exp(own - peak)
            total = jnp.sum(own, -1, keepdims=True)
            mix = dot_rows(own.astype(BF16), v[low:])
            if block:
                past = jnp.exp(past - peak)
                total = total + jnp.sum(past, -1, keepdims=True)
                mix = mix + dot_rows(past.astype(BF16), v[:low])
            mixed.append(mix / total)
            stat = jnp.where(lane == head, peak + jnp.log(total), stat)
        stats[low:high, :] = stat
        value = jnp.concatenate(mixed, axis=1)
        mixed_out[low:high, :] = value
        att[block] = fold_heads(value.astype(BF16))


def ffn_forward(
    pos, att, tokens, vectors, wide_gains, weights,
    hidden, acts, middle, unit_four, slope, scale_four,
    w_out, w_up, up, sems,
):
    rows, width = tokens.shape
    copies = [
        pltpu.make_async_copy(weights.at[:, pl.ds(0, width)], w_out, sems.at[0]),
        pltpu.make_async_copy(weights.at[:, pl.ds(width, w_up.shape[1])], w_up, sems.at[1]),
    ]
    run_copies(copies)
    attended = jnp.concatenate([unfold_heads(att[j]) for j in range(4)], axis=1).astype(F32)
    unit, _ = row_stats(attended)
    inner_low = (unit * vectors[2:3, :] + vectors[3:4, :]).astype(BF16)
    acts[:, width:] = inner_low
    copies[0].wait()
    mid = tokens[...].astype(F32) + dot_rows(inner_low, w_out[...])
    middle[...] = mid
    unit, _ = row_stats(mid)
    low = (unit * vectors[4:5, :] + vectors[5:6, :]).astype(BF16)
    acts[:, :width] = low
    copies[1].wait()
    up[...] = dot_rows(low, w_up[...])
    step = 64
    gain, bias = wide_gains[0:1, :], wide_gains[1:2, :]

    def chunk(i, carry):
        at = pl.ds(pl.multiple_of(i * step, step), step)
        value = up[at, :]
        gate = 0.5 * (1.0 + lax.erf(value * (2.0**-0.5)))
        slope[at, :] = (gate + value * jnp.exp(-0.5 * value * value) * (0.5 / math.pi) ** 0.5).astype(
            BF16
        )
        unit, scale = row_stats(value * gate)
        unit_four[at, :] = unit.astype(BF16)
        hidden[at, :] = (unit * gain + bias).astype(BF16)
        scale_four[at, :] = jnp.broadcast_to(scale, (step, 128))
        return carry

    lax.fori_loop(0, rows // step, chunk, 0, unroll=True)


def down_copies(pos, stacks, target, sems):
    rows = stacks[0].shape[1]
    plane = 2 * (pos[0] % 2) + pos[1] // 2
    copies = []
    for other in range(2):
        for mask in range(4):
            for z in range(4):
                slot = 2 * (4 * z + (plane ^ mask)) + (pos[1] % 2 ^ other)
                copies.append(
                    pltpu.make_async_copy(
                        stacks[other * 4 + mask].at[z],
                        target.at[pl.ds(pl.multiple_of(slot * rows, rows), rows)],
                        sems.at[len(copies)],
                    )
                )
    return copies


def fold(value):
    total = value[:, :128]
    for start in range(128, value.shape[1], 128):
        total = total + value[:, start : start + 128]
    return total


def ffn_backward(
    pos, att, cot, vectors, wide_gains, middle, hidden_far, unit_four, slope, scale_four, weights,
    s0, s1, s2, s3, s4, s5, s6, s7,
    output, grads, d_middle, d0, d1, d2, d3, vector_grads, wide_grads,
    w_down, w_out, w_up, hidden, units, slopes, d_hidden, sems,
):
    rows, width = cot.shape
    wide = w_up.shape[1]
    copies = down_copies(pos, (s0, s1, s2, s3, s4, s5, s6, s7), w_down, sems)
    later = []
    for source, target in (
        (unit_four, units),
        (hidden_far, hidden),
        (slope, slopes),
        (weights.at[:, pl.ds(width, wide)], w_up),
        (weights.at[:, pl.ds(0, width)], w_out),
    ):
        later.append(pltpu.make_async_copy(source, target, sems.at[len(copies) + len(later)]))
    run_copies(copies)
    run_copies(later)
    wait_copies(copies)
    wait_copies(later[:2])

    def first_grad(q):
        return dot_back(cot[...], w_down[q * width : (q + 1) * width, :])

    def fold_rows(value):
        total = value[:8]
        for start in range(8, rows, 8):
            total = total + value[start : start + 8]
        return jnp.sum(total, 0, keepdims=True)

    current = first_grad(0)
    first = jnp.zeros((rows, 128), F32)
    second = jnp.zeros((rows, 128), F32)
    out = middle[...]
    for q in range(4):
        at = slice(q * width, (q + 1) * width)
        if q < 3:
            following = first_grad(q + 1)
        out = out + dot_rows(hidden[:, at], w_down[at, :])
        d_hidden[:, at] = current
        unit = units[:, at].astype(F32)
        part = current * unit
        wide_grads[0:1, at] = fold_rows(part)
        wide_grads[1:2, at] = fold_rows(current)
        gain = wide_gains[0:1, at]
        first = first + fold(current * gain)
        second = second + fold(part * gain)
        current = following
    output[...] = out.astype(BF16)
    first = jnp.sum(first, -1, keepdims=True) * (1.0 / wide)
    second = jnp.sum(second, -1, keepdims=True) * (1.0 / wide)
    scale = scale_four[:, 0:1]
    wait_copies(later[2:])

    def second_grad(q):
        at = slice(q * width, (q + 1) * width)
        grad = d_hidden[:, at] * wide_gains[0:1, at] - first - units[:, at].astype(F32) * second
        grad = (scale * grad * slopes[:, at].astype(F32)).astype(BF16)
        grads[:, at] = grad
        return grad

    d_normed = 0.0
    for q in range(4):
        d_normed = d_normed + dot_back(second_grad(q), w_up[:, q * width : (q + 1) * width])
    unit, scale = row_stats(middle[...])
    gain_three = jnp.sum(d_normed * unit, 0, keepdims=True)
    bias_three = jnp.sum(d_normed, 0, keepdims=True)
    d_mid = cot[...].astype(F32) + norm_back(d_normed * vectors[4:5, :], unit, scale)
    d_middle[...] = d_mid
    d_mid_low = d_mid.astype(BF16)
    grads[:, wide:] = d_mid_low
    d_inner = dot_back(d_mid_low, w_out[...])
    attended = jnp.concatenate([unfold_heads(att[j]) for j in range(4)], axis=1).astype(F32)
    unit, scale = row_stats(attended)
    gain_two = jnp.sum(d_inner * unit, 0, keepdims=True)
    bias_two = jnp.sum(d_inner, 0, keepdims=True)
    vector_grads[...] = jnp.concatenate(
        [gain_two, bias_two, gain_three, bias_three, jnp.zeros((4, width), F32)], axis=0
    )
    back = norm_back(d_inner * vectors[2:3, :], unit, scale).astype(BF16)
    span = width // 4
    parts = [back[:, j * span : (j + 1) * span] for j in range(4)]
    for k, target in enumerate((d0, d1, d2, d3)):
        value = parts[k]
        for j in range(4):
            if j != k:
                value = jnp.where((pos[1] ^ k) == j, parts[j], value)
        target[...] = fold_heads(value)


def piece_copies(pos, held, targets, sems, zs):
    chip = pos[0] * 2 + pos[1] // 2
    copies = []
    for start, masks, target in targets:
        for i, plane in enumerate(masks):
            for z in zs:
                slot = ((chip ^ plane) & 3) + 4 * z
                copies.append(
                    pltpu.make_async_copy(
                        held.at[slot, :, pl.ds(start, target.shape[3])],
                        target.at[i, z],
                        sems.at[len(copies)],
                    )
                )
    return copies


def down_grads(pos, hidden, cot, mine_far, theirs_far, mine, theirs, sems):
    rows = mine.shape[2]
    plane = 2 * (pos[0] % 2) + pos[1] // 2
    first = pos[1] % 2 == 0
    copies = []
    for pair in range(hidden.shape[1] // (4 * rows)):
        value = dot_outer(hidden[:, 4 * rows * pair : 4 * rows * (pair + 1)], cot[...]).astype(BF16)
        for i in range(2):
            chip = 2 * pair + i
            low, high = value[2 * i * rows : (2 * i + 1) * rows], value[(2 * i + 1) * rows : (2 * i + 2) * rows]
            mine[chip // 4, (chip % 4) ^ plane] = jnp.where(first, low, high)
            theirs[chip // 4, (chip % 4) ^ plane] = jnp.where(first, high, low)
        if pair % 2:
            z = pair // 2
            for k, (source, target) in enumerate(((mine, mine_far), (theirs, theirs_far))):
                copies.append(pltpu.make_async_copy(source.at[z], target.at[z], sems.at[k, z]))
                copies[-1].start()
    wait_copies(copies)


def up_grads(
    pos, acts, acts_other, g0, g1, down_mine, down_got,
    keep_a, send_a, keep_b, send_b, down_grad,
    held, left, right, chosen, down, out_sems, sems,
):
    rows = held.shape[1]
    core = pos[1] % 2
    width = acts.shape[1] // 2
    wide = 4 * width
    copies = []

    def load(source, target):
        copies.append(pltpu.make_async_copy(source, target, sems.at[len(copies)]))
        copies[-1].start()

    for i, source in enumerate((acts, acts_other)):
        load(source, left.at[i])
    for i, source in enumerate((g0, g1)):
        load(source, right.at[i])
    for i, source in enumerate((down_mine, down_got)):
        load(source, down.at[i])
    row = lax.broadcasted_iota(jnp.int32, (width, width // 2), 0)
    column = lax.broadcasted_iota(jnp.int32, (width, width // 2), 1)
    take = (row // rows == 2 * (column // rows) + core) & (row % rows == column % rows)
    take = take.astype(BF16)
    wait_copies(copies[:2])
    for i in range(2):
        for part in range(2):
            at = slice(part * width // 2, (part + 1) * width // 2)
            chosen[i, :, at] = dot_rows(
                left[i, :, part * width : (part + 1) * width], take
            ).astype(BF16)
    cut = keep_a.shape[3]
    pieces = ((0, (0, 1), keep_a), (0, (2, 3), send_a), (cut, (0, 2), keep_b), (cut, (1, 3), send_b))
    tile = 384
    wait_copies(copies[2:4])
    outs = []
    for c in range(0, wide + width, tile):
        from_up = c >= width
        source = c - width if from_up else wide + c
        first = 0 if from_up else width // 2
        value = 0.0
        for i in range(2):
            value = value + dot_outer(
                chosen[i, :, first : first + width // 2], right[i, :, source : source + tile]
            )
        for chip in range(16):
            held[chip, :, c : c + tile] = value[chip * rows : (chip + 1) * rows].astype(BF16)
        if c + tile == cut or c + tile == wide + width:
            part = len(outs)
            outs.append(
                piece_copies(pos, held, pieces[2 * part : 2 * part + 2], out_sems.at[part], range(4))
            )
            run_copies(outs[-1])
    wait_copies(copies[4:])
    for z in range(down.shape[1]):
        down[0, z] = down[0, z] + down[1, z]
    outs.append([pltpu.make_async_copy(down.at[0], down_grad, sems.at[0])])
    run_copies(outs[-1])
    for group in outs:
        wait_copies(group)


def gather_wide(grads, width):
    quarter = width // 32
    run = 4 * quarter
    place = lax.broadcasted_iota(jnp.int32, (run, 4 * run), 1)
    row = lax.broadcasted_iota(jnp.int32, (run, 4 * run), 0)
    lane = lax.broadcasted_iota(jnp.int32, (run, 128), 1)
    rows = jnp.concatenate([grads, jnp.zeros((126, grads.shape[1]), F32)], axis=0).astype(BF16)
    pieces = []
    for m in range(8):
        piece = jnp.zeros((run, 128), F32)
        for c in range(4):
            want = (row // quarter) * run + c * quarter + row % quarter
            put = (place == want).astype(BF16)
            got = dot_back(put, rows[:, m * 4 * run : (m + 1) * 4 * run])
            for v in range(2):
                piece = piece + jnp.where(lane == 6 + 4 * v + c, got[:, v : v + 1], 0.0)
        pieces.append(piece)
    return jnp.concatenate(pieces, axis=0)


def attention_backward(
    pos, d0, d1, d2, d3, normed_far, units_far, proj, weight_far, mixed, stats, vector_grads,
    wide_grads,
    own, own_far, other, p0, p1,
    d_out, d_proj, tt, held, d_normed, normed, units, weight, load_sems, sems,
):
    rows, width = d0.shape[0] * 2 // 3, normed.shape[1]
    loads = [
        pltpu.make_async_copy(source, target, load_sems.at[i])
        for i, (source, target) in enumerate(
            ((weight_far, weight), (units_far, units), (normed_far, normed))
        )
    ]
    run_copies(loads)
    head_dim = width // HEADS
    span = d_out.shape[1]
    heads = span // head_dim
    dp, blk = pos[0], pos[1]
    for k, source in enumerate((d0, d1, d2, d3)):
        d_out[pl.ds(pl.multiple_of((blk ^ k) * rows, rows), rows), :] = unfold_heads(source[...])
    scale = head_dim ** (-0.5)
    below = lax.broadcasted_iota(jnp.int32, (rows, rows), 1) <= lax.broadcasted_iota(
        jnp.int32, (rows, rows), 0
    )
    for head in range(heads):
        at_q = slice(head * head_dim, (head + 1) * head_dim)
        at_k = slice(span + head * head_dim, span + (head + 1) * head_dim)
        at_v = slice(2 * span + head * head_dim, 2 * span + (head + 1) * head_dim)
        tt[...] = jnp.zeros_like(tt)
        for block in range(4):
            low, high = block * rows, (block + 1) * rows
            q = proj[low:high, at_q] * BF16(scale)
            d = d_out[low:high, at_q]
            log_total = stats[low:high, head : head + 1]
            delta = jnp.sum(d.astype(F32) * mixed[low:high, at_q], -1, keepdims=True)
            d_query = 0.0
            for start, end in [(low, high)] + ([(0, low)] if block else []):
                score = dot_back(q, proj[start:end, at_k])
                if start == low:
                    score = jnp.where(below, score, masked_score)
                score = jnp.exp(score - log_total)
                grad = dot_back(d, proj[start:end, at_v])
                d_score = (score * (grad - delta)).astype(BF16)
                d_query = d_query + dot_rows(d_score, proj[start:end, at_k])
                tt[0, :, start:end] += dot_outer(q, d_score)
                tt[1, :, start:end] += dot_outer(d, score.astype(BF16))
            d_proj[low:high, at_q] = (d_query * scale).astype(BF16)
        d_proj[:, at_k] = jnp.transpose(tt[0]).astype(BF16)
        d_proj[:, at_v] = jnp.transpose(tt[1]).astype(BF16)
    columns = weight.shape[1]
    vector_sums = []
    wait_copies(loads[:2])
    for j in range(4):
        at = slice(j * rows, (j + 1) * rows)
        grad = dot_back(d_proj[at, :], weight[:, : 3 * span])
        unit = units[at, :].astype(F32)
        vector_sums.append((jnp.sum(grad * unit, 0, keepdims=True), jnp.sum(grad, 0, keepdims=True)))
        d_normed[j ^ blk] = grad.astype(BF16)
    copies = [
        pltpu.make_async_copy(d_normed.at[k], target, sems.at[8 + k])
        for k, target in enumerate((own, other.at[0], own_far, other.at[1]))
    ]
    run_copies(copies)
    loads[2].wait()
    sums = [sum(v[i] for v in vector_sums) for i in range(2)]
    turned = jnp.transpose(
        jnp.concatenate(
            sums + [vector_grads[0:4, :], jnp.zeros((128 - 6, width), F32)], axis=0
        )
    ) + gather_wide(wide_grads[...], width)
    slot_rows = held.shape[1]
    for r in range(0, width, 2 * slot_rows):
        value = dot_outer(normed[:, r : r + 2 * slot_rows], d_proj[...])
        value = jnp.concatenate(
            [value, turned[r : r + 2 * slot_rows, : columns - 3 * span]], axis=1
        ).astype(BF16)
        held[r // slot_rows] = value[:slot_rows]
        held[r // slot_rows + 1] = value[slot_rows:]
    pieces = []
    for x, target in enumerate((p0, p1)):
        for z in range(4):
            slot = ((dp ^ x) & 1) + 2 * z
            pieces.append(pltpu.make_async_copy(held.at[slot], target.at[z], sems.at[x * 4 + z]))
    run_copies(pieces)
    wait_copies(copies + pieces)


def local_kernel(kernel, outs, ins, scratch=(), us=2, in_any=(), out_any=(), after=(), passed=(), mib=16):
    here = pl.BlockSpec(memory_space=pltpu.VMEM)
    far = pl.BlockSpec(memory_space=pl.ANY)
    specs = [pl.BlockSpec(memory_space=pltpu.SMEM)]
    specs += [far if i in in_any else here for i in range(1, len(ins))]
    specs += [far] * (len(after) + len(passed))
    unread = len(ins) + len(after) + len(passed)
    ends = unread + len(outs)

    def run(*refs):
        kernel(*refs[: len(ins)], *refs[unread:ends], *refs[ends + len(passed) :])

    return pl.pallas_call(
        run,
        out_shape=[*outs, *(shape_of(v.dtype, *v.shape) for v in passed)],
        in_specs=specs,
        out_specs=[far if i in out_any else here for i in range(len(outs))] + [far] * len(passed),
        input_output_aliases={
            len(ins) + len(after) + i: len(outs) + i for i in range(len(passed))
        },
        scratch_shapes=list(scratch),
        compiler_params=pltpu.CompilerParams(vmem_limit_bytes=mib * 1024 * 1024),
        cost_estimate=pl.CostEstimate(
            flops=int(us * 1.15e9) // 100, bytes_accessed=int(us * 3.6e6) // 100, transcendentals=0
        ),
    )(*ins, *after, *passed)


def shape_of(dtype, *shape):
    return jax.ShapeDtypeStruct(shape, dtype)


def z_exchange(own):
    return [own] + [swap(own, mask) for mask in Z_MASKS[1:]]


def pack_weights(
    pos, w_qkv, w_out, w_up, gains, wide_gains, packed, slices
):
    rows, width = w_out.shape
    span = width // 4
    packed[:, :width] = w_out[...]
    packed[:, width:] = w_up[...]
    wide = wide_gains[...].astype(F32)
    lines = [gains[...].astype(F32)] + [
        wide[i : i + 1, c * rows : (c + 1) * rows] for i in range(2) for c in range(4)
    ]
    square = jnp.concatenate(lines + [jnp.zeros((128 - 14, rows), F32)], axis=0)
    square = jnp.concatenate([square, jnp.zeros((128, 128 - rows), F32)], axis=1)
    ends = jnp.transpose(square)[:rows, : slices.shape[2] - 3 * span].astype(BF16)
    for j in range(4):
        parts = [w_qkv[:, p * width + j * span : p * width + (j + 1) * span] for p in range(3)]
        slices[j] = jnp.concatenate(parts + [ends], axis=1)

def stack_z(pos, b0, b1, b2, b3, target):
    for k, part in enumerate((b0, b1, b2, b3)):
        target[(pos[0] // 2) ^ k] = part[...]


def nothing(pos):
    pass


def sum_first(pos, keep_a, got_a, keep_b, got_b, own_a, send_a, own_b, send_b):
    for keep, got, own, send in ((keep_a, got_a, own_a, send_a), (keep_b, got_b, own_b, send_b)):
        own[...] = keep[0].astype(F32) + got[0].astype(F32)
        send[...] = (keep[1].astype(F32) + got[1].astype(F32)).astype(BF16)


def sum_second(pos, own_a, got_a, own_b, got_b, total):
    cut = own_a.shape[2]
    total[:, :, :cut] = (own_a[...] + got_a[...].astype(F32)).astype(BF16)
    total[:, :, cut:] = (own_b[...] + got_b[...].astype(F32)).astype(BF16)


def sum_two(pos, p0, p1, z0, z1, z2, z3):
    for k, target in enumerate((z0, z1, z2, z3)):
        at = (pos[0] // 2) ^ k
        target[...] = (p0[at].astype(F32) + p1[at].astype(F32)).astype(target.dtype)


def join_heads(pos, parts, grad, e0, e1, e2, e3, e4, e5, e6, e7):
    width = grad.shape[1] // 3
    span = width // 4
    rows = grad.shape[0]
    for j in range(4):
        for p in range(3):
            grad[:, p * width + j * span : p * width + (j + 1) * span] = parts[
                j, :, p * span : (p + 1) * span
            ]
    tail = (3 * span // 128) * 128
    last = (parts[0] + parts[1]) + (parts[2] + parts[3])
    square = jnp.concatenate([last[:, tail:], jnp.zeros((128 - rows, 128), F32)], axis=0)
    ends = jnp.transpose(square)[3 * span - tail : 3 * span - tail + 16]
    for i, target in enumerate((e0, e1, e2, e3, e4, e5)):
        target[...] = ends[i : i + 1, :rows]
    for i, target in enumerate((e6, e7)):
        first = 6 + 4 * i
        target[...] = jnp.concatenate(
            [ends[first + c : first + c + 1, :rows] for c in range(4)], axis=1
        )


def far_pair(pos, own, core_part, target):
    target[...] = (own[...].astype(F32) + core_part[1].astype(F32)).astype(BF16)


def sum_four(pos, p0, p1, p2, p3, total):
    total[...] = (p0[...].astype(F32) + p1[...].astype(F32)) + (
        p2[...].astype(F32) + p3[...].astype(F32)
    )


def input_back(pos, own, core_part, far, tokens, d_middle, vectors, input_grad):
    grad = own[...].astype(F32) + core_part[0].astype(F32) + far[...].astype(F32)
    unit, scale = row_stats(tokens[...].astype(F32))
    input_grad[...] = (d_middle[...] + norm_back(grad * vectors[0:1, :], unit, scale)).astype(BF16)


def groups_of(fixed):
    numbers = range(lax.axis_size("dp") * lax.axis_size("blk"))
    return [[i for i in numbers if i & fixed == j] for j in numbers if j & fixed == j]


def fast_body(
    tokens, cotangent, doc_lengths, w_qkv, w_out, w_up, w_down,
    ln1_gain, ln1_bias, ln2_gain, ln2_bias, ln3_gain, ln3_bias, ln4_gain, ln4_bias,
):
    rows, width = tokens.shape
    shard = w_qkv.shape[0]
    ff = w_up.shape[1]
    head_dim = width // HEADS
    span = width // 4
    group = rows * 4
    columns = -(-(3 * span + 16) // 128) * 128
    slot_rows = 4 * shard
    both = ("dp", "blk")
    along_z = groups_of(CORE + Y_LINK + X_LINK)
    in_plane = groups_of(CORE + 3 * Z_LINK)
    dp, blk = lax.axis_index("dp"), lax.axis_index("blk")
    pos = jnp.stack([dp, blk]).astype(jnp.int32)

    def gather(value, groups):
        return lax.all_gather(value, both, axis=0, axis_index_groups=groups)

    def scatter(value, groups):
        return lax.psum_scatter(
            value, both, scatter_dimension=0, axis_index_groups=groups, tiled=False
        )

    norms = [ln1_gain, ln1_bias, ln2_gain, ln2_bias, ln3_gain, ln3_bias]
    gains = jnp.stack(norms)
    wide_gains = jnp.stack([ln4_gain, ln4_bias])
    packed, slices = local_kernel(
        pack_weights,
        [shape_of(BF16, shard, width + ff), shape_of(BF16, 4, shard, columns)],
        [pos, w_qkv, w_out, w_up, gains, wide_gains],
    )
    weights = lax.all_gather(packed, both, axis=0, tiled=True)

    token_y = swap(tokens, Y_LINK)

    slices = lax.all_to_all(slices, "blk", 0, 0).reshape(slot_rows, columns)
    down_own, slices = local_kernel(
        stack_z,
        [shape_of(BF16, 4, *w_down.shape)],
        [pos, w_down] + [swap(w_down, mask) for mask in Z_MASKS[1:]],
        after=(token_y,),
        passed=(slices,),
    )
    slices = gather(slices, along_z)
    slices, down_own, down_x = local_kernel(
        nothing, [], [pos], passed=(slices, down_own, swap(down_own, X_LINK)), mib=1
    )
    down_parts = [down_own, swap(down_own, Y_LINK), down_x, swap(down_x, Y_LINK)]
    token_core, token_both = swap(tokens, CORE), swap(token_y, CORE)
    slices_x = swap(slices, X_LINK)

    tokens_group = [tokens, token_core, token_y, token_both]
    packed_rows = rows * 3 // 2
    normed, units, proj, weight, vectors, wide, att, mixed, stats = local_kernel(
        attention_forward,
        [
            shape_of(BF16, group, width),
            shape_of(BF16, group, width),
            shape_of(BF16, group, columns),
            shape_of(BF16, width, columns),
            shape_of(F32, 8, width),
            shape_of(F32, 2, ff),
            shape_of(BF16, 4, packed_rows, 128),
            shape_of(F32, group, span),
            shape_of(F32, group, 128),
        ],
        [pos, *tokens_group, slices, slices_x],
        us=11,
        mib=56,
    )
    att, *down_parts = local_kernel(nothing, [], [pos], mib=56, passed=(att, *down_parts))
    down_all = down_parts + [swap(value, CORE) for value in down_parts]
    att = lax.all_to_all(att, "blk", 0, 0)
    hidden, acts, middle, unit_four, slope, scale_four = local_kernel(
        ffn_forward,
        [
            shape_of(BF16, rows, ff),
            shape_of(BF16, rows, 2 * width),
            shape_of(F32, rows, width),
            shape_of(BF16, rows, ff),
            shape_of(BF16, rows, ff),
            shape_of(F32, rows, 128),
        ],
        [pos, att, tokens, vectors, wide, weights],
        [
            pltpu.VMEM((width, width), BF16),
            pltpu.VMEM((width, ff), BF16),
            pltpu.VMEM((rows, ff), F32),
            pltpu.SemaphoreType.DMA((2,)),
        ],
        in_any=(5,),
        after=down_all[4:],
        us=12,
        mib=56,
    )
    down_mine, down_theirs = local_kernel(
        down_grads,
        [shape_of(BF16, 4, 4, *w_down.shape)] * 2,
        [pos, hidden, cotangent],
        [pltpu.VMEM((4, 4, *w_down.shape), BF16)] * 2 + [pltpu.SemaphoreType.DMA((2, 4))],
        out_any=(0, 1),
        us=5,
        mib=56,
    )
    down_got = swap(down_theirs, CORE)
    acts_other = swap(acts, CORE)
    output, grads, d_middle, d0, d1, d2, d3, vector_grads, wide_grads = local_kernel(
        ffn_backward,
        [
            shape_of(BF16, rows, width),
            shape_of(BF16, rows, ff + width),
            shape_of(F32, rows, width),
            *[shape_of(BF16, packed_rows, 128)] * 4,
            shape_of(F32, 8, width),
            shape_of(F32, 2, ff),
        ],
        [
            pos, att, cotangent, vectors, wide, middle, hidden, unit_four, slope, scale_four,
            weights, *down_all,
        ],
        [
            pltpu.VMEM((ff, width), BF16),
            pltpu.VMEM((width, width), BF16),
            pltpu.VMEM((width, ff), BF16),
            pltpu.VMEM((rows, ff), BF16),
            pltpu.VMEM((rows, ff), BF16),
            pltpu.VMEM((rows, ff), BF16),
            pltpu.VMEM((rows, ff), F32),
            pltpu.SemaphoreType.DMA((37,)),
        ],
        in_any=(6, 7, 8, *range(10, 19)),
        us=15,
        after=(down_mine,),
        mib=56,
    )
    d_att = [d0] + [swap(value, k) for k, value in ((1, d1), (2, d2), (3, d3))]
    grads_other = swap(grads, CORE)
    a_columns = -(-(width + ff) // (2 * 384)) * 384
    piece_a = (4, shard, a_columns)
    piece_b = (4, shard, width + ff - a_columns)
    keep_a, send_a, keep_b, send_b, down_grad = local_kernel(
        up_grads,
        [shape_of(BF16, 2, *piece_a)] * 2
        + [shape_of(BF16, 2, *piece_b)] * 2
        + [shape_of(BF16, *down_mine.shape)],
        [pos, acts, acts_other, grads, grads_other, down_mine, down_got],
        [
            pltpu.VMEM((16, shard, width + ff), BF16),
            pltpu.VMEM((2, rows, 2 * width), BF16),
            pltpu.VMEM((2, rows, width + ff), BF16),
            pltpu.VMEM((2, rows, width), BF16),
            pltpu.VMEM((2, *down_mine.shape), BF16),
            pltpu.SemaphoreType.DMA((2, 16)),
            pltpu.SemaphoreType.DMA((6,)),
        ],
        in_any=range(1, 7),
        out_any=range(5),
        after=d_att[1:],
        mib=56,
    )
    down_first = scatter(down_grad, along_z)
    got_a, got_b = swap(send_a, X_LINK), swap(send_b, Y_LINK)

    def total_of(pieces):
        return sum(piece.astype(F32) for piece in pieces)

    own_part, own_far, other_part, p0, p1 = local_kernel(
        attention_backward,
        [shape_of(BF16, rows, width)] * 2
        + [shape_of(BF16, 2, rows, width)]
        + [shape_of(BF16, 4, slot_rows, columns)] * 2,
        [
            pos, *d_att, normed, units, proj, weight, mixed, stats, vector_grads, wide_grads
        ],
        [
            pltpu.VMEM((group, span), BF16),
            pltpu.VMEM((group, 3 * span), BF16),
            pltpu.VMEM((2, head_dim, group), F32),
            pltpu.VMEM((8, slot_rows, columns), BF16),
            pltpu.VMEM((4, rows, width), BF16),
            pltpu.VMEM((group, width), BF16),
            pltpu.VMEM((group, width), BF16),
            pltpu.VMEM((width, columns), BF16),
            pltpu.SemaphoreType.DMA((3,)),
            pltpu.SemaphoreType.DMA((12,)),
        ],
        in_any=(5, 6, 8),
        out_any=range(5),
        after=(keep_a,),
        us=20,
        mib=56,
    )
    own_a, send_a, own_b, send_b = local_kernel(
        sum_first,
        [
            shape_of(F32, *piece_a),
            shape_of(BF16, *piece_a),
            shape_of(F32, *piece_b),
            shape_of(BF16, *piece_b),
        ],
        [pos, keep_a, got_a, keep_b, got_b],
        after=(own_part,),
    )
    (other_part,) = local_kernel(
        nothing, [], [pos], after=(send_a,), passed=(other_part,), mib=56
    )
    got_a, got_b = swap(send_a, Y_LINK), swap(send_b, X_LINK)
    core_part = swap(other_part, CORE)
    (pair_far,) = local_kernel(
        far_pair,
        [shape_of(BF16, rows, width)],
        [pos, own_far, core_part],
    )
    far_part = swap(pair_far, Y_LINK)
    up_total, p1 = local_kernel(
        sum_second,
        [shape_of(BF16, 4, shard, width + ff)],
        [pos, own_a, got_a, own_b, got_b],
        after=(pair_far,),
        passed=(p1,),
    )
    up_sum = scatter(up_total, along_z).astype(F32)
    grad_out, grad_up = up_sum[:, :width], up_sum[:, width:]
    *head_z, down_first = local_kernel(
        sum_two,
        [shape_of(F32 if z == 0 else BF16, slot_rows, columns) for z in range(4)],
        [pos, p0, swap(p1, X_LINK)],
        passed=(down_first,),
    )
    head_z = [head_z[0]] + [swap(head_z[z], Z_MASKS[z]) for z in range(1, 4)]
    down_plane = [down_first[0]] + [
        swap(down_first[k], PLANE_MASKS[k]) for k in range(1, 4)
    ]
    (grad_down,) = local_kernel(
        sum_four, [shape_of(F32, *w_down.shape)], [pos, *down_plane]
    )
    (input_grad,) = local_kernel(
        input_back,
        [shape_of(BF16, rows, width)],
        [pos, own_part, core_part, far_part, tokens, d_middle, vectors],
    )
    head_parts = total_of(head_z).reshape(4, shard, columns)
    head_parts = lax.all_to_all(head_parts, "blk", 0, 0)
    grad_qkv, *ends = local_kernel(
        join_heads,
        [shape_of(F32, shard, 3 * width)]
        + [shape_of(F32, 1, shard)] * 6
        + [shape_of(F32, 1, 4 * shard)] * 2,
        [pos, head_parts],
    )
    ends = [value.reshape(-1) for value in ends]
    return (output, input_grad, grad_qkv, grad_out, grad_up, grad_down, *ends)


def layer(*arrays):
    one_document = arrays[2].shape[1] == 1
    if lax.axis_size("dp") == 8 and lax.axis_size("blk") == 4 and one_document:
        return fast_body(*arrays)
    return general_body(*arrays)


def solution(mesh):
    placed = (
        P(("dp", "blk"), None),
        P(("dp", "blk"), None),
        P("dp", None),
        P(("dp", "blk"), None),
        P(("dp", "blk"), None),
        P(("dp", "blk"), None),
        P(("dp", "blk"), None),
        P(("dp", "blk")),
        P(("dp", "blk")),
        P(("dp", "blk")),
        P(("dp", "blk")),
        P(("dp", "blk")),
        P(("dp", "blk")),
        P(("dp", "blk")),
        P(("dp", "blk")),
    )
    return jax.shard_map(
        layer,
        mesh=mesh,
        in_specs=placed,
        out_specs=(
            P(("dp", "blk"), None),
            P(("dp", "blk"), None),
            P(("dp", "blk"), None),
            P(("dp", "blk"), None),
            P(("dp", "blk"), None),
            P(("dp", "blk"), None),
            P(("dp", "blk")),
            P(("dp", "blk")),
            P(("dp", "blk")),
            P(("dp", "blk")),
            P(("dp", "blk")),
            P(("dp", "blk")),
            P(("dp", "blk")),
            P(("dp", "blk")),
        ),
        check_vma=False,
    )
```

```python
import functools
import math

import jax
import jax.numpy as jnp
from jax import lax
from jax.experimental import pallas as pl
from jax.experimental.pallas import tpu as pltpu
from jax.sharding import PartitionSpec as P

HEADS = 12


epsilon = 1e-05
masked_score = -1000000000.0


def shifted(shard, axis, by):
    devices = lax.axis_size(axis)
    pairs = [(i, i + by) for i in range(devices) if 0 <= i + by < devices]
    return lax.ppermute(shard, axis, pairs)


def shifted_2(value, axis, steps):
    count = lax.axis_size(axis)
    pairs = [(source, (source + steps) % count) for source in range(count)]
    return lax.ppermute(value, axis, pairs)


def layer_norm(values, norm_gain, norm_bias):
    centre = jnp.mean(values, -1, keepdims=True)
    centred = values - centre
    spread = jnp.mean(centred * centred, -1, keepdims=True)
    return centred * lax.rsqrt(spread + epsilon) * norm_gain + norm_bias


def ffn_norm(up_value, norm_gain, norm_bias):
    return layer_norm(jax.nn.gelu(up_value, approximate=False), norm_gain, norm_bias)


def doc_place(row_ids, doc_row, row_count, blocks):
    device = row_ids // row_count
    local = row_ids % row_count
    shares = doc_row // blocks
    ends = jnp.cumsum(shares, dtype=jnp.int32)
    starts = ends - shares
    doc = jnp.sum((local[:, None] >= ends[None, :]).astype(jnp.int32), -1, dtype=jnp.int32)
    pick = (doc[:, None] == jnp.arange(doc_row.shape[0], dtype=jnp.int32)[None, :]).astype(
        jnp.int32
    )
    share_of = jnp.sum(pick * shares[None, :], -1, dtype=jnp.int32)
    start_of = jnp.sum(pick * starts[None, :], -1, dtype=jnp.int32)
    return (doc, device * share_of + local - start_of)


def visible(query_doc, query_place, key_doc, key_place):
    return (query_doc[:, None] == key_doc[None, :]) & (key_place[None, :] <= query_place[:, None])


def outer_sum(first_operand, second_operand):
    return lax.dot_general(
        first_operand, second_operand, (((0,), (0,)), ((), ())), preferred_element_type=jnp.float32
    )


def back_product(gradient, weight):
    return lax.dot_general(
        gradient, weight, (((1,), (1,)), ((), ())), preferred_element_type=jnp.float32
    )


def score_grads(
    query_heads, dout_heads, lse_heads, delta_heads, allowed, key_heads, value_heads, score_scale
):
    scores = (
        jnp.einsum("qhd,khd->hqk", query_heads, key_heads, preferred_element_type=jnp.float32)
        * score_scale
    )
    probabilities = jnp.where(allowed[None], jnp.exp(scores - lse_heads[:, :, None]), 0.0)
    weight_grad = jnp.einsum(
        "qhd,khd->hqk", dout_heads, value_heads, preferred_element_type=jnp.float32
    )
    score_grad = (probabilities * (weight_grad - delta_heads[:, :, None])).astype(jnp.bfloat16)
    return (probabilities.astype(jnp.bfloat16), score_grad)


def general_body(
    tokens,
    cotangent,
    doc_lengths,
    w_qkv,
    w_out,
    w_up,
    w_down,
    ln1_gain,
    ln1_bias,
    ln2_gain,
    ln2_bias,
    ln3_gain,
    ln3_bias,
    ln4_gain,
    ln4_bias,
):
    gathered = (
        lax.all_gather(w_qkv, ("dp", "blk"), axis=0, tiled=True),
        lax.all_gather(w_out, ("dp", "blk"), axis=0, tiled=True),
        lax.all_gather(w_up, ("dp", "blk"), axis=0, tiled=True),
        lax.all_gather(w_down, ("dp", "blk"), axis=0, tiled=True),
        lax.all_gather(ln1_gain, ("dp", "blk"), axis=0, tiled=True),
        lax.all_gather(ln1_bias, ("dp", "blk"), axis=0, tiled=True),
        lax.all_gather(ln2_gain, ("dp", "blk"), axis=0, tiled=True),
        lax.all_gather(ln2_bias, ("dp", "blk"), axis=0, tiled=True),
        lax.all_gather(ln3_gain, ("dp", "blk"), axis=0, tiled=True),
        lax.all_gather(ln3_bias, ("dp", "blk"), axis=0, tiled=True),
        lax.all_gather(ln4_gain, ("dp", "blk"), axis=0, tiled=True),
        lax.all_gather(ln4_bias, ("dp", "blk"), axis=0, tiled=True),
    )
    qkv_full, out_full, up_full, down_full = (gathered[0], gathered[1], gathered[2], gathered[3])
    norm_params = [value.astype(jnp.float32) for value in gathered[4:]]
    gain_one, bias_one, gain_two, bias_two, gain_three, bias_three, gain_four, bias_four = (
        norm_params
    )
    row_count, model_width = tokens.shape
    head_dim = model_width // HEADS
    score_scale = head_dim ** (-0.5)
    doc_row = doc_lengths[0]
    blocks = lax.axis_size("blk")
    place_index = lax.axis_index("blk")
    query_doc, query_place = doc_place(
        place_index * row_count + jnp.arange(row_count, dtype=jnp.int32), doc_row, row_count, blocks
    )

    def key_meta(first_row, count):
        return doc_place(first_row + jnp.arange(count, dtype=jnp.int32), doc_row, row_count, blocks)

    residual_in = tokens.astype(jnp.float32)
    normed = layer_norm(residual_in, gain_one, bias_one).astype(jnp.bfloat16)
    projected = jnp.dot(normed, qkv_full, preferred_element_type=jnp.float32).astype(jnp.bfloat16)
    queries = projected[:, :model_width]
    keys_own = projected[:, model_width : 2 * model_width]
    values_own = projected[:, 2 * model_width :]
    query_heads = queries.reshape(row_count, HEADS, head_dim)
    start_state = (
        jnp.full((HEADS, row_count), masked_score, jnp.float32),
        jnp.zeros((HEADS, row_count), jnp.float32),
        jnp.zeros((HEADS, row_count, head_dim), jnp.float32),
    )
    running = start_state
    key_part = lax.all_gather(keys_own, "blk", axis=0, tiled=True)
    value_part = lax.all_gather(values_own, "blk", axis=0, tiled=True)
    part_rows = key_part.shape[0]
    step_rows = math.gcd(part_rows, 512)
    count = part_rows // step_rows

    def one_step(state, element):
        key_block, value_block, block_start = element
        key_doc, key_place = key_meta(block_start, step_rows)
        allowed = visible(query_doc, query_place, key_doc, key_place)
        scores = (
            jnp.einsum(
                "qhd,khd->hqk",
                query_heads,
                key_block.reshape(step_rows, HEADS, head_dim),
                preferred_element_type=jnp.float32,
            )
            * score_scale
        )
        scores = jnp.where(allowed[None], scores, masked_score)
        peak_old, total_old, weighted_old = state
        peak_new = jnp.maximum(peak_old, jnp.max(scores, -1))
        weights = jnp.where(allowed[None], jnp.exp(scores - peak_new[:, :, None]), 0.0)
        factor = jnp.exp(peak_old - peak_new)
        total_new = total_old * factor + jnp.sum(weights, -1)
        weighted_new = weighted_old * factor[:, :, None] + jnp.einsum(
            "hqk,khd->hqd",
            weights.astype(jnp.bfloat16),
            value_block.reshape(step_rows, HEADS, head_dim),
            preferred_element_type=jnp.float32,
        )
        return ((peak_new, total_new, weighted_new), None)

    starts = jnp.arange(count, dtype=jnp.int32) * step_rows
    running, _ = lax.scan(
        one_step,
        running,
        (
            key_part.reshape(count, step_rows, model_width),
            value_part.reshape(count, step_rows, model_width),
            starts,
        ),
    )
    peak_score, total_weight, weighted_sum = running
    log_total = peak_score + jnp.log(total_weight)
    attended = (
        (weighted_sum / total_weight[:, :, None]).transpose(1, 0, 2).reshape(row_count, model_width)
    )
    inner = layer_norm(attended, gain_two, bias_two).astype(jnp.bfloat16)
    middle = residual_in + jnp.dot(inner, out_full, preferred_element_type=jnp.float32)
    normed_two = layer_norm(middle, gain_three, bias_three).astype(jnp.bfloat16)
    up_value = jnp.dot(normed_two, up_full, preferred_element_type=jnp.float32)
    hidden = ffn_norm(up_value, gain_four, bias_four).astype(jnp.bfloat16)
    output = (middle + jnp.dot(hidden, down_full, preferred_element_type=jnp.float32)).astype(
        jnp.bfloat16
    )
    grad_down = outer_sum(hidden, cotangent)
    d_hidden = back_product(cotangent, down_full)
    _, ffn_pullback = jax.vjp(ffn_norm, up_value, gain_four, bias_four)
    d_up, grad_gain_four, grad_bias_four = ffn_pullback(d_hidden)
    d_up_low = d_up.astype(jnp.bfloat16)
    grad_up = outer_sum(normed_two, d_up_low)
    _, third_pullback = jax.vjp(layer_norm, middle, gain_three, bias_three)
    d_middle_norm, grad_gain_three, grad_bias_three = third_pullback(
        back_product(d_up_low, up_full)
    )
    d_middle = cotangent.astype(jnp.float32) + d_middle_norm
    d_middle_low = d_middle.astype(jnp.bfloat16)
    grad_out = outer_sum(inner, d_middle_low)
    _, second_pullback = jax.vjp(layer_norm, attended, gain_two, bias_two)
    d_attended, grad_gain_two, grad_bias_two = second_pullback(back_product(d_middle_low, out_full))
    d_attended_low = d_attended.astype(jnp.bfloat16)
    dout_heads = d_attended_low.reshape(row_count, HEADS, head_dim)
    delta = jnp.einsum(
        "qhd,qhd->hq",
        d_attended_low.astype(jnp.float32).reshape(row_count, HEADS, head_dim),
        attended.reshape(row_count, HEADS, head_dim),
    )

    def turn(turn_index, loop_state):
        kv_now, grads_now, query_grad = loop_state
        source = (place_index - turn_index) % blocks
        key_doc, key_place = key_meta(source * row_count, row_count)
        allowed = visible(query_doc, query_place, key_doc, key_place)
        key_heads = kv_now[0].reshape(row_count, HEADS, head_dim)
        value_heads = kv_now[1].reshape(row_count, HEADS, head_dim)
        probabilities, score_grad = score_grads(
            query_heads, dout_heads, log_total, delta, allowed, key_heads, value_heads, score_scale
        )
        query_grad = (
            query_grad
            + jnp.einsum("hqk,khd->qhd", score_grad, key_heads, preferred_element_type=jnp.float32)
            * score_scale
        )
        key_grad = (
            jnp.einsum("hqk,qhd->khd", score_grad, query_heads, preferred_element_type=jnp.float32)
            * score_scale
        )
        value_grad = jnp.einsum(
            "hqk,qhd->khd", probabilities, dout_heads, preferred_element_type=jnp.float32
        )
        grads_now = grads_now + jnp.stack(
            [key_grad.reshape(row_count, model_width), value_grad.reshape(row_count, model_width)]
        )
        kv_now = shifted(kv_now, "blk", 1)
        grads_now = shifted_2(grads_now.astype(jnp.bfloat16), "blk", 1).astype(grads_now.dtype)
        return (kv_now, grads_now, query_grad)

    loop_start = (
        jnp.stack([keys_own, values_own]),
        jnp.zeros((2, row_count, model_width), jnp.float32),
        jnp.zeros((row_count, HEADS, head_dim), jnp.float32),
    )
    _, kv_grads, query_grad = lax.fori_loop(0, blocks, turn, loop_start)
    key_grad_all = kv_grads[0]
    value_grad_all = kv_grads[1]
    d_projected = jnp.concatenate(
        [query_grad.reshape(row_count, model_width), key_grad_all, value_grad_all], axis=1
    ).astype(jnp.bfloat16)
    grad_qkv = outer_sum(normed, d_projected)
    _, first_pullback = jax.vjp(layer_norm, residual_in, gain_one, bias_one)
    d_input_norm, grad_gain_one, grad_bias_one = first_pullback(back_product(d_projected, qkv_full))
    input_grad = (d_middle + d_input_norm).astype(jnp.bfloat16)
    summed = (
        lax.psum_scatter(grad_qkv, ("dp", "blk"), scatter_dimension=0, tiled=True),
        lax.psum_scatter(grad_out, ("dp", "blk"), scatter_dimension=0, tiled=True),
        lax.psum_scatter(grad_up, ("dp", "blk"), scatter_dimension=0, tiled=True),
        lax.psum_scatter(grad_down, ("dp", "blk"), scatter_dimension=0, tiled=True),
        lax.psum_scatter(grad_gain_one, ("dp", "blk"), scatter_dimension=0, tiled=True),
        lax.psum_scatter(grad_bias_one, ("dp", "blk"), scatter_dimension=0, tiled=True),
        lax.psum_scatter(grad_gain_two, ("dp", "blk"), scatter_dimension=0, tiled=True),
        lax.psum_scatter(grad_bias_two, ("dp", "blk"), scatter_dimension=0, tiled=True),
        lax.psum_scatter(grad_gain_three, ("dp", "blk"), scatter_dimension=0, tiled=True),
        lax.psum_scatter(grad_bias_three, ("dp", "blk"), scatter_dimension=0, tiled=True),
        lax.psum_scatter(grad_gain_four, ("dp", "blk"), scatter_dimension=0, tiled=True),
        lax.psum_scatter(grad_bias_four, ("dp", "blk"), scatter_dimension=0, tiled=True),
    )
    return (output, input_grad) + tuple(summed)


F32 = jnp.float32
BF16 = jnp.bfloat16
CORE, Y_LINK, X_LINK, Z_LINK = 1, 2, 4, 8
Z_MASKS = (0, 8, 16, 24)
PLANE_MASKS = (0, Y_LINK, X_LINK, X_LINK + Y_LINK)


def swap(value, mask):
    devices = lax.axis_size("dp") * lax.axis_size("blk")
    return lax.ppermute(value, ("dp", "blk"), [(i, i ^ mask) for i in range(devices)])


def dot_rows(a, b):
    return lax.dot_general(a, b, (((1,), (0,)), ((), ())), preferred_element_type=F32)


def dot_back(a, b):
    return lax.dot_general(a, b, (((1,), (1,)), ((), ())), preferred_element_type=F32)


def dot_outer(a, b):
    return lax.dot_general(a, b, (((0,), (0,)), ((), ())), preferred_element_type=F32)


def row_stats(values):
    centre = jnp.mean(values, -1, keepdims=True)
    centred = values - centre
    spread = jnp.mean(centred * centred, -1, keepdims=True)
    scale = lax.rsqrt(spread + epsilon)
    return centred * scale, scale


def norm_back(grad_unit, unit, scale):
    first = jnp.mean(grad_unit, -1, keepdims=True)
    second = jnp.mean(grad_unit * unit, -1, keepdims=True)
    return scale * (grad_unit - first - unit * second)


def run_copies(copies):
    for copy in copies:
        copy.start()


def wait_copies(copies):
    for copy in copies:
        copy.wait()


def spread_wide(columns, width):
    quarter = width // 32
    run = 4 * quarter
    place = lax.broadcasted_iota(jnp.int32, (run, 4 * run), 1)
    row = lax.broadcasted_iota(jnp.int32, (run, 4 * run), 0)
    lines = []
    for first in (0, 4):
        pieces = []
        for m in range(8):
            piece = 0.0
            for c in range(4):
                want = (row // quarter) * run + c * quarter + row % quarter
                put = (place == want).astype(BF16)
                got = dot_outer(columns[m * run : (m + 1) * run, first : first + 8], put)
                piece = piece + got[c : c + 1]
            pieces.append(piece)
        lines.append(jnp.concatenate(pieces, axis=1))
    return jnp.concatenate(lines, axis=0)


def fold_heads(value):
    rows = value.shape[0] // 2
    last = jnp.concatenate([value[:rows, 128:], value[rows:, 128:]], axis=1)
    return jnp.concatenate([value[:, :128], last], axis=0)


def unfold_heads(value):
    rows = value.shape[0] // 3
    last = value[2 * rows :]
    last = jnp.concatenate([last[:, :64], last[:, 64:]], axis=0)
    return jnp.concatenate([value[: 2 * rows], last], axis=1)


def attention_forward(
    pos, t0, t1, t2, t3, own, other, normed, units, proj, weight, vectors, wide, att, mixed_out, stats
):
    rows, width = t0.shape
    slot_rows = own.shape[1]
    head_dim = width // HEADS
    span = mixed_out.shape[1]
    heads = span // head_dim
    blk = pos[1]
    for x, source in enumerate((own, other)):
        for z in range(4):
            slot = 2 * z + (pos[0] % 2 ^ x)
            at = pl.ds(pl.multiple_of(slot * slot_rows, slot_rows), slot_rows)
            weight[at, :] = source[z]
    tail = (3 * span // 128) * 128
    first = 3 * span - tail
    turned = jnp.transpose(weight[:, tail:].astype(F32))
    vectors[...] = turned[first : first + 8, :]
    wide[...] = spread_wide(weight[:, tail + first + 6 : tail + first + 22], width)
    gain, bias = vectors[0:1, :], vectors[1:2, :]
    for k, source in enumerate((t0, t1, t2, t3)):
        unit, _ = row_stats(source[...].astype(F32))
        at = pl.ds(pl.multiple_of((blk ^ k) * rows, rows), rows)
        value = (unit * gain + bias).astype(BF16)
        normed[at, :] = value
        units[at, :] = unit.astype(BF16)
        proj[at, :] = dot_rows(value, weight[...]).astype(BF16)
    scale = head_dim ** (-0.5)
    below = lax.broadcasted_iota(jnp.int32, (rows, rows), 1) <= lax.broadcasted_iota(
        jnp.int32, (rows, rows), 0
    )
    lane = lax.broadcasted_iota(jnp.int32, (rows, 128), 1)
    for block in range(4):
        mixed = []
        low, high = block * rows, (block + 1) * rows
        stat = jnp.zeros((rows, 128), F32)
        for head in range(heads):
            q = proj[low:high, head * head_dim : (head + 1) * head_dim] * BF16(scale)
            k = proj[:high, span + head * head_dim : span + (head + 1) * head_dim]
            v = proj[:high, 2 * span + head * head_dim : 2 * span + (head + 1) * head_dim]
            own = jnp.where(below, dot_back(q, k[low:]), masked_score)
            peak = jnp.max(own, -1, keepdims=True)
            if block:
                past = dot_back(q, k[:low])
                peak = jnp.maximum(peak, jnp.max(past, -1, keepdims=True))
            own = jnp.exp(own - peak)
            total = jnp.sum(own, -1, keepdims=True)
            mix = dot_rows(own.astype(BF16), v[low:])
            if block:
                past = jnp.exp(past - peak)
                total = total + jnp.sum(past, -1, keepdims=True)
                mix = mix + dot_rows(past.astype(BF16), v[:low])
            mixed.append(mix / total)
            stat = jnp.where(lane == head, peak + jnp.log(total), stat)
        stats[low:high, :] = stat
        value = jnp.concatenate(mixed, axis=1)
        mixed_out[low:high, :] = value
        att[block] = fold_heads(value.astype(BF16))


def ffn_forward(
    pos, att, tokens, vectors, wide_gains, weights,
    hidden, acts, middle, unit_four, slope, scale_four,
    w_out, w_up, up, sems,
):
    rows, width = tokens.shape
    copies = [
        pltpu.make_async_copy(weights.at[:, pl.ds(0, width)], w_out, sems.at[0]),
        pltpu.make_async_copy(weights.at[:, pl.ds(width, w_up.shape[1])], w_up, sems.at[1]),
    ]
    run_copies(copies)
    attended = jnp.concatenate([unfold_heads(att[j]) for j in range(4)], axis=1).astype(F32)
    unit, _ = row_stats(attended)
    inner_low = (unit * vectors[2:3, :] + vectors[3:4, :]).astype(BF16)
    acts[:, width:] = inner_low
    copies[0].wait()
    mid = tokens[...].astype(F32) + dot_rows(inner_low, w_out[...])
    middle[...] = mid
    unit, _ = row_stats(mid)
    low = (unit * vectors[4:5, :] + vectors[5:6, :]).astype(BF16)
    acts[:, :width] = low
    copies[1].wait()
    up[...] = dot_rows(low, w_up[...])
    step = 64
    gain, bias = wide_gains[0:1, :], wide_gains[1:2, :]

    def chunk(i, carry):
        at = pl.ds(pl.multiple_of(i * step, step), step)
        value = up[at, :]
        gate = 0.5 * (1.0 + lax.erf(value * (2.0**-0.5)))
        slope[at, :] = (gate + value * jnp.exp(-0.5 * value * value) * (0.5 / math.pi) ** 0.5).astype(
            BF16
        )
        unit, scale = row_stats(value * gate)
        unit_four[at, :] = unit.astype(BF16)
        hidden[at, :] = (unit * gain + bias).astype(BF16)
        scale_four[at, :] = jnp.broadcast_to(scale, (step, 128))
        return carry

    lax.fori_loop(0, rows // step, chunk, 0, unroll=True)


def down_copies(pos, stacks, target, sems):
    rows = stacks[0].shape[1]
    plane = 2 * (pos[0] % 2) + pos[1] // 2
    copies = []
    for other in range(2):
        for mask in range(4):
            for z in range(4):
                slot = 2 * (4 * z + (plane ^ mask)) + (pos[1] % 2 ^ other)
                copies.append(
                    pltpu.make_async_copy(
                        stacks[other * 4 + mask].at[z],
                        target.at[pl.ds(pl.multiple_of(slot * rows, rows), rows)],
                        sems.at[len(copies)],
                    )
                )
    return copies


def fold(value):
    total = value[:, :128]
    for start in range(128, value.shape[1], 128):
        total = total + value[:, start : start + 128]
    return total


def ffn_backward(
    pos, att, cot, vectors, wide_gains, middle, hidden_far, unit_four, slope, scale_four, weights,
    s0, s1, s2, s3, s4, s5, s6, s7,
    output, grads, d_middle, d0, d1, d2, d3, vector_grads, wide_grads,
    w_down, w_out, w_up, hidden, units, slopes, d_hidden, sems,
):
    rows, width = cot.shape
    wide = w_up.shape[1]
    copies = down_copies(pos, (s0, s1, s2, s3, s4, s5, s6, s7), w_down, sems)
    later = []
    for source, target in (
        (unit_four, units),
        (hidden_far, hidden),
        (slope, slopes),
        (weights.at[:, pl.ds(width, wide)], w_up),
        (weights.at[:, pl.ds(0, width)], w_out),
    ):
        later.append(pltpu.make_async_copy(source, target, sems.at[len(copies) + len(later)]))
    by_z = [copies[q::4] for q in range(4)]
    run_copies(by_z[0] + later[:1] + by_z[1] + later[1:2] + by_z[2] + by_z[3] + later[2:])

    def first_grad(q):
        wait_copies(by_z[q] + later[: 2 if q == 0 else 0])
        return dot_back(cot[...], w_down[q * width : (q + 1) * width, :])

    def fold_rows(value):
        total = value[:8]
        for start in range(8, rows, 8):
            total = total + value[start : start + 8]
        return jnp.sum(total, 0, keepdims=True)

    current = first_grad(0)
    first = jnp.zeros((rows, 128), F32)
    second = jnp.zeros((rows, 128), F32)
    out = middle[...]
    for q in range(4):
        at = slice(q * width, (q + 1) * width)
        if q < 3:
            following = first_grad(q + 1)
        out = out + dot_rows(hidden[:, at], w_down[at, :])
        d_hidden[:, at] = current
        unit = units[:, at].astype(F32)
        part = current * unit
        wide_grads[0:1, at] = fold_rows(part)
        wide_grads[1:2, at] = fold_rows(current)
        gain = wide_gains[0:1, at]
        first = first + fold(current * gain)
        second = second + fold(part * gain)
        current = following
    output[...] = out.astype(BF16)
    first = jnp.sum(first, -1, keepdims=True) * (1.0 / wide)
    second = jnp.sum(second, -1, keepdims=True) * (1.0 / wide)
    scale = scale_four[:, 0:1]
    wait_copies(later[2:])

    def second_grad(q):
        at = slice(q * width, (q + 1) * width)
        grad = d_hidden[:, at] * wide_gains[0:1, at] - first - units[:, at].astype(F32) * second
        grad = (scale * grad * slopes[:, at].astype(F32)).astype(BF16)
        grads[:, at] = grad
        return grad

    d_normed = 0.0
    for q in range(4):
        d_normed = d_normed + dot_back(second_grad(q), w_up[:, q * width : (q + 1) * width])
    unit, scale = row_stats(middle[...])
    gain_three = jnp.sum(d_normed * unit, 0, keepdims=True)
    bias_three = jnp.sum(d_normed, 0, keepdims=True)
    d_mid = cot[...].astype(F32) + norm_back(d_normed * vectors[4:5, :], unit, scale)
    d_middle[...] = d_mid
    d_mid_low = d_mid.astype(BF16)
    grads[:, wide:] = d_mid_low
    d_inner = dot_back(d_mid_low, w_out[...])
    attended = jnp.concatenate([unfold_heads(att[j]) for j in range(4)], axis=1).astype(F32)
    unit, scale = row_stats(attended)
    gain_two = jnp.sum(d_inner * unit, 0, keepdims=True)
    bias_two = jnp.sum(d_inner, 0, keepdims=True)
    vector_grads[...] = jnp.concatenate(
        [gain_two, bias_two, gain_three, bias_three, jnp.zeros((4, width), F32)], axis=0
    )
    back = norm_back(d_inner * vectors[2:3, :], unit, scale).astype(BF16)
    span = width // 4
    parts = [back[:, j * span : (j + 1) * span] for j in range(4)]
    for k, target in enumerate((d0, d1, d2, d3)):
        value = parts[k]
        for j in range(4):
            if j != k:
                value = jnp.where((pos[1] ^ k) == j, parts[j], value)
        target[...] = fold_heads(value)


def piece_copies(pos, held, targets, sems, zs):
    chip = pos[0] * 2 + pos[1] // 2
    copies = []
    for start, masks, target in targets:
        for i, plane in enumerate(masks):
            for z in zs:
                slot = ((chip ^ plane) & 3) + 4 * z
                copies.append(
                    pltpu.make_async_copy(
                        held.at[slot, :, pl.ds(start, target.shape[3])],
                        target.at[i, z],
                        sems.at[len(copies)],
                    )
                )
    return copies


def down_grads(pos, hidden, cot, mine_far, theirs_far, mine, theirs, sems):
    rows = mine.shape[2]
    plane = 2 * (pos[0] % 2) + pos[1] // 2
    first = pos[1] % 2 == 0
    copies = []
    for pair in range(hidden.shape[1] // (4 * rows)):
        value = dot_outer(hidden[:, 4 * rows * pair : 4 * rows * (pair + 1)], cot[...]).astype(BF16)
        for i in range(2):
            chip = 2 * pair + i
            low, high = value[2 * i * rows : (2 * i + 1) * rows], value[(2 * i + 1) * rows : (2 * i + 2) * rows]
            mine[chip // 4, (chip % 4) ^ plane] = jnp.where(first, low, high)
            theirs[chip // 4, (chip % 4) ^ plane] = jnp.where(first, high, low)
        if pair % 2:
            z = pair // 2
            for k, (source, target) in enumerate(((mine, mine_far), (theirs, theirs_far))):
                copies.append(pltpu.make_async_copy(source.at[z], target.at[z], sems.at[k, z]))
                copies[-1].start()
    wait_copies(copies)


def up_grads(
    pos, acts, acts_other, g0, g1, down_mine, down_got,
    keep_a, send_a, keep_b, send_b, down_grad,
    held, left, right, chosen, down, out_sems, sems,
):
    rows = held.shape[1]
    core = pos[1] % 2
    width = acts.shape[1] // 2
    wide = 4 * width
    copies = []

    def load(source, target):
        copies.append(pltpu.make_async_copy(source, target, sems.at[len(copies)]))
        copies[-1].start()

    for i, source in enumerate((acts, acts_other)):
        load(source, left.at[i])
    for i, source in enumerate((g0, g1)):
        load(source, right.at[i])
    for i, source in enumerate((down_mine, down_got)):
        load(source, down.at[i])
    row = lax.broadcasted_iota(jnp.int32, (width, width // 2), 0)
    column = lax.broadcasted_iota(jnp.int32, (width, width // 2), 1)
    take = (row // rows == 2 * (column // rows) + core) & (row % rows == column % rows)
    take = take.astype(BF16)
    wait_copies(copies[:2])
    for i in range(2):
        for part in range(2):
            at = slice(part * width // 2, (part + 1) * width // 2)
            chosen[i, :, at] = dot_rows(
                left[i, :, part * width : (part + 1) * width], take
            ).astype(BF16)
    cut = keep_a.shape[3]
    pieces = ((0, (0, 1), keep_a), (0, (2, 3), send_a), (cut, (0, 2), keep_b), (cut, (1, 3), send_b))
    tile = 384
    wait_copies(copies[2:4])
    outs = []
    for c in range(0, wide + width, tile):
        from_up = c >= width
        source = c - width if from_up else wide + c
        first = 0 if from_up else width // 2
        value = 0.0
        for i in range(2):
            value = value + dot_outer(
                chosen[i, :, first : first + width // 2], right[i, :, source : source + tile]
            )
        for chip in range(16):
            held[chip, :, c : c + tile] = value[chip * rows : (chip + 1) * rows].astype(BF16)
        if c + tile == cut or c + tile == wide + width:
            part = len(outs)
            outs.append(
                piece_copies(pos, held, pieces[2 * part : 2 * part + 2], out_sems.at[part], range(4))
            )
            run_copies(outs[-1])
    wait_copies(copies[4:])
    for z in range(down.shape[1]):
        down[0, z] = down[0, z] + down[1, z]
    outs.append([pltpu.make_async_copy(down.at[0], down_grad, sems.at[0])])
    run_copies(outs[-1])
    for group in outs:
        wait_copies(group)


def gather_wide(grads, width):
    quarter = width // 32
    run = 4 * quarter
    place = lax.broadcasted_iota(jnp.int32, (run, 4 * run), 1)
    row = lax.broadcasted_iota(jnp.int32, (run, 4 * run), 0)
    lane = lax.broadcasted_iota(jnp.int32, (run, 128), 1)
    rows = jnp.concatenate([grads, jnp.zeros((126, grads.shape[1]), F32)], axis=0).astype(BF16)
    pieces = []
    for m in range(8):
        piece = jnp.zeros((run, 128), F32)
        for c in range(4):
            want = (row // quarter) * run + c * quarter + row % quarter
            put = (place == want).astype(BF16)
            got = dot_back(put, rows[:, m * 4 * run : (m + 1) * 4 * run])
            for v in range(2):
                piece = piece + jnp.where(lane == 6 + 4 * v + c, got[:, v : v + 1], 0.0)
        pieces.append(piece)
    return jnp.concatenate(pieces, axis=0)


def attention_backward(
    pos, d0, d1, d2, d3, normed_far, units_far, proj, weight_far, mixed, stats, vector_grads,
    wide_grads,
    own, own_far, other, p0, p1,
    d_out, d_proj, tt, held, d_normed, normed, units, weight, load_sems, sems,
):
    rows, width = d0.shape[0] * 2 // 3, normed.shape[1]
    loads = [
        pltpu.make_async_copy(source, target, load_sems.at[i])
        for i, (source, target) in enumerate(
            ((weight_far, weight), (units_far, units), (normed_far, normed))
        )
    ]
    run_copies(loads)
    head_dim = width // HEADS
    span = d_out.shape[1]
    heads = span // head_dim
    dp, blk = pos[0], pos[1]
    for k, source in enumerate((d0, d1, d2, d3)):
        d_out[pl.ds(pl.multiple_of((blk ^ k) * rows, rows), rows), :] = unfold_heads(source[...])
    scale = head_dim ** (-0.5)
    below = lax.broadcasted_iota(jnp.int32, (rows, rows), 1) <= lax.broadcasted_iota(
        jnp.int32, (rows, rows), 0
    )
    for head in range(heads):
        at_q = slice(head * head_dim, (head + 1) * head_dim)
        at_k = slice(span + head * head_dim, span + (head + 1) * head_dim)
        at_v = slice(2 * span + head * head_dim, 2 * span + (head + 1) * head_dim)
        tt[...] = jnp.zeros_like(tt)
        for block in range(4):
            low, high = block * rows, (block + 1) * rows
            q = proj[low:high, at_q] * BF16(scale)
            d = d_out[low:high, at_q]
            log_total = stats[low:high, head : head + 1]
            delta = jnp.sum(d.astype(F32) * mixed[low:high, at_q], -1, keepdims=True)
            d_query = 0.0
            for start, end in [(low, high)] + ([(0, low)] if block else []):
                score = dot_back(q, proj[start:end, at_k])
                if start == low:
                    score = jnp.where(below, score, masked_score)
                score = jnp.exp(score - log_total)
                grad = dot_back(d, proj[start:end, at_v])
                d_score = (score * (grad - delta)).astype(BF16)
                d_query = d_query + dot_rows(d_score, proj[start:end, at_k])
                tt[0, :, start:end] += dot_outer(q, d_score)
                tt[1, :, start:end] += dot_outer(d, score.astype(BF16))
            d_proj[low:high, at_q] = (d_query * scale).astype(BF16)
        d_proj[:, at_k] = jnp.transpose(tt[0]).astype(BF16)
        d_proj[:, at_v] = jnp.transpose(tt[1]).astype(BF16)
    columns = weight.shape[1]
    vector_sums = []
    wait_copies(loads[:2])
    for j in range(4):
        at = slice(j * rows, (j + 1) * rows)
        grad = dot_back(d_proj[at, :], weight[:, : 3 * span])
        unit = units[at, :].astype(F32)
        vector_sums.append((jnp.sum(grad * unit, 0, keepdims=True), jnp.sum(grad, 0, keepdims=True)))
        d_normed[j ^ blk] = grad.astype(BF16)
    copies = [
        pltpu.make_async_copy(d_normed.at[k], target, sems.at[8 + k])
        for k, target in enumerate((own, other.at[0], own_far, other.at[1]))
    ]
    run_copies(copies)
    loads[2].wait()
    sums = [sum(v[i] for v in vector_sums) for i in range(2)]
    turned = jnp.transpose(
        jnp.concatenate(
            sums + [vector_grads[0:4, :], jnp.zeros((128 - 6, width), F32)], axis=0
        )
    ) + gather_wide(wide_grads[...], width)
    slot_rows = held.shape[1]
    for r in range(0, width, 2 * slot_rows):
        value = dot_outer(normed[:, r : r + 2 * slot_rows], d_proj[...])
        value = jnp.concatenate(
            [value, turned[r : r + 2 * slot_rows, : columns - 3 * span]], axis=1
        ).astype(BF16)
        held[r // slot_rows] = value[:slot_rows]
        held[r // slot_rows + 1] = value[slot_rows:]
    pieces = []
    for x, target in enumerate((p0, p1)):
        for z in range(4):
            slot = ((dp ^ x) & 1) + 2 * z
            pieces.append(pltpu.make_async_copy(held.at[slot], target.at[z], sems.at[x * 4 + z]))
    run_copies(pieces)
    wait_copies(copies + pieces)


def local_kernel(kernel, outs, ins, scratch=(), us=2, in_any=(), out_any=(), after=(), passed=(), mib=16):
    here = pl.BlockSpec(memory_space=pltpu.VMEM)
    far = pl.BlockSpec(memory_space=pl.ANY)
    specs = [pl.BlockSpec(memory_space=pltpu.SMEM)]
    specs += [far if i in in_any else here for i in range(1, len(ins))]
    specs += [far] * (len(after) + len(passed))
    unread = len(ins) + len(after) + len(passed)
    ends = unread + len(outs)

    def run(*refs):
        kernel(*refs[: len(ins)], *refs[unread:ends], *refs[ends + len(passed) :])

    return pl.pallas_call(
        run,
        out_shape=[*outs, *(shape_of(v.dtype, *v.shape) for v in passed)],
        in_specs=specs,
        out_specs=[far if i in out_any else here for i in range(len(outs))] + [far] * len(passed),
        input_output_aliases={
            len(ins) + len(after) + i: len(outs) + i for i in range(len(passed))
        },
        scratch_shapes=list(scratch),
        compiler_params=pltpu.CompilerParams(vmem_limit_bytes=mib * 1024 * 1024),
        cost_estimate=pl.CostEstimate(
            flops=int(us * 1.15e9) // 100, bytes_accessed=int(us * 3.6e6) // 100, transcendentals=0
        ),
    )(*ins, *after, *passed)


def shape_of(dtype, *shape):
    return jax.ShapeDtypeStruct(shape, dtype)


def z_exchange(own):
    return [own] + [swap(own, mask) for mask in Z_MASKS[1:]]


def pack_weights(
    pos, w_qkv, w_out, w_up, gains, wide_gains, packed, slices
):
    rows, width = w_out.shape
    span = width // 4
    packed[:, :width] = w_out[...]
    packed[:, width:] = w_up[...]
    wide = wide_gains[...].astype(F32)
    lines = [gains[...].astype(F32)] + [
        wide[i : i + 1, c * rows : (c + 1) * rows] for i in range(2) for c in range(4)
    ]
    square = jnp.concatenate(lines + [jnp.zeros((128 - 14, rows), F32)], axis=0)
    square = jnp.concatenate([square, jnp.zeros((128, 128 - rows), F32)], axis=1)
    ends = jnp.transpose(square)[:rows, : slices.shape[2] - 3 * span].astype(BF16)
    for j in range(4):
        parts = [w_qkv[:, p * width + j * span : p * width + (j + 1) * span] for p in range(3)]
        slices[j] = jnp.concatenate(parts + [ends], axis=1)

def stack_z(pos, b0, b1, b2, b3, target):
    for k, part in enumerate((b0, b1, b2, b3)):
        target[(pos[0] // 2) ^ k] = part[...]


def nothing(pos):
    pass


def sum_first(pos, keep_a, got_a, keep_b, got_b, own_a, send_a, own_b, send_b):
    for keep, got, own, send in ((keep_a, got_a, own_a, send_a), (keep_b, got_b, own_b, send_b)):
        own[...] = keep[0].astype(F32) + got[0].astype(F32)
        send[...] = (keep[1].astype(F32) + got[1].astype(F32)).astype(BF16)


def sum_second(pos, own_a, got_a, own_b, got_b, total):
    cut = own_a.shape[2]
    total[:, :, :cut] = (own_a[...] + got_a[...].astype(F32)).astype(BF16)
    total[:, :, cut:] = (own_b[...] + got_b[...].astype(F32)).astype(BF16)


def sum_two(pos, p0, p1, z0, z1, z2, z3):
    for k, target in enumerate((z0, z1, z2, z3)):
        at = (pos[0] // 2) ^ k
        target[...] = (p0[at].astype(F32) + p1[at].astype(F32)).astype(target.dtype)


def join_heads(pos, parts, grad, e0, e1, e2, e3, e4, e5, e6, e7):
    width = grad.shape[1] // 3
    span = width // 4
    rows = grad.shape[0]
    for j in range(4):
        for p in range(3):
            grad[:, p * width + j * span : p * width + (j + 1) * span] = parts[
                j, :, p * span : (p + 1) * span
            ]
    tail = (3 * span // 128) * 128
    last = (parts[0] + parts[1]) + (parts[2] + parts[3])
    square = jnp.concatenate([last[:, tail:], jnp.zeros((128 - rows, 128), F32)], axis=0)
    ends = jnp.transpose(square)[3 * span - tail : 3 * span - tail + 16]
    for i, target in enumerate((e0, e1, e2, e3, e4, e5)):
        target[...] = ends[i : i + 1, :rows]
    for i, target in enumerate((e6, e7)):
        first = 6 + 4 * i
        target[...] = jnp.concatenate(
            [ends[first + c : first + c + 1, :rows] for c in range(4)], axis=1
        )


def far_pair(pos, own, core_part, target):
    target[...] = (own[...].astype(F32) + core_part[1].astype(F32)).astype(BF16)


def sum_four(pos, p0, p1, p2, p3, total):
    total[...] = (p0[...].astype(F32) + p1[...].astype(F32)) + (
        p2[...].astype(F32) + p3[...].astype(F32)
    )


def input_back(pos, own, core_part, far, tokens, d_middle, vectors, input_grad):
    grad = own[...].astype(F32) + core_part[0].astype(F32) + far[...].astype(F32)
    unit, scale = row_stats(tokens[...].astype(F32))
    input_grad[...] = (d_middle[...] + norm_back(grad * vectors[0:1, :], unit, scale)).astype(BF16)


def groups_of(fixed):
    numbers = range(lax.axis_size("dp") * lax.axis_size("blk"))
    return [[i for i in numbers if i & fixed == j] for j in numbers if j & fixed == j]


def fast_body(
    tokens, cotangent, doc_lengths, w_qkv, w_out, w_up, w_down,
    ln1_gain, ln1_bias, ln2_gain, ln2_bias, ln3_gain, ln3_bias, ln4_gain, ln4_bias,
):
    rows, width = tokens.shape
    shard = w_qkv.shape[0]
    ff = w_up.shape[1]
    head_dim = width // HEADS
    span = width // 4
    group = rows * 4
    columns = -(-(3 * span + 16) // 128) * 128
    slot_rows = 4 * shard
    both = ("dp", "blk")
    along_z = groups_of(CORE + Y_LINK + X_LINK)
    in_plane = groups_of(CORE + 3 * Z_LINK)
    dp, blk = lax.axis_index("dp"), lax.axis_index("blk")
    pos = jnp.stack([dp, blk]).astype(jnp.int32)

    def gather(value, groups):
        return lax.all_gather(value, both, axis=0, axis_index_groups=groups)

    def scatter(value, groups):
        return lax.psum_scatter(
            value, both, scatter_dimension=0, axis_index_groups=groups, tiled=False
        )

    norms = [ln1_gain, ln1_bias, ln2_gain, ln2_bias, ln3_gain, ln3_bias]
    gains = jnp.stack(norms)
    wide_gains = jnp.stack([ln4_gain, ln4_bias])
    packed, slices = local_kernel(
        pack_weights,
        [shape_of(BF16, shard, width + ff), shape_of(BF16, 4, shard, columns)],
        [pos, w_qkv, w_out, w_up, gains, wide_gains],
    )
    weights = lax.all_gather(packed, both, axis=0, tiled=True)

    token_y = swap(tokens, Y_LINK)

    slices = lax.all_to_all(slices, "blk", 0, 0).reshape(slot_rows, columns)
    down_own, slices = local_kernel(
        stack_z,
        [shape_of(BF16, 4, *w_down.shape)],
        [pos, w_down] + [swap(w_down, mask) for mask in Z_MASKS[1:]],
        after=(token_y,),
        passed=(slices,),
    )
    slices, down_own, down_x = local_kernel(
        stack_z,
        [shape_of(BF16, 4, slot_rows, columns)],
        [pos, slices] + [swap(slices, mask) for mask in Z_MASKS[1:]],
        passed=(down_own, swap(down_own, X_LINK)),
    )
    down_parts = [down_own, swap(down_own, Y_LINK), down_x, swap(down_x, Y_LINK)]
    token_core, token_both = swap(tokens, CORE), swap(token_y, CORE)
    slices_x = swap(slices, X_LINK)

    tokens_group = [tokens, token_core, token_y, token_both]
    packed_rows = rows * 3 // 2
    normed, units, proj, weight, vectors, wide, att, mixed, stats = local_kernel(
        attention_forward,
        [
            shape_of(BF16, group, width),
            shape_of(BF16, group, width),
            shape_of(BF16, group, columns),
            shape_of(BF16, width, columns),
            shape_of(F32, 8, width),
            shape_of(F32, 2, ff),
            shape_of(BF16, 4, packed_rows, 128),
            shape_of(F32, group, span),
            shape_of(F32, group, 128),
        ],
        [pos, *tokens_group, slices, slices_x],
        us=11,
        mib=56,
    )
    att = lax.all_to_all(att, "blk", 0, 0)
    down_parts = list(
        local_kernel(nothing, [], [pos], mib=56, after=(att,), passed=down_parts)
    )
    down_all = down_parts + [swap(value, CORE) for value in down_parts]
    hidden, acts, middle, unit_four, slope, scale_four = local_kernel(
        ffn_forward,
        [
            shape_of(BF16, rows, ff),
            shape_of(BF16, rows, 2 * width),
            shape_of(F32, rows, width),
            shape_of(BF16, rows, ff),
            shape_of(BF16, rows, ff),
            shape_of(F32, rows, 128),
        ],
        [pos, att, tokens, vectors, wide, weights],
        [
            pltpu.VMEM((width, width), BF16),
            pltpu.VMEM((width, ff), BF16),
            pltpu.VMEM((rows, ff), F32),
            pltpu.SemaphoreType.DMA((2,)),
        ],
        in_any=(5,),
        us=12,
        mib=56,
    )
    down_mine, down_theirs = local_kernel(
        down_grads,
        [shape_of(BF16, 4, 4, *w_down.shape)] * 2,
        [pos, hidden, cotangent],
        [pltpu.VMEM((4, 4, *w_down.shape), BF16)] * 2 + [pltpu.SemaphoreType.DMA((2, 4))],
        out_any=(0, 1),
        us=5,
        mib=56,
    )
    acts_other = swap(acts, CORE)
    output, grads, d_middle, d0, d1, d2, d3, vector_grads, wide_grads, down_theirs = local_kernel(
        ffn_backward,
        [
            shape_of(BF16, rows, width),
            shape_of(BF16, rows, ff + width),
            shape_of(F32, rows, width),
            *[shape_of(BF16, packed_rows, 128)] * 4,
            shape_of(F32, 8, width),
            shape_of(F32, 2, ff),
        ],
        [
            pos, att, cotangent, vectors, wide, middle, hidden, unit_four, slope, scale_four,
            weights, *down_all,
        ],
        [
            pltpu.VMEM((ff, width), BF16),
            pltpu.VMEM((width, width), BF16),
            pltpu.VMEM((width, ff), BF16),
            pltpu.VMEM((rows, ff), BF16),
            pltpu.VMEM((rows, ff), BF16),
            pltpu.VMEM((rows, ff), BF16),
            pltpu.VMEM((rows, ff), F32),
            pltpu.SemaphoreType.DMA((37,)),
        ],
        in_any=(6, 7, 8, *range(10, 19)),
        us=15,
        after=(down_mine, acts_other),
        passed=(down_theirs,),
        mib=56,
    )
    d_att = [d0] + [swap(value, k) for k, value in ((1, d1), (2, d2), (3, d3))]
    grads_other, down_got = swap(grads, CORE), swap(down_theirs, CORE)
    a_columns = -(-(width + ff) // (2 * 384)) * 384
    piece_a = (4, shard, a_columns)
    piece_b = (4, shard, width + ff - a_columns)
    keep_a, send_a, keep_b, send_b, down_grad = local_kernel(
        up_grads,
        [shape_of(BF16, 2, *piece_a)] * 2
        + [shape_of(BF16, 2, *piece_b)] * 2
        + [shape_of(BF16, *down_mine.shape)],
        [pos, acts, acts_other, grads, grads_other, down_mine, down_got],
        [
            pltpu.VMEM((16, shard, width + ff), BF16),
            pltpu.VMEM((2, rows, 2 * width), BF16),
            pltpu.VMEM((2, rows, width + ff), BF16),
            pltpu.VMEM((2, rows, width), BF16),
            pltpu.VMEM((2, *down_mine.shape), BF16),
            pltpu.SemaphoreType.DMA((2, 16)),
            pltpu.SemaphoreType.DMA((6,)),
        ],
        in_any=range(1, 7),
        out_any=range(5),
        after=d_att[1:],
        mib=56,
    )
    down_first = scatter(down_grad, along_z)
    got_a, got_b = swap(send_a, X_LINK), swap(send_b, Y_LINK)

    def total_of(pieces):
        return sum(piece.astype(F32) for piece in pieces)

    own_part, own_far, other_part, p0, p1 = local_kernel(
        attention_backward,
        [shape_of(BF16, rows, width)] * 2
        + [shape_of(BF16, 2, rows, width)]
        + [shape_of(BF16, 4, slot_rows, columns)] * 2,
        [
            pos, *d_att, normed, units, proj, weight, mixed, stats, vector_grads, wide_grads
        ],
        [
            pltpu.VMEM((group, span), BF16),
            pltpu.VMEM((group, 3 * span), BF16),
            pltpu.VMEM((2, head_dim, group), F32),
            pltpu.VMEM((8, slot_rows, columns), BF16),
            pltpu.VMEM((4, rows, width), BF16),
            pltpu.VMEM((group, width), BF16),
            pltpu.VMEM((group, width), BF16),
            pltpu.VMEM((width, columns), BF16),
            pltpu.SemaphoreType.DMA((3,)),
            pltpu.SemaphoreType.DMA((12,)),
        ],
        in_any=(5, 6, 8),
        out_any=range(5),
        after=(keep_a,),
        us=20,
        mib=56,
    )
    own_a, send_a, own_b, send_b = local_kernel(
        sum_first,
        [
            shape_of(F32, *piece_a),
            shape_of(BF16, *piece_a),
            shape_of(F32, *piece_b),
            shape_of(BF16, *piece_b),
        ],
        [pos, keep_a, got_a, keep_b, got_b],
        after=(own_part,),
    )
    (other_part,) = local_kernel(
        nothing, [], [pos], after=(send_a,), passed=(other_part,), mib=56
    )
    got_a, got_b = swap(send_a, Y_LINK), swap(send_b, X_LINK)
    core_part = swap(other_part, CORE)
    (pair_far,) = local_kernel(
        far_pair,
        [shape_of(BF16, rows, width)],
        [pos, own_far, core_part],
    )
    far_part = swap(pair_far, Y_LINK)
    up_total, p1 = local_kernel(
        sum_second,
        [shape_of(BF16, 4, shard, width + ff)],
        [pos, own_a, got_a, own_b, got_b],
        after=(pair_far,),
        passed=(p1,),
    )
    up_sum = scatter(up_total, along_z).astype(F32)
    grad_out, grad_up = up_sum[:, :width], up_sum[:, width:]
    *head_z, down_first = local_kernel(
        sum_two,
        [shape_of(F32 if z == 0 else BF16, slot_rows, columns) for z in range(4)],
        [pos, p0, swap(p1, X_LINK)],
        passed=(down_first,),
    )
    (input_grad,) = local_kernel(
        input_back,
        [shape_of(BF16, rows, width)],
        [pos, own_part, core_part, far_part, tokens, d_middle, vectors],
        after=(head_z[0],),
    )
    head_z = [head_z[0]] + [swap(head_z[z], Z_MASKS[z]) for z in range(1, 4)]
    down_plane = [down_first[0]] + [
        swap(down_first[k], PLANE_MASKS[k]) for k in range(1, 4)
    ]
    (grad_down,) = local_kernel(
        sum_four, [shape_of(F32, *w_down.shape)], [pos, *down_plane]
    )
    head_parts = total_of(head_z).reshape(4, shard, columns)
    head_parts = lax.all_to_all(head_parts, "blk", 0, 0)
    grad_qkv, *ends = local_kernel(
        join_heads,
        [shape_of(F32, shard, 3 * width)]
        + [shape_of(F32, 1, shard)] * 6
        + [shape_of(F32, 1, 4 * shard)] * 2,
        [pos, head_parts],
    )
    ends = [value.reshape(-1) for value in ends]
    return (output, input_grad, grad_qkv, grad_out, grad_up, grad_down, *ends)


def layer(*arrays):
    one_document = arrays[2].shape[1] == 1
    if lax.axis_size("dp") == 8 and lax.axis_size("blk") == 4 and one_document:
        return fast_body(*arrays)
    return general_body(*arrays)


def solution(mesh):
    placed = (
        P(("dp", "blk"), None),
        P(("dp", "blk"), None),
        P("dp", None),
        P(("dp", "blk"), None),
        P(("dp", "blk"), None),
        P(("dp", "blk"), None),
        P(("dp", "blk"), None),
        P(("dp", "blk")),
        P(("dp", "blk")),
        P(("dp", "blk")),
        P(("dp", "blk")),
        P(("dp", "blk")),
        P(("dp", "blk")),
        P(("dp", "blk")),
        P(("dp", "blk")),
    )
    return jax.shard_map(
        layer,
        mesh=mesh,
        in_specs=placed,
        out_specs=(
            P(("dp", "blk"), None),
            P(("dp", "blk"), None),
            P(("dp", "blk"), None),
            P(("dp", "blk"), None),
            P(("dp", "blk"), None),
            P(("dp", "blk"), None),
            P(("dp", "blk")),
            P(("dp", "blk")),
            P(("dp", "blk")),
            P(("dp", "blk")),
            P(("dp", "blk")),
            P(("dp", "blk")),
            P(("dp", "blk")),
            P(("dp", "blk")),
        ),
        check_vma=False,
    )
```

```python
import functools
import math

import jax
import jax.numpy as jnp
from jax import lax
from jax.experimental import pallas as pl
from jax.experimental.pallas import tpu as pltpu
from jax.sharding import PartitionSpec as P

HEADS = 12


epsilon = 1e-05
masked_score = -1000000000.0


def shifted(shard, axis, by):
    devices = lax.axis_size(axis)
    pairs = [(i, i + by) for i in range(devices) if 0 <= i + by < devices]
    return lax.ppermute(shard, axis, pairs)


def shifted_2(value, axis, steps):
    count = lax.axis_size(axis)
    pairs = [(source, (source + steps) % count) for source in range(count)]
    return lax.ppermute(value, axis, pairs)


def layer_norm(values, norm_gain, norm_bias):
    centre = jnp.mean(values, -1, keepdims=True)
    centred = values - centre
    spread = jnp.mean(centred * centred, -1, keepdims=True)
    return centred * lax.rsqrt(spread + epsilon) * norm_gain + norm_bias


def ffn_norm(up_value, norm_gain, norm_bias):
    return layer_norm(jax.nn.gelu(up_value, approximate=False), norm_gain, norm_bias)


def doc_place(row_ids, doc_row, row_count, blocks):
    device = row_ids // row_count
    local = row_ids % row_count
    shares = doc_row // blocks
    ends = jnp.cumsum(shares, dtype=jnp.int32)
    starts = ends - shares
    doc = jnp.sum((local[:, None] >= ends[None, :]).astype(jnp.int32), -1, dtype=jnp.int32)
    pick = (doc[:, None] == jnp.arange(doc_row.shape[0], dtype=jnp.int32)[None, :]).astype(
        jnp.int32
    )
    share_of = jnp.sum(pick * shares[None, :], -1, dtype=jnp.int32)
    start_of = jnp.sum(pick * starts[None, :], -1, dtype=jnp.int32)
    return (doc, device * share_of + local - start_of)


def visible(query_doc, query_place, key_doc, key_place):
    return (query_doc[:, None] == key_doc[None, :]) & (key_place[None, :] <= query_place[:, None])


def outer_sum(first_operand, second_operand):
    return lax.dot_general(
        first_operand, second_operand, (((0,), (0,)), ((), ())), preferred_element_type=jnp.float32
    )


def back_product(gradient, weight):
    return lax.dot_general(
        gradient, weight, (((1,), (1,)), ((), ())), preferred_element_type=jnp.float32
    )


def score_grads(
    query_heads, dout_heads, lse_heads, delta_heads, allowed, key_heads, value_heads, score_scale
):
    scores = (
        jnp.einsum("qhd,khd->hqk", query_heads, key_heads, preferred_element_type=jnp.float32)
        * score_scale
    )
    probabilities = jnp.where(allowed[None], jnp.exp(scores - lse_heads[:, :, None]), 0.0)
    weight_grad = jnp.einsum(
        "qhd,khd->hqk", dout_heads, value_heads, preferred_element_type=jnp.float32
    )
    score_grad = (probabilities * (weight_grad - delta_heads[:, :, None])).astype(jnp.bfloat16)
    return (probabilities.astype(jnp.bfloat16), score_grad)


def general_body(
    tokens,
    cotangent,
    doc_lengths,
    w_qkv,
    w_out,
    w_up,
    w_down,
    ln1_gain,
    ln1_bias,
    ln2_gain,
    ln2_bias,
    ln3_gain,
    ln3_bias,
    ln4_gain,
    ln4_bias,
):
    gathered = (
        lax.all_gather(w_qkv, ("dp", "blk"), axis=0, tiled=True),
        lax.all_gather(w_out, ("dp", "blk"), axis=0, tiled=True),
        lax.all_gather(w_up, ("dp", "blk"), axis=0, tiled=True),
        lax.all_gather(w_down, ("dp", "blk"), axis=0, tiled=True),
        lax.all_gather(ln1_gain, ("dp", "blk"), axis=0, tiled=True),
        lax.all_gather(ln1_bias, ("dp", "blk"), axis=0, tiled=True),
        lax.all_gather(ln2_gain, ("dp", "blk"), axis=0, tiled=True),
        lax.all_gather(ln2_bias, ("dp", "blk"), axis=0, tiled=True),
        lax.all_gather(ln3_gain, ("dp", "blk"), axis=0, tiled=True),
        lax.all_gather(ln3_bias, ("dp", "blk"), axis=0, tiled=True),
        lax.all_gather(ln4_gain, ("dp", "blk"), axis=0, tiled=True),
        lax.all_gather(ln4_bias, ("dp", "blk"), axis=0, tiled=True),
    )
    qkv_full, out_full, up_full, down_full = (gathered[0], gathered[1], gathered[2], gathered[3])
    norm_params = [value.astype(jnp.float32) for value in gathered[4:]]
    gain_one, bias_one, gain_two, bias_two, gain_three, bias_three, gain_four, bias_four = (
        norm_params
    )
    row_count, model_width = tokens.shape
    head_dim = model_width // HEADS
    score_scale = head_dim ** (-0.5)
    doc_row = doc_lengths[0]
    blocks = lax.axis_size("blk")
    place_index = lax.axis_index("blk")
    query_doc, query_place = doc_place(
        place_index * row_count + jnp.arange(row_count, dtype=jnp.int32), doc_row, row_count, blocks
    )

    def key_meta(first_row, count):
        return doc_place(first_row + jnp.arange(count, dtype=jnp.int32), doc_row, row_count, blocks)

    residual_in = tokens.astype(jnp.float32)
    normed = layer_norm(residual_in, gain_one, bias_one).astype(jnp.bfloat16)
    projected = jnp.dot(normed, qkv_full, preferred_element_type=jnp.float32).astype(jnp.bfloat16)
    queries = projected[:, :model_width]
    keys_own = projected[:, model_width : 2 * model_width]
    values_own = projected[:, 2 * model_width :]
    query_heads = queries.reshape(row_count, HEADS, head_dim)
    start_state = (
        jnp.full((HEADS, row_count), masked_score, jnp.float32),
        jnp.zeros((HEADS, row_count), jnp.float32),
        jnp.zeros((HEADS, row_count, head_dim), jnp.float32),
    )
    running = start_state
    key_part = lax.all_gather(keys_own, "blk", axis=0, tiled=True)
    value_part = lax.all_gather(values_own, "blk", axis=0, tiled=True)
    part_rows = key_part.shape[0]
    step_rows = math.gcd(part_rows, 512)
    count = part_rows // step_rows

    def one_step(state, element):
        key_block, value_block, block_start = element
        key_doc, key_place = key_meta(block_start, step_rows)
        allowed = visible(query_doc, query_place, key_doc, key_place)
        scores = (
            jnp.einsum(
                "qhd,khd->hqk",
                query_heads,
                key_block.reshape(step_rows, HEADS, head_dim),
                preferred_element_type=jnp.float32,
            )
            * score_scale
        )
        scores = jnp.where(allowed[None], scores, masked_score)
        peak_old, total_old, weighted_old = state
        peak_new = jnp.maximum(peak_old, jnp.max(scores, -1))
        weights = jnp.where(allowed[None], jnp.exp(scores - peak_new[:, :, None]), 0.0)
        factor = jnp.exp(peak_old - peak_new)
        total_new = total_old * factor + jnp.sum(weights, -1)
        weighted_new = weighted_old * factor[:, :, None] + jnp.einsum(
            "hqk,khd->hqd",
            weights.astype(jnp.bfloat16),
            value_block.reshape(step_rows, HEADS, head_dim),
            preferred_element_type=jnp.float32,
        )
        return ((peak_new, total_new, weighted_new), None)

    starts = jnp.arange(count, dtype=jnp.int32) * step_rows
    running, _ = lax.scan(
        one_step,
        running,
        (
            key_part.reshape(count, step_rows, model_width),
            value_part.reshape(count, step_rows, model_width),
            starts,
        ),
    )
    peak_score, total_weight, weighted_sum = running
    log_total = peak_score + jnp.log(total_weight)
    attended = (
        (weighted_sum / total_weight[:, :, None]).transpose(1, 0, 2).reshape(row_count, model_width)
    )
    inner = layer_norm(attended, gain_two, bias_two).astype(jnp.bfloat16)
    middle = residual_in + jnp.dot(inner, out_full, preferred_element_type=jnp.float32)
    normed_two = layer_norm(middle, gain_three, bias_three).astype(jnp.bfloat16)
    up_value = jnp.dot(normed_two, up_full, preferred_element_type=jnp.float32)
    hidden = ffn_norm(up_value, gain_four, bias_four).astype(jnp.bfloat16)
    output = (middle + jnp.dot(hidden, down_full, preferred_element_type=jnp.float32)).astype(
        jnp.bfloat16
    )
    grad_down = outer_sum(hidden, cotangent)
    d_hidden = back_product(cotangent, down_full)
    _, ffn_pullback = jax.vjp(ffn_norm, up_value, gain_four, bias_four)
    d_up, grad_gain_four, grad_bias_four = ffn_pullback(d_hidden)
    d_up_low = d_up.astype(jnp.bfloat16)
    grad_up = outer_sum(normed_two, d_up_low)
    _, third_pullback = jax.vjp(layer_norm, middle, gain_three, bias_three)
    d_middle_norm, grad_gain_three, grad_bias_three = third_pullback(
        back_product(d_up_low, up_full)
    )
    d_middle = cotangent.astype(jnp.float32) + d_middle_norm
    d_middle_low = d_middle.astype(jnp.bfloat16)
    grad_out = outer_sum(inner, d_middle_low)
    _, second_pullback = jax.vjp(layer_norm, attended, gain_two, bias_two)
    d_attended, grad_gain_two, grad_bias_two = second_pullback(back_product(d_middle_low, out_full))
    d_attended_low = d_attended.astype(jnp.bfloat16)
    dout_heads = d_attended_low.reshape(row_count, HEADS, head_dim)
    delta = jnp.einsum(
        "qhd,qhd->hq",
        d_attended_low.astype(jnp.float32).reshape(row_count, HEADS, head_dim),
        attended.reshape(row_count, HEADS, head_dim),
    )

    def turn(turn_index, loop_state):
        kv_now, grads_now, query_grad = loop_state
        source = (place_index - turn_index) % blocks
        key_doc, key_place = key_meta(source * row_count, row_count)
        allowed = visible(query_doc, query_place, key_doc, key_place)
        key_heads = kv_now[0].reshape(row_count, HEADS, head_dim)
        value_heads = kv_now[1].reshape(row_count, HEADS, head_dim)
        probabilities, score_grad = score_grads(
            query_heads, dout_heads, log_total, delta, allowed, key_heads, value_heads, score_scale
        )
        query_grad = (
            query_grad
            + jnp.einsum("hqk,khd->qhd", score_grad, key_heads, preferred_element_type=jnp.float32)
            * score_scale
        )
        key_grad = (
            jnp.einsum("hqk,qhd->khd", score_grad, query_heads, preferred_element_type=jnp.float32)
            * score_scale
        )
        value_grad = jnp.einsum(
            "hqk,qhd->khd", probabilities, dout_heads, preferred_element_type=jnp.float32
        )
        grads_now = grads_now + jnp.stack(
            [key_grad.reshape(row_count, model_width), value_grad.reshape(row_count, model_width)]
        )
        kv_now = shifted(kv_now, "blk", 1)
        grads_now = shifted_2(grads_now.astype(jnp.bfloat16), "blk", 1).astype(grads_now.dtype)
        return (kv_now, grads_now, query_grad)

    loop_start = (
        jnp.stack([keys_own, values_own]),
        jnp.zeros((2, row_count, model_width), jnp.float32),
        jnp.zeros((row_count, HEADS, head_dim), jnp.float32),
    )
    _, kv_grads, query_grad = lax.fori_loop(0, blocks, turn, loop_start)
    key_grad_all = kv_grads[0]
    value_grad_all = kv_grads[1]
    d_projected = jnp.concatenate(
        [query_grad.reshape(row_count, model_width), key_grad_all, value_grad_all], axis=1
    ).astype(jnp.bfloat16)
    grad_qkv = outer_sum(normed, d_projected)
    _, first_pullback = jax.vjp(layer_norm, residual_in, gain_one, bias_one)
    d_input_norm, grad_gain_one, grad_bias_one = first_pullback(back_product(d_projected, qkv_full))
    input_grad = (d_middle + d_input_norm).astype(jnp.bfloat16)
    summed = (
        lax.psum_scatter(grad_qkv, ("dp", "blk"), scatter_dimension=0, tiled=True),
        lax.psum_scatter(grad_out, ("dp", "blk"), scatter_dimension=0, tiled=True),
        lax.psum_scatter(grad_up, ("dp", "blk"), scatter_dimension=0, tiled=True),
        lax.psum_scatter(grad_down, ("dp", "blk"), scatter_dimension=0, tiled=True),
        lax.psum_scatter(grad_gain_one, ("dp", "blk"), scatter_dimension=0, tiled=True),
        lax.psum_scatter(grad_bias_one, ("dp", "blk"), scatter_dimension=0, tiled=True),
        lax.psum_scatter(grad_gain_two, ("dp", "blk"), scatter_dimension=0, tiled=True),
        lax.psum_scatter(grad_bias_two, ("dp", "blk"), scatter_dimension=0, tiled=True),
        lax.psum_scatter(grad_gain_three, ("dp", "blk"), scatter_dimension=0, tiled=True),
        lax.psum_scatter(grad_bias_three, ("dp", "blk"), scatter_dimension=0, tiled=True),
        lax.psum_scatter(grad_gain_four, ("dp", "blk"), scatter_dimension=0, tiled=True),
        lax.psum_scatter(grad_bias_four, ("dp", "blk"), scatter_dimension=0, tiled=True),
    )
    return (output, input_grad) + tuple(summed)


F32 = jnp.float32
BF16 = jnp.bfloat16
CORE, Y_LINK, X_LINK, Z_LINK = 1, 2, 4, 8
Z_MASKS = (0, 8, 16, 24)
PLANE_MASKS = (0, Y_LINK, X_LINK, X_LINK + Y_LINK)


def swap(value, mask):
    devices = lax.axis_size("dp") * lax.axis_size("blk")
    return lax.ppermute(value, ("dp", "blk"), [(i, i ^ mask) for i in range(devices)])


def dot_rows(a, b):
    return lax.dot_general(a, b, (((1,), (0,)), ((), ())), preferred_element_type=F32)


def dot_back(a, b):
    return lax.dot_general(a, b, (((1,), (1,)), ((), ())), preferred_element_type=F32)


def dot_outer(a, b):
    return lax.dot_general(a, b, (((0,), (0,)), ((), ())), preferred_element_type=F32)


def row_stats(values):
    centre = jnp.mean(values, -1, keepdims=True)
    centred = values - centre
    spread = jnp.mean(centred * centred, -1, keepdims=True)
    scale = lax.rsqrt(spread + epsilon)
    return centred * scale, scale


def norm_back(grad_unit, unit, scale):
    first = jnp.mean(grad_unit, -1, keepdims=True)
    second = jnp.mean(grad_unit * unit, -1, keepdims=True)
    return scale * (grad_unit - first - unit * second)


def run_copies(copies):
    for copy in copies:
        copy.start()


def wait_copies(copies):
    for copy in copies:
        copy.wait()


def spread_wide(columns, width):
    quarter = width // 32
    run = 4 * quarter
    place = lax.broadcasted_iota(jnp.int32, (run, 4 * run), 1)
    row = lax.broadcasted_iota(jnp.int32, (run, 4 * run), 0)
    lines = []
    for first in (0, 4):
        pieces = []
        for m in range(8):
            piece = 0.0
            for c in range(4):
                want = (row // quarter) * run + c * quarter + row % quarter
                put = (place == want).astype(BF16)
                got = dot_outer(columns[m * run : (m + 1) * run, first : first + 8], put)
                piece = piece + got[c : c + 1]
            pieces.append(piece)
        lines.append(jnp.concatenate(pieces, axis=1))
    return jnp.concatenate(lines, axis=0)


def fold_heads(value):
    rows = value.shape[0] // 2
    last = jnp.concatenate([value[:rows, 128:], value[rows:, 128:]], axis=1)
    return jnp.concatenate([value[:, :128], last], axis=0)


def unfold_heads(value):
    rows = value.shape[0] // 3
    last = value[2 * rows :]
    last = jnp.concatenate([last[:, :64], last[:, 64:]], axis=0)
    return jnp.concatenate([value[: 2 * rows], last], axis=1)


def attention_forward(
    pos, t0, t1, t2, t3, own, other, normed, units, proj, weight, vectors, wide, att, mixed_out, stats
):
    rows, width = t0.shape
    slot_rows = own.shape[1]
    head_dim = width // HEADS
    span = mixed_out.shape[1]
    heads = span // head_dim
    blk = pos[1]
    for x, source in enumerate((own, other)):
        for z in range(4):
            slot = 2 * z + (pos[0] % 2 ^ x)
            at = pl.ds(pl.multiple_of(slot * slot_rows, slot_rows), slot_rows)
            weight[at, :] = source[z]
    tail = (3 * span // 128) * 128
    first = 3 * span - tail
    turned = jnp.transpose(weight[:, tail:].astype(F32))
    vectors[...] = turned[first : first + 8, :]
    wide[...] = spread_wide(weight[:, tail + first + 6 : tail + first + 22], width)
    gain, bias = vectors[0:1, :], vectors[1:2, :]
    for k, source in enumerate((t0, t1, t2, t3)):
        unit, _ = row_stats(source[...].astype(F32))
        at = pl.ds(pl.multiple_of((blk ^ k) * rows, rows), rows)
        value = (unit * gain + bias).astype(BF16)
        normed[at, :] = value
        units[at, :] = unit.astype(BF16)
        proj[at, :] = dot_rows(value, weight[...]).astype(BF16)
    scale = head_dim ** (-0.5)
    below = lax.broadcasted_iota(jnp.int32, (rows, rows), 1) <= lax.broadcasted_iota(
        jnp.int32, (rows, rows), 0
    )
    lane = lax.broadcasted_iota(jnp.int32, (rows, 128), 1)
    for block in range(4):
        mixed = []
        low, high = block * rows, (block + 1) * rows
        stat = jnp.zeros((rows, 128), F32)
        for head in range(heads):
            q = proj[low:high, head * head_dim : (head + 1) * head_dim] * BF16(scale)
            k = proj[:high, span + head * head_dim : span + (head + 1) * head_dim]
            v = proj[:high, 2 * span + head * head_dim : 2 * span + (head + 1) * head_dim]
            own = jnp.where(below, dot_back(q, k[low:]), masked_score)
            peak = jnp.max(own, -1, keepdims=True)
            if block:
                past = dot_back(q, k[:low])
                peak = jnp.maximum(peak, jnp.max(past, -1, keepdims=True))
            own = jnp.exp(own - peak)
            total = jnp.sum(own, -1, keepdims=True)
            mix = dot_rows(own.astype(BF16), v[low:])
            if block:
                past = jnp.exp(past - peak)
                total = total + jnp.sum(past, -1, keepdims=True)
                mix = mix + dot_rows(past.astype(BF16), v[:low])
            mixed.append(mix / total)
            stat = jnp.where(lane == head, peak + jnp.log(total), stat)
        stats[low:high, :] = stat
        value = jnp.concatenate(mixed, axis=1)
        mixed_out[low:high, :] = value
        att[block] = fold_heads(value.astype(BF16))


def ffn_forward(
    pos, att, tokens, vectors, wide_gains, weights,
    hidden, acts, middle, unit_four, slope, scale_four,
    w_out, w_up, up, sems,
):
    rows, width = tokens.shape
    copies = [
        pltpu.make_async_copy(weights.at[:, pl.ds(0, width)], w_out, sems.at[0]),
        pltpu.make_async_copy(weights.at[:, pl.ds(width, w_up.shape[1])], w_up, sems.at[1]),
    ]
    run_copies(copies)
    attended = jnp.concatenate([unfold_heads(att[j]) for j in range(4)], axis=1).astype(F32)
    unit, _ = row_stats(attended)
    inner_low = (unit * vectors[2:3, :] + vectors[3:4, :]).astype(BF16)
    acts[:, width:] = inner_low
    copies[0].wait()
    mid = tokens[...].astype(F32) + dot_rows(inner_low, w_out[...])
    middle[...] = mid
    unit, _ = row_stats(mid)
    low = (unit * vectors[4:5, :] + vectors[5:6, :]).astype(BF16)
    acts[:, :width] = low
    copies[1].wait()
    up[...] = dot_rows(low, w_up[...])
    step = 64
    gain, bias = wide_gains[0:1, :], wide_gains[1:2, :]

    def chunk(i, carry):
        at = pl.ds(pl.multiple_of(i * step, step), step)
        value = up[at, :]
        gate = 0.5 * (1.0 + lax.erf(value * (2.0**-0.5)))
        slope[at, :] = (gate + value * jnp.exp(-0.5 * value * value) * (0.5 / math.pi) ** 0.5).astype(
            BF16
        )
        unit, scale = row_stats(value * gate)
        unit_four[at, :] = unit.astype(BF16)
        hidden[at, :] = (unit * gain + bias).astype(BF16)
        scale_four[at, :] = jnp.broadcast_to(scale, (step, 128))
        return carry

    lax.fori_loop(0, rows // step, chunk, 0, unroll=True)


def down_copies(pos, stacks, target, sems):
    rows = stacks[0].shape[1]
    plane = 2 * (pos[0] % 2) + pos[1] // 2
    copies = []
    for other in range(2):
        for mask in range(4):
            for z in range(4):
                slot = 2 * (4 * z + (plane ^ mask)) + (pos[1] % 2 ^ other)
                copies.append(
                    pltpu.make_async_copy(
                        stacks[other * 4 + mask].at[z],
                        target.at[pl.ds(pl.multiple_of(slot * rows, rows), rows)],
                        sems.at[len(copies)],
                    )
                )
    return copies


def fold(value):
    total = value[:, :128]
    for start in range(128, value.shape[1], 128):
        total = total + value[:, start : start + 128]
    return total


def ffn_backward(
    pos, att, cot, vectors, wide_gains, middle, hidden_far, unit_four, slope, scale_four, weights,
    s0, s1, s2, s3, s4, s5, s6, s7,
    output, grads, d_middle, d0, d1, d2, d3, vector_grads, wide_grads,
    w_down, w_out, w_up, hidden, units, slopes, d_hidden, sems,
):
    rows, width = cot.shape
    wide = w_up.shape[1]
    copies = down_copies(pos, (s0, s1, s2, s3, s4, s5, s6, s7), w_down, sems)
    later = []
    for source, target in (
        (unit_four, units),
        (hidden_far, hidden),
        (slope, slopes),
        (weights.at[:, pl.ds(width, wide)], w_up),
        (weights.at[:, pl.ds(0, width)], w_out),
    ):
        later.append(pltpu.make_async_copy(source, target, sems.at[len(copies) + len(later)]))
    by_z = [copies[q::4] for q in range(4)]
    run_copies(by_z[0] + later[:1] + by_z[1] + later[1:2] + by_z[2] + by_z[3] + later[2:])

    def first_grad(q):
        wait_copies(by_z[q] + later[: 2 if q == 0 else 0])
        return dot_back(cot[...], w_down[q * width : (q + 1) * width, :])

    def fold_rows(value):
        total = value[:8]
        for start in range(8, rows, 8):
            total = total + value[start : start + 8]
        return jnp.sum(total, 0, keepdims=True)

    current = first_grad(0)
    first = jnp.zeros((rows, 128), F32)
    second = jnp.zeros((rows, 128), F32)
    out = middle[...]
    for q in range(4):
        at = slice(q * width, (q + 1) * width)
        if q < 3:
            following = first_grad(q + 1)
        out = out + dot_rows(hidden[:, at], w_down[at, :])
        d_hidden[:, at] = current
        unit = units[:, at].astype(F32)
        part = current * unit
        wide_grads[0:1, at] = fold_rows(part)
        wide_grads[1:2, at] = fold_rows(current)
        gain = wide_gains[0:1, at]
        first = first + fold(current * gain)
        second = second + fold(part * gain)
        current = following
    output[...] = out.astype(BF16)
    first = jnp.sum(first, -1, keepdims=True) * (1.0 / wide)
    second = jnp.sum(second, -1, keepdims=True) * (1.0 / wide)
    scale = scale_four[:, 0:1]
    wait_copies(later[2:])

    def second_grad(q):
        at = slice(q * width, (q + 1) * width)
        grad = d_hidden[:, at] * wide_gains[0:1, at] - first - units[:, at].astype(F32) * second
        grad = (scale * grad * slopes[:, at].astype(F32)).astype(BF16)
        grads[:, at] = grad
        return grad

    d_normed = 0.0
    for q in range(4):
        d_normed = d_normed + dot_back(second_grad(q), w_up[:, q * width : (q + 1) * width])
    unit, scale = row_stats(middle[...])
    gain_three = jnp.sum(d_normed * unit, 0, keepdims=True)
    bias_three = jnp.sum(d_normed, 0, keepdims=True)
    d_mid = cot[...].astype(F32) + norm_back(d_normed * vectors[4:5, :], unit, scale)
    d_middle[...] = d_mid
    d_mid_low = d_mid.astype(BF16)
    grads[:, wide:] = d_mid_low
    d_inner = dot_back(d_mid_low, w_out[...])
    attended = jnp.concatenate([unfold_heads(att[j]) for j in range(4)], axis=1).astype(F32)
    unit, scale = row_stats(attended)
    gain_two = jnp.sum(d_inner * unit, 0, keepdims=True)
    bias_two = jnp.sum(d_inner, 0, keepdims=True)
    vector_grads[...] = jnp.concatenate(
        [gain_two, bias_two, gain_three, bias_three, jnp.zeros((4, width), F32)], axis=0
    )
    back = norm_back(d_inner * vectors[2:3, :], unit, scale).astype(BF16)
    span = width // 4
    parts = [back[:, j * span : (j + 1) * span] for j in range(4)]
    for k, target in enumerate((d0, d1, d2, d3)):
        value = parts[k]
        for j in range(4):
            if j != k:
                value = jnp.where((pos[1] ^ k) == j, parts[j], value)
        target[...] = fold_heads(value)


def piece_copies(pos, held, targets, sems, zs):
    chip = pos[0] * 2 + pos[1] // 2
    copies = []
    for start, masks, target in targets:
        for i, plane in enumerate(masks):
            for z in zs:
                slot = ((chip ^ plane) & 3) + 4 * z
                copies.append(
                    pltpu.make_async_copy(
                        held.at[slot, :, pl.ds(start, target.shape[3])],
                        target.at[i, z],
                        sems.at[len(copies)],
                    )
                )
    return copies


def down_grads(pos, hidden, cot, mine_far, theirs_far, mine, theirs, sems):
    rows = mine.shape[2]
    plane = 2 * (pos[0] % 2) + pos[1] // 2
    first = pos[1] % 2 == 0
    copies = []
    for pair in range(hidden.shape[1] // (4 * rows)):
        value = dot_outer(hidden[:, 4 * rows * pair : 4 * rows * (pair + 1)], cot[...]).astype(BF16)
        for i in range(2):
            chip = 2 * pair + i
            low, high = value[2 * i * rows : (2 * i + 1) * rows], value[(2 * i + 1) * rows : (2 * i + 2) * rows]
            mine[chip // 4, (chip % 4) ^ plane] = jnp.where(first, low, high)
            theirs[chip // 4, (chip % 4) ^ plane] = jnp.where(first, high, low)
        if pair % 2:
            z = pair // 2
            for k, (source, target) in enumerate(((mine, mine_far), (theirs, theirs_far))):
                copies.append(pltpu.make_async_copy(source.at[z], target.at[z], sems.at[k, z]))
                copies[-1].start()
    wait_copies(copies)


def up_grads(
    pos, acts, acts_other, g0, g1, down_mine, down_got,
    keep_a, send_a, keep_b, send_b, down_grad,
    held, left, right, chosen, down, out_sems, sems,
):
    rows = held.shape[1]
    core = pos[1] % 2
    width = acts.shape[1] // 2
    wide = 4 * width
    copies = []

    def load(source, target):
        copies.append(pltpu.make_async_copy(source, target, sems.at[len(copies)]))
        copies[-1].start()

    for i, source in enumerate((acts, acts_other)):
        load(source, left.at[i])
    for i, source in enumerate((g0, g1)):
        load(source, right.at[i])
    for i, source in enumerate((down_mine, down_got)):
        load(source, down.at[i])
    row = lax.broadcasted_iota(jnp.int32, (width, width // 2), 0)
    column = lax.broadcasted_iota(jnp.int32, (width, width // 2), 1)
    take = (row // rows == 2 * (column // rows) + core) & (row % rows == column % rows)
    take = take.astype(BF16)
    wait_copies(copies[:2])
    for i in range(2):
        for part in range(2):
            at = slice(part * width // 2, (part + 1) * width // 2)
            chosen[i, :, at] = dot_rows(
                left[i, :, part * width : (part + 1) * width], take
            ).astype(BF16)
    cut = keep_a.shape[3]
    pieces = ((0, (0, 1), keep_a), (0, (2, 3), send_a), (cut, (0, 2), keep_b), (cut, (1, 3), send_b))
    tile = 384
    wait_copies(copies[2:4])
    outs = []
    for c in range(0, wide + width, tile):
        from_up = c >= width
        source = c - width if from_up else wide + c
        first = 0 if from_up else width // 2
        value = 0.0
        for i in range(2):
            value = value + dot_outer(
                chosen[i, :, first : first + width // 2], right[i, :, source : source + tile]
            )
        for chip in range(16):
            held[chip, :, c : c + tile] = value[chip * rows : (chip + 1) * rows].astype(BF16)
        if c + tile == cut or c + tile == wide + width:
            part = len(outs)
            outs.append(
                piece_copies(pos, held, pieces[2 * part : 2 * part + 2], out_sems.at[part], range(4))
            )
            run_copies(outs[-1])
    wait_copies(copies[4:])
    for z in range(down.shape[1]):
        down[0, z] = down[0, z] + down[1, z]
    outs.append([pltpu.make_async_copy(down.at[0], down_grad, sems.at[0])])
    run_copies(outs[-1])
    for group in outs:
        wait_copies(group)


def gather_wide(grads, width):
    quarter = width // 32
    run = 4 * quarter
    place = lax.broadcasted_iota(jnp.int32, (run, 4 * run), 1)
    row = lax.broadcasted_iota(jnp.int32, (run, 4 * run), 0)
    lane = lax.broadcasted_iota(jnp.int32, (run, 128), 1)
    rows = jnp.concatenate([grads, jnp.zeros((126, grads.shape[1]), F32)], axis=0).astype(BF16)
    pieces = []
    for m in range(8):
        piece = jnp.zeros((run, 128), F32)
        for c in range(4):
            want = (row // quarter) * run + c * quarter + row % quarter
            put = (place == want).astype(BF16)
            got = dot_back(put, rows[:, m * 4 * run : (m + 1) * 4 * run])
            for v in range(2):
                piece = piece + jnp.where(lane == 6 + 4 * v + c, got[:, v : v + 1], 0.0)
        pieces.append(piece)
    return jnp.concatenate(pieces, axis=0)


def attention_backward(
    pos, d0, d1, d2, d3, normed_far, units_far, proj, weight_far, mixed, stats, vector_grads,
    wide_grads,
    own, own_far, other, p0, p1,
    d_out, d_proj, tt, held, d_normed, normed, units, weight, load_sems, sems,
):
    rows, width = d0.shape[0] * 2 // 3, normed.shape[1]
    loads = [
        pltpu.make_async_copy(source, target, load_sems.at[i])
        for i, (source, target) in enumerate(
            ((weight_far, weight), (units_far, units), (normed_far, normed))
        )
    ]
    run_copies(loads)
    head_dim = width // HEADS
    span = d_out.shape[1]
    heads = span // head_dim
    dp, blk = pos[0], pos[1]
    for k, source in enumerate((d0, d1, d2, d3)):
        d_out[pl.ds(pl.multiple_of((blk ^ k) * rows, rows), rows), :] = unfold_heads(source[...])
    scale = head_dim ** (-0.5)
    below = lax.broadcasted_iota(jnp.int32, (rows, rows), 1) <= lax.broadcasted_iota(
        jnp.int32, (rows, rows), 0
    )
    for head in range(heads):
        at_q = slice(head * head_dim, (head + 1) * head_dim)
        at_k = slice(span + head * head_dim, span + (head + 1) * head_dim)
        at_v = slice(2 * span + head * head_dim, 2 * span + (head + 1) * head_dim)
        tt[...] = jnp.zeros_like(tt)
        for block in range(4):
            low, high = block * rows, (block + 1) * rows
            q = proj[low:high, at_q] * BF16(scale)
            d = d_out[low:high, at_q]
            log_total = stats[low:high, head : head + 1]
            delta = jnp.sum(d.astype(F32) * mixed[low:high, at_q], -1, keepdims=True)
            d_query = 0.0
            for start, end in [(low, high)] + ([(0, low)] if block else []):
                score = dot_back(q, proj[start:end, at_k])
                if start == low:
                    score = jnp.where(below, score, masked_score)
                score = jnp.exp(score - log_total)
                grad = dot_back(d, proj[start:end, at_v])
                d_score = (score * (grad - delta)).astype(BF16)
                d_query = d_query + dot_rows(d_score, proj[start:end, at_k])
                tt[0, :, start:end] += dot_outer(q, d_score)
                tt[1, :, start:end] += dot_outer(d, score.astype(BF16))
            d_proj[low:high, at_q] = (d_query * scale).astype(BF16)
        d_proj[:, at_k] = jnp.transpose(tt[0]).astype(BF16)
        d_proj[:, at_v] = jnp.transpose(tt[1]).astype(BF16)
    columns = weight.shape[1]
    vector_sums = []
    wait_copies(loads[:2])
    for j in range(4):
        at = slice(j * rows, (j + 1) * rows)
        grad = dot_back(d_proj[at, :], weight[:, : 3 * span])
        unit = units[at, :].astype(F32)
        vector_sums.append((jnp.sum(grad * unit, 0, keepdims=True), jnp.sum(grad, 0, keepdims=True)))
        d_normed[j ^ blk] = grad.astype(BF16)
    copies = [
        pltpu.make_async_copy(d_normed.at[k], target, sems.at[8 + k])
        for k, target in enumerate((own, other.at[0], own_far, other.at[1]))
    ]
    run_copies(copies)
    loads[2].wait()
    sums = [sum(v[i] for v in vector_sums) for i in range(2)]
    turned = jnp.transpose(
        jnp.concatenate(
            sums + [vector_grads[0:4, :], jnp.zeros((128 - 6, width), F32)], axis=0
        )
    ) + gather_wide(wide_grads[...], width)
    slot_rows = held.shape[1]
    for r in range(0, width, 2 * slot_rows):
        value = dot_outer(normed[:, r : r + 2 * slot_rows], d_proj[...])
        value = jnp.concatenate(
            [value, turned[r : r + 2 * slot_rows, : columns - 3 * span]], axis=1
        ).astype(BF16)
        held[r // slot_rows] = value[:slot_rows]
        held[r // slot_rows + 1] = value[slot_rows:]
    pieces = []
    for x, target in enumerate((p0, p1)):
        for z in range(4):
            slot = ((dp ^ x) & 1) + 2 * z
            pieces.append(pltpu.make_async_copy(held.at[slot], target.at[z], sems.at[x * 4 + z]))
    run_copies(pieces)
    wait_copies(copies + pieces)


def local_kernel(kernel, outs, ins, scratch=(), us=2, in_any=(), out_any=(), after=(), passed=(), mib=16):
    here = pl.BlockSpec(memory_space=pltpu.VMEM)
    far = pl.BlockSpec(memory_space=pl.ANY)
    specs = [pl.BlockSpec(memory_space=pltpu.SMEM)]
    specs += [far if i in in_any else here for i in range(1, len(ins))]
    specs += [far] * (len(after) + len(passed))
    unread = len(ins) + len(after) + len(passed)
    ends = unread + len(outs)

    def run(*refs):
        kernel(*refs[: len(ins)], *refs[unread:ends], *refs[ends + len(passed) :])

    return pl.pallas_call(
        run,
        out_shape=[*outs, *(shape_of(v.dtype, *v.shape) for v in passed)],
        in_specs=specs,
        out_specs=[far if i in out_any else here for i in range(len(outs))] + [far] * len(passed),
        input_output_aliases={
            len(ins) + len(after) + i: len(outs) + i for i in range(len(passed))
        },
        scratch_shapes=list(scratch),
        compiler_params=pltpu.CompilerParams(vmem_limit_bytes=mib * 1024 * 1024),
        cost_estimate=pl.CostEstimate(
            flops=int(us * 1.15e9) // 100, bytes_accessed=int(us * 3.6e6) // 100, transcendentals=0
        ),
    )(*ins, *after, *passed)


def shape_of(dtype, *shape):
    return jax.ShapeDtypeStruct(shape, dtype)


def z_exchange(own):
    return [own] + [swap(own, mask) for mask in Z_MASKS[1:]]


def pack_weights(
    pos, w_qkv, w_out, w_up, gains, wide_gains, packed, slices
):
    rows, width = w_out.shape
    span = width // 4
    packed[:, :width] = w_out[...]
    packed[:, width:] = w_up[...]
    wide = wide_gains[...].astype(F32)
    lines = [gains[...].astype(F32)] + [
        wide[i : i + 1, c * rows : (c + 1) * rows] for i in range(2) for c in range(4)
    ]
    square = jnp.concatenate(lines + [jnp.zeros((128 - 14, rows), F32)], axis=0)
    square = jnp.concatenate([square, jnp.zeros((128, 128 - rows), F32)], axis=1)
    ends = jnp.transpose(square)[:rows, : slices.shape[2] - 3 * span].astype(BF16)
    for j in range(4):
        parts = [w_qkv[:, p * width + j * span : p * width + (j + 1) * span] for p in range(3)]
        slices[j] = jnp.concatenate(parts + [ends], axis=1)

def stack_z(pos, b0, b1, b2, b3, target):
    for k, part in enumerate((b0, b1, b2, b3)):
        target[(pos[0] // 2) ^ k] = part[...]


def nothing(pos):
    pass


def sum_first(pos, keep_a, got_a, keep_b, got_b, own_a, send_a, own_b, send_b):
    for keep, got, own, send in ((keep_a, got_a, own_a, send_a), (keep_b, got_b, own_b, send_b)):
        own[...] = keep[0].astype(F32) + got[0].astype(F32)
        send[...] = (keep[1].astype(F32) + got[1].astype(F32)).astype(BF16)


def sum_second(pos, own_a, got_a, own_b, got_b, total):
    cut = own_a.shape[2]
    total[:, :, :cut] = (own_a[...] + got_a[...].astype(F32)).astype(BF16)
    total[:, :, cut:] = (own_b[...] + got_b[...].astype(F32)).astype(BF16)


def sum_two(pos, p0, p1, z0, z1, z2, z3):
    for k, target in enumerate((z0, z1, z2, z3)):
        at = (pos[0] // 2) ^ k
        target[...] = (p0[at].astype(F32) + p1[at].astype(F32)).astype(target.dtype)


def join_heads(pos, parts, grad, e0, e1, e2, e3, e4, e5, e6, e7):
    width = grad.shape[1] // 3
    span = width // 4
    rows = grad.shape[0]
    for j in range(4):
        for p in range(3):
            grad[:, p * width + j * span : p * width + (j + 1) * span] = parts[
                j, :, p * span : (p + 1) * span
            ]
    tail = (3 * span // 128) * 128
    last = (parts[0] + parts[1]) + (parts[2] + parts[3])
    square = jnp.concatenate([last[:, tail:], jnp.zeros((128 - rows, 128), F32)], axis=0)
    ends = jnp.transpose(square)[3 * span - tail : 3 * span - tail + 16]
    for i, target in enumerate((e0, e1, e2, e3, e4, e5)):
        target[...] = ends[i : i + 1, :rows]
    for i, target in enumerate((e6, e7)):
        first = 6 + 4 * i
        target[...] = jnp.concatenate(
            [ends[first + c : first + c + 1, :rows] for c in range(4)], axis=1
        )


def far_pair(pos, own, core_part, target):
    target[...] = (own[...].astype(F32) + core_part[1].astype(F32)).astype(BF16)


def sum_four(pos, p0, p1, p2, p3, total):
    total[...] = (p0[...].astype(F32) + p1[...].astype(F32)) + (
        p2[...].astype(F32) + p3[...].astype(F32)
    )


def input_back(pos, own, core_part, far, tokens, d_middle, vectors, input_grad):
    grad = own[...].astype(F32) + core_part[0].astype(F32) + far[...].astype(F32)
    unit, scale = row_stats(tokens[...].astype(F32))
    input_grad[...] = (d_middle[...] + norm_back(grad * vectors[0:1, :], unit, scale)).astype(BF16)


def groups_of(fixed):
    numbers = range(lax.axis_size("dp") * lax.axis_size("blk"))
    return [[i for i in numbers if i & fixed == j] for j in numbers if j & fixed == j]


def fast_body(
    tokens, cotangent, doc_lengths, w_qkv, w_out, w_up, w_down,
    ln1_gain, ln1_bias, ln2_gain, ln2_bias, ln3_gain, ln3_bias, ln4_gain, ln4_bias,
):
    rows, width = tokens.shape
    shard = w_qkv.shape[0]
    ff = w_up.shape[1]
    head_dim = width // HEADS
    span = width // 4
    group = rows * 4
    columns = -(-(3 * span + 16) // 128) * 128
    slot_rows = 4 * shard
    both = ("dp", "blk")
    along_z = groups_of(CORE + Y_LINK + X_LINK)
    in_plane = groups_of(CORE + 3 * Z_LINK)
    dp, blk = lax.axis_index("dp"), lax.axis_index("blk")
    pos = jnp.stack([dp, blk]).astype(jnp.int32)

    def gather(value, groups):
        return lax.all_gather(value, both, axis=0, axis_index_groups=groups)

    def scatter(value, groups):
        return lax.psum_scatter(
            value, both, scatter_dimension=0, axis_index_groups=groups, tiled=False
        )

    norms = [ln1_gain, ln1_bias, ln2_gain, ln2_bias, ln3_gain, ln3_bias]
    gains = jnp.stack(norms)
    wide_gains = jnp.stack([ln4_gain, ln4_bias])
    packed, slices = local_kernel(
        pack_weights,
        [shape_of(BF16, shard, width + ff), shape_of(BF16, 4, shard, columns)],
        [pos, w_qkv, w_out, w_up, gains, wide_gains],
        mib=56,
    )
    weights = lax.all_gather(packed, both, axis=0, tiled=True)

    token_y = swap(tokens, Y_LINK)

    slices = lax.all_to_all(slices, "blk", 0, 0).reshape(slot_rows, columns)
    down_own, slices = local_kernel(
        stack_z,
        [shape_of(BF16, 4, *w_down.shape)],
        [pos, w_down] + [swap(w_down, mask) for mask in Z_MASKS[1:]],
        after=(token_y,),
        passed=(slices,),
    )
    slices, down_own, down_x, down_y = local_kernel(
        stack_z,
        [shape_of(BF16, 4, slot_rows, columns)],
        [pos, slices] + [swap(slices, mask) for mask in Z_MASKS[1:]],
        passed=(down_own, swap(down_own, X_LINK), swap(down_own, Y_LINK)),
    )
    down_parts = [down_own, down_y, down_x, swap(down_x, Y_LINK)]
    token_core, token_both = swap(tokens, CORE), swap(token_y, CORE)
    slices_x = swap(slices, X_LINK)

    tokens_group = [tokens, token_core, token_y, token_both]
    packed_rows = rows * 3 // 2
    normed, units, proj, weight, vectors, wide, att, mixed, stats = local_kernel(
        attention_forward,
        [
            shape_of(BF16, group, width),
            shape_of(BF16, group, width),
            shape_of(BF16, group, columns),
            shape_of(BF16, width, columns),
            shape_of(F32, 8, width),
            shape_of(F32, 2, ff),
            shape_of(BF16, 4, packed_rows, 128),
            shape_of(F32, group, span),
            shape_of(F32, group, 128),
        ],
        [pos, *tokens_group, slices, slices_x],
        us=11,
        mib=56,
    )
    att = lax.all_to_all(att, "blk", 0, 0)
    down_parts = list(
        local_kernel(nothing, [], [pos], mib=56, after=(att,), passed=down_parts)
    )
    down_all = down_parts + [swap(value, CORE) for value in down_parts]
    hidden, acts, middle, unit_four, slope, scale_four = local_kernel(
        ffn_forward,
        [
            shape_of(BF16, rows, ff),
            shape_of(BF16, rows, 2 * width),
            shape_of(F32, rows, width),
            shape_of(BF16, rows, ff),
            shape_of(BF16, rows, ff),
            shape_of(F32, rows, 128),
        ],
        [pos, att, tokens, vectors, wide, weights],
        [
            pltpu.VMEM((width, width), BF16),
            pltpu.VMEM((width, ff), BF16),
            pltpu.VMEM((rows, ff), F32),
            pltpu.SemaphoreType.DMA((2,)),
        ],
        in_any=(5,),
        us=12,
        mib=56,
    )
    down_mine, down_theirs = local_kernel(
        down_grads,
        [shape_of(BF16, 4, 4, *w_down.shape)] * 2,
        [pos, hidden, cotangent],
        [pltpu.VMEM((4, 4, *w_down.shape), BF16)] * 2 + [pltpu.SemaphoreType.DMA((2, 4))],
        out_any=(0, 1),
        us=5,
        mib=56,
    )
    acts_other = swap(acts, CORE)
    output, grads, d_middle, d0, d1, d2, d3, vector_grads, wide_grads, down_theirs = local_kernel(
        ffn_backward,
        [
            shape_of(BF16, rows, width),
            shape_of(BF16, rows, ff + width),
            shape_of(F32, rows, width),
            *[shape_of(BF16, packed_rows, 128)] * 4,
            shape_of(F32, 8, width),
            shape_of(F32, 2, ff),
        ],
        [
            pos, att, cotangent, vectors, wide, middle, hidden, unit_four, slope, scale_four,
            weights, *down_all,
        ],
        [
            pltpu.VMEM((ff, width), BF16),
            pltpu.VMEM((width, width), BF16),
            pltpu.VMEM((width, ff), BF16),
            pltpu.VMEM((rows, ff), BF16),
            pltpu.VMEM((rows, ff), BF16),
            pltpu.VMEM((rows, ff), BF16),
            pltpu.VMEM((rows, ff), F32),
            pltpu.SemaphoreType.DMA((37,)),
        ],
        in_any=(6, 7, 8, *range(10, 19)),
        us=15,
        after=(down_mine, acts_other),
        passed=(down_theirs,),
        mib=56,
    )
    d_att = [d0] + [swap(value, k) for k, value in ((1, d1), (2, d2), (3, d3))]
    grads_other, down_got = swap(grads, CORE), swap(down_theirs, CORE)
    a_columns = -(-(width + ff) // (2 * 384)) * 384
    piece_a = (4, shard, a_columns)
    piece_b = (4, shard, width + ff - a_columns)
    keep_a, send_a, keep_b, send_b, down_grad = local_kernel(
        up_grads,
        [shape_of(BF16, 2, *piece_a)] * 2
        + [shape_of(BF16, 2, *piece_b)] * 2
        + [shape_of(BF16, *down_mine.shape)],
        [pos, acts, acts_other, grads, grads_other, down_mine, down_got],
        [
            pltpu.VMEM((16, shard, width + ff), BF16),
            pltpu.VMEM((2, rows, 2 * width), BF16),
            pltpu.VMEM((2, rows, width + ff), BF16),
            pltpu.VMEM((2, rows, width), BF16),
            pltpu.VMEM((2, *down_mine.shape), BF16),
            pltpu.SemaphoreType.DMA((2, 16)),
            pltpu.SemaphoreType.DMA((6,)),
        ],
        in_any=range(1, 7),
        out_any=range(5),
        after=d_att[1:],
        mib=56,
    )
    down_first = scatter(down_grad, along_z)
    got_a, got_b = swap(send_a, X_LINK), swap(send_b, Y_LINK)

    def total_of(pieces):
        return sum(piece.astype(F32) for piece in pieces)

    own_part, own_far, other_part, p0, p1 = local_kernel(
        attention_backward,
        [shape_of(BF16, rows, width)] * 2
        + [shape_of(BF16, 2, rows, width)]
        + [shape_of(BF16, 4, slot_rows, columns)] * 2,
        [
            pos, *d_att, normed, units, proj, weight, mixed, stats, vector_grads, wide_grads
        ],
        [
            pltpu.VMEM((group, span), BF16),
            pltpu.VMEM((group, 3 * span), BF16),
            pltpu.VMEM((2, head_dim, group), F32),
            pltpu.VMEM((8, slot_rows, columns), BF16),
            pltpu.VMEM((4, rows, width), BF16),
            pltpu.VMEM((group, width), BF16),
            pltpu.VMEM((group, width), BF16),
            pltpu.VMEM((width, columns), BF16),
            pltpu.SemaphoreType.DMA((3,)),
            pltpu.SemaphoreType.DMA((12,)),
        ],
        in_any=(5, 6, 8),
        out_any=range(5),
        after=(keep_a,),
        us=20,
        mib=56,
    )
    own_a, send_a, own_b, send_b = local_kernel(
        sum_first,
        [
            shape_of(F32, *piece_a),
            shape_of(BF16, *piece_a),
            shape_of(F32, *piece_b),
            shape_of(BF16, *piece_b),
        ],
        [pos, keep_a, got_a, keep_b, got_b],
        after=(own_part,),
    )
    (other_part,) = local_kernel(
        nothing, [], [pos], after=(send_a,), passed=(other_part,), mib=56
    )
    got_a, got_b = swap(send_a, Y_LINK), swap(send_b, X_LINK)
    core_part = swap(other_part, CORE)
    (pair_far,) = local_kernel(
        far_pair,
        [shape_of(BF16, rows, width)],
        [pos, own_far, core_part],
    )
    far_part = swap(pair_far, Y_LINK)
    up_total, p1 = local_kernel(
        sum_second,
        [shape_of(BF16, 4, shard, width + ff)],
        [pos, own_a, got_a, own_b, got_b],
        after=(pair_far,),
        passed=(p1,),
    )
    up_sum = scatter(up_total, along_z).astype(F32)
    grad_out, grad_up = up_sum[:, :width], up_sum[:, width:]
    *head_z, down_first = local_kernel(
        sum_two,
        [shape_of(F32 if z == 0 else BF16, slot_rows, columns) for z in range(4)],
        [pos, p0, swap(p1, X_LINK)],
        passed=(down_first,),
        mib=56,
    )
    (input_grad,) = local_kernel(
        input_back,
        [shape_of(BF16, rows, width)],
        [pos, own_part, core_part, far_part, tokens, d_middle, vectors],
        after=(head_z[0],),
    )
    head_z = [head_z[0]] + [swap(head_z[z], Z_MASKS[z]) for z in range(1, 4)]
    down_plane = [down_first[0]] + [
        swap(down_first[k], PLANE_MASKS[k]) for k in range(1, 4)
    ]
    (grad_down,) = local_kernel(
        sum_four, [shape_of(F32, *w_down.shape)], [pos, *down_plane]
    )
    (head_sum,) = local_kernel(
        sum_four, [shape_of(F32, slot_rows, columns)], [pos, *head_z], after=(input_grad,)
    )
    head_parts = head_sum.reshape(4, shard, columns)
    head_parts = lax.all_to_all(head_parts, "blk", 0, 0)
    grad_qkv, *ends = local_kernel(
        join_heads,
        [shape_of(F32, shard, 3 * width)]
        + [shape_of(F32, 1, shard)] * 6
        + [shape_of(F32, 1, 4 * shard)] * 2,
        [pos, head_parts],
    )
    ends = [value.reshape(-1) for value in ends]
    return (output, input_grad, grad_qkv, grad_out, grad_up, grad_down, *ends)


def layer(*arrays):
    one_document = arrays[2].shape[1] == 1
    if lax.axis_size("dp") == 8 and lax.axis_size("blk") == 4 and one_document:
        return fast_body(*arrays)
    return general_body(*arrays)


def solution(mesh):
    placed = (
        P(("dp", "blk"), None),
        P(("dp", "blk"), None),
        P("dp", None),
        P(("dp", "blk"), None),
        P(("dp", "blk"), None),
        P(("dp", "blk"), None),
        P(("dp", "blk"), None),
        P(("dp", "blk")),
        P(("dp", "blk")),
        P(("dp", "blk")),
        P(("dp", "blk")),
        P(("dp", "blk")),
        P(("dp", "blk")),
        P(("dp", "blk")),
        P(("dp", "blk")),
    )
    return jax.shard_map(
        layer,
        mesh=mesh,
        in_specs=placed,
        out_specs=(
            P(("dp", "blk"), None),
            P(("dp", "blk"), None),
            P(("dp", "blk"), None),
            P(("dp", "blk"), None),
            P(("dp", "blk"), None),
            P(("dp", "blk"), None),
            P(("dp", "blk")),
            P(("dp", "blk")),
            P(("dp", "blk")),
            P(("dp", "blk")),
            P(("dp", "blk")),
            P(("dp", "blk")),
            P(("dp", "blk")),
            P(("dp", "blk")),
        ),
        check_vma=False,
    )
```

```python
import functools
import math

import jax
import jax.numpy as jnp
from jax import lax
from jax.experimental import pallas as pl
from jax.experimental.pallas import tpu as pltpu
from jax.sharding import PartitionSpec as P

HEADS = 12


epsilon = 1e-05
masked_score = -1000000000.0


def shifted(shard, axis, by):
    devices = lax.axis_size(axis)
    pairs = [(i, i + by) for i in range(devices) if 0 <= i + by < devices]
    return lax.ppermute(shard, axis, pairs)


def shifted_2(value, axis, steps):
    count = lax.axis_size(axis)
    pairs = [(source, (source + steps) % count) for source in range(count)]
    return lax.ppermute(value, axis, pairs)


def layer_norm(values, norm_gain, norm_bias):
    centre = jnp.mean(values, -1, keepdims=True)
    centred = values - centre
    spread = jnp.mean(centred * centred, -1, keepdims=True)
    return centred * lax.rsqrt(spread + epsilon) * norm_gain + norm_bias


def ffn_norm(up_value, norm_gain, norm_bias):
    return layer_norm(jax.nn.gelu(up_value, approximate=False), norm_gain, norm_bias)


def doc_place(row_ids, doc_row, row_count, blocks):
    device = row_ids // row_count
    local = row_ids % row_count
    shares = doc_row // blocks
    ends = jnp.cumsum(shares, dtype=jnp.int32)
    starts = ends - shares
    doc = jnp.sum((local[:, None] >= ends[None, :]).astype(jnp.int32), -1, dtype=jnp.int32)
    pick = (doc[:, None] == jnp.arange(doc_row.shape[0], dtype=jnp.int32)[None, :]).astype(
        jnp.int32
    )
    share_of = jnp.sum(pick * shares[None, :], -1, dtype=jnp.int32)
    start_of = jnp.sum(pick * starts[None, :], -1, dtype=jnp.int32)
    return (doc, device * share_of + local - start_of)


def visible(query_doc, query_place, key_doc, key_place):
    return (query_doc[:, None] == key_doc[None, :]) & (key_place[None, :] <= query_place[:, None])


def outer_sum(first_operand, second_operand):
    return lax.dot_general(
        first_operand, second_operand, (((0,), (0,)), ((), ())), preferred_element_type=jnp.float32
    )


def back_product(gradient, weight):
    return lax.dot_general(
        gradient, weight, (((1,), (1,)), ((), ())), preferred_element_type=jnp.float32
    )


def score_grads(
    query_heads, dout_heads, lse_heads, delta_heads, allowed, key_heads, value_heads, score_scale
):
    scores = (
        jnp.einsum("qhd,khd->hqk", query_heads, key_heads, preferred_element_type=jnp.float32)
        * score_scale
    )
    probabilities = jnp.where(allowed[None], jnp.exp(scores - lse_heads[:, :, None]), 0.0)
    weight_grad = jnp.einsum(
        "qhd,khd->hqk", dout_heads, value_heads, preferred_element_type=jnp.float32
    )
    score_grad = (probabilities * (weight_grad - delta_heads[:, :, None])).astype(jnp.bfloat16)
    return (probabilities.astype(jnp.bfloat16), score_grad)


def general_body(
    tokens,
    cotangent,
    doc_lengths,
    w_qkv,
    w_out,
    w_up,
    w_down,
    ln1_gain,
    ln1_bias,
    ln2_gain,
    ln2_bias,
    ln3_gain,
    ln3_bias,
    ln4_gain,
    ln4_bias,
):
    gathered = (
        lax.all_gather(w_qkv, ("dp", "blk"), axis=0, tiled=True),
        lax.all_gather(w_out, ("dp", "blk"), axis=0, tiled=True),
        lax.all_gather(w_up, ("dp", "blk"), axis=0, tiled=True),
        lax.all_gather(w_down, ("dp", "blk"), axis=0, tiled=True),
        lax.all_gather(ln1_gain, ("dp", "blk"), axis=0, tiled=True),
        lax.all_gather(ln1_bias, ("dp", "blk"), axis=0, tiled=True),
        lax.all_gather(ln2_gain, ("dp", "blk"), axis=0, tiled=True),
        lax.all_gather(ln2_bias, ("dp", "blk"), axis=0, tiled=True),
        lax.all_gather(ln3_gain, ("dp", "blk"), axis=0, tiled=True),
        lax.all_gather(ln3_bias, ("dp", "blk"), axis=0, tiled=True),
        lax.all_gather(ln4_gain, ("dp", "blk"), axis=0, tiled=True),
        lax.all_gather(ln4_bias, ("dp", "blk"), axis=0, tiled=True),
    )
    qkv_full, out_full, up_full, down_full = (gathered[0], gathered[1], gathered[2], gathered[3])
    norm_params = [value.astype(jnp.float32) for value in gathered[4:]]
    gain_one, bias_one, gain_two, bias_two, gain_three, bias_three, gain_four, bias_four = (
        norm_params
    )
    row_count, model_width = tokens.shape
    head_dim = model_width // HEADS
    score_scale = head_dim ** (-0.5)
    doc_row = doc_lengths[0]
    blocks = lax.axis_size("blk")
    place_index = lax.axis_index("blk")
    query_doc, query_place = doc_place(
        place_index * row_count + jnp.arange(row_count, dtype=jnp.int32), doc_row, row_count, blocks
    )

    def key_meta(first_row, count):
        return doc_place(first_row + jnp.arange(count, dtype=jnp.int32), doc_row, row_count, blocks)

    residual_in = tokens.astype(jnp.float32)
    normed = layer_norm(residual_in, gain_one, bias_one).astype(jnp.bfloat16)
    projected = jnp.dot(normed, qkv_full, preferred_element_type=jnp.float32).astype(jnp.bfloat16)
    queries = projected[:, :model_width]
    keys_own = projected[:, model_width : 2 * model_width]
    values_own = projected[:, 2 * model_width :]
    query_heads = queries.reshape(row_count, HEADS, head_dim)
    start_state = (
        jnp.full((HEADS, row_count), masked_score, jnp.float32),
        jnp.zeros((HEADS, row_count), jnp.float32),
        jnp.zeros((HEADS, row_count, head_dim), jnp.float32),
    )
    running = start_state
    key_part = lax.all_gather(keys_own, "blk", axis=0, tiled=True)
    value_part = lax.all_gather(values_own, "blk", axis=0, tiled=True)
    part_rows = key_part.shape[0]
    step_rows = math.gcd(part_rows, 512)
    count = part_rows // step_rows

    def one_step(state, element):
        key_block, value_block, block_start = element
        key_doc, key_place = key_meta(block_start, step_rows)
        allowed = visible(query_doc, query_place, key_doc, key_place)
        scores = (
            jnp.einsum(
                "qhd,khd->hqk",
                query_heads,
                key_block.reshape(step_rows, HEADS, head_dim),
                preferred_element_type=jnp.float32,
            )
            * score_scale
        )
        scores = jnp.where(allowed[None], scores, masked_score)
        peak_old, total_old, weighted_old = state
        peak_new = jnp.maximum(peak_old, jnp.max(scores, -1))
        weights = jnp.where(allowed[None], jnp.exp(scores - peak_new[:, :, None]), 0.0)
        factor = jnp.exp(peak_old - peak_new)
        total_new = total_old * factor + jnp.sum(weights, -1)
        weighted_new = weighted_old * factor[:, :, None] + jnp.einsum(
            "hqk,khd->hqd",
            weights.astype(jnp.bfloat16),
            value_block.reshape(step_rows, HEADS, head_dim),
            preferred_element_type=jnp.float32,
        )
        return ((peak_new, total_new, weighted_new), None)

    starts = jnp.arange(count, dtype=jnp.int32) * step_rows
    running, _ = lax.scan(
        one_step,
        running,
        (
            key_part.reshape(count, step_rows, model_width),
            value_part.reshape(count, step_rows, model_width),
            starts,
        ),
    )
    peak_score, total_weight, weighted_sum = running
    log_total = peak_score + jnp.log(total_weight)
    attended = (
        (weighted_sum / total_weight[:, :, None]).transpose(1, 0, 2).reshape(row_count, model_width)
    )
    inner = layer_norm(attended, gain_two, bias_two).astype(jnp.bfloat16)
    middle = residual_in + jnp.dot(inner, out_full, preferred_element_type=jnp.float32)
    normed_two = layer_norm(middle, gain_three, bias_three).astype(jnp.bfloat16)
    up_value = jnp.dot(normed_two, up_full, preferred_element_type=jnp.float32)
    hidden = ffn_norm(up_value, gain_four, bias_four).astype(jnp.bfloat16)
    output = (middle + jnp.dot(hidden, down_full, preferred_element_type=jnp.float32)).astype(
        jnp.bfloat16
    )
    grad_down = outer_sum(hidden, cotangent)
    d_hidden = back_product(cotangent, down_full)
    _, ffn_pullback = jax.vjp(ffn_norm, up_value, gain_four, bias_four)
    d_up, grad_gain_four, grad_bias_four = ffn_pullback(d_hidden)
    d_up_low = d_up.astype(jnp.bfloat16)
    grad_up = outer_sum(normed_two, d_up_low)
    _, third_pullback = jax.vjp(layer_norm, middle, gain_three, bias_three)
    d_middle_norm, grad_gain_three, grad_bias_three = third_pullback(
        back_product(d_up_low, up_full)
    )
    d_middle = cotangent.astype(jnp.float32) + d_middle_norm
    d_middle_low = d_middle.astype(jnp.bfloat16)
    grad_out = outer_sum(inner, d_middle_low)
    _, second_pullback = jax.vjp(layer_norm, attended, gain_two, bias_two)
    d_attended, grad_gain_two, grad_bias_two = second_pullback(back_product(d_middle_low, out_full))
    d_attended_low = d_attended.astype(jnp.bfloat16)
    dout_heads = d_attended_low.reshape(row_count, HEADS, head_dim)
    delta = jnp.einsum(
        "qhd,qhd->hq",
        d_attended_low.astype(jnp.float32).reshape(row_count, HEADS, head_dim),
        attended.reshape(row_count, HEADS, head_dim),
    )

    def turn(turn_index, loop_state):
        kv_now, grads_now, query_grad = loop_state
        source = (place_index - turn_index) % blocks
        key_doc, key_place = key_meta(source * row_count, row_count)
        allowed = visible(query_doc, query_place, key_doc, key_place)
        key_heads = kv_now[0].reshape(row_count, HEADS, head_dim)
        value_heads = kv_now[1].reshape(row_count, HEADS, head_dim)
        probabilities, score_grad = score_grads(
            query_heads, dout_heads, log_total, delta, allowed, key_heads, value_heads, score_scale
        )
        query_grad = (
            query_grad
            + jnp.einsum("hqk,khd->qhd", score_grad, key_heads, preferred_element_type=jnp.float32)
            * score_scale
        )
        key_grad = (
            jnp.einsum("hqk,qhd->khd", score_grad, query_heads, preferred_element_type=jnp.float32)
            * score_scale
        )
        value_grad = jnp.einsum(
            "hqk,qhd->khd", probabilities, dout_heads, preferred_element_type=jnp.float32
        )
        grads_now = grads_now + jnp.stack(
            [key_grad.reshape(row_count, model_width), value_grad.reshape(row_count, model_width)]
        )
        kv_now = shifted(kv_now, "blk", 1)
        grads_now = shifted_2(grads_now.astype(jnp.bfloat16), "blk", 1).astype(grads_now.dtype)
        return (kv_now, grads_now, query_grad)

    loop_start = (
        jnp.stack([keys_own, values_own]),
        jnp.zeros((2, row_count, model_width), jnp.float32),
        jnp.zeros((row_count, HEADS, head_dim), jnp.float32),
    )
    _, kv_grads, query_grad = lax.fori_loop(0, blocks, turn, loop_start)
    key_grad_all = kv_grads[0]
    value_grad_all = kv_grads[1]
    d_projected = jnp.concatenate(
        [query_grad.reshape(row_count, model_width), key_grad_all, value_grad_all], axis=1
    ).astype(jnp.bfloat16)
    grad_qkv = outer_sum(normed, d_projected)
    _, first_pullback = jax.vjp(layer_norm, residual_in, gain_one, bias_one)
    d_input_norm, grad_gain_one, grad_bias_one = first_pullback(back_product(d_projected, qkv_full))
    input_grad = (d_middle + d_input_norm).astype(jnp.bfloat16)
    summed = (
        lax.psum_scatter(grad_qkv, ("dp", "blk"), scatter_dimension=0, tiled=True),
        lax.psum_scatter(grad_out, ("dp", "blk"), scatter_dimension=0, tiled=True),
        lax.psum_scatter(grad_up, ("dp", "blk"), scatter_dimension=0, tiled=True),
        lax.psum_scatter(grad_down, ("dp", "blk"), scatter_dimension=0, tiled=True),
        lax.psum_scatter(grad_gain_one, ("dp", "blk"), scatter_dimension=0, tiled=True),
        lax.psum_scatter(grad_bias_one, ("dp", "blk"), scatter_dimension=0, tiled=True),
        lax.psum_scatter(grad_gain_two, ("dp", "blk"), scatter_dimension=0, tiled=True),
        lax.psum_scatter(grad_bias_two, ("dp", "blk"), scatter_dimension=0, tiled=True),
        lax.psum_scatter(grad_gain_three, ("dp", "blk"), scatter_dimension=0, tiled=True),
        lax.psum_scatter(grad_bias_three, ("dp", "blk"), scatter_dimension=0, tiled=True),
        lax.psum_scatter(grad_gain_four, ("dp", "blk"), scatter_dimension=0, tiled=True),
        lax.psum_scatter(grad_bias_four, ("dp", "blk"), scatter_dimension=0, tiled=True),
    )
    return (output, input_grad) + tuple(summed)


F32 = jnp.float32
BF16 = jnp.bfloat16
CORE, Y_LINK, X_LINK, Z_LINK = 1, 2, 4, 8
Z_MASKS = (0, 8, 16, 24)
PLANE_MASKS = (0, Y_LINK, X_LINK, X_LINK + Y_LINK)


def swap(value, mask):
    devices = lax.axis_size("dp") * lax.axis_size("blk")
    return lax.ppermute(value, ("dp", "blk"), [(i, i ^ mask) for i in range(devices)])


def dot_rows(a, b):
    return lax.dot_general(a, b, (((1,), (0,)), ((), ())), preferred_element_type=F32)


def dot_back(a, b):
    return lax.dot_general(a, b, (((1,), (1,)), ((), ())), preferred_element_type=F32)


def dot_outer(a, b):
    return lax.dot_general(a, b, (((0,), (0,)), ((), ())), preferred_element_type=F32)


def row_stats(values):
    centre = jnp.mean(values, -1, keepdims=True)
    centred = values - centre
    spread = jnp.mean(centred * centred, -1, keepdims=True)
    scale = lax.rsqrt(spread + epsilon)
    return centred * scale, scale


def norm_back(grad_unit, unit, scale):
    first = jnp.mean(grad_unit, -1, keepdims=True)
    second = jnp.mean(grad_unit * unit, -1, keepdims=True)
    return scale * (grad_unit - first - unit * second)


def run_copies(copies):
    for copy in copies:
        copy.start()


def wait_copies(copies):
    for copy in copies:
        copy.wait()


def spread_wide(columns, width):
    quarter = width // 32
    run = 4 * quarter
    place = lax.broadcasted_iota(jnp.int32, (run, 4 * run), 1)
    row = lax.broadcasted_iota(jnp.int32, (run, 4 * run), 0)
    lines = []
    for first in (0, 4):
        pieces = []
        for m in range(8):
            piece = 0.0
            for c in range(4):
                want = (row // quarter) * run + c * quarter + row % quarter
                put = (place == want).astype(BF16)
                got = dot_outer(columns[m * run : (m + 1) * run, first : first + 8], put)
                piece = piece + got[c : c + 1]
            pieces.append(piece)
        lines.append(jnp.concatenate(pieces, axis=1))
    return jnp.concatenate(lines, axis=0)


def fold_heads(value):
    rows = value.shape[0] // 2
    last = jnp.concatenate([value[:rows, 128:], value[rows:, 128:]], axis=1)
    return jnp.concatenate([value[:, :128], last], axis=0)


def unfold_heads(value):
    rows = value.shape[0] // 3
    last = value[2 * rows :]
    last = jnp.concatenate([last[:, :64], last[:, 64:]], axis=0)
    return jnp.concatenate([value[: 2 * rows], last], axis=1)


def attention_forward(
    pos, t0, t1, t2, t3, own, other, normed, units, proj, weight, vectors, wide, att, mixed_out, stats
):
    rows, width = t0.shape
    slot_rows = own.shape[1]
    head_dim = width // HEADS
    span = mixed_out.shape[1]
    heads = span // head_dim
    blk = pos[1]
    for x, source in enumerate((own, other)):
        for z in range(4):
            slot = 2 * z + (pos[0] % 2 ^ x)
            at = pl.ds(pl.multiple_of(slot * slot_rows, slot_rows), slot_rows)
            weight[at, :] = source[z]
    tail = (3 * span // 128) * 128
    first = 3 * span - tail
    turned = jnp.transpose(weight[:, tail:].astype(F32))
    vectors[...] = turned[first : first + 8, :]
    wide[...] = spread_wide(weight[:, tail + first + 6 : tail + first + 22], width)
    gain, bias = vectors[0:1, :], vectors[1:2, :]
    for k, source in enumerate((t0, t1, t2, t3)):
        unit, _ = row_stats(source[...].astype(F32))
        at = pl.ds(pl.multiple_of((blk ^ k) * rows, rows), rows)
        value = (unit * gain + bias).astype(BF16)
        normed[at, :] = value
        units[at, :] = unit.astype(BF16)
        proj[at, :] = dot_rows(value, weight[...]).astype(BF16)
    scale = head_dim ** (-0.5)
    below = lax.broadcasted_iota(jnp.int32, (rows, rows), 1) <= lax.broadcasted_iota(
        jnp.int32, (rows, rows), 0
    )
    lane = lax.broadcasted_iota(jnp.int32, (rows, 128), 1)
    for block in range(4):
        mixed = []
        low, high = block * rows, (block + 1) * rows
        stat = jnp.zeros((rows, 128), F32)
        for head in range(heads):
            q = proj[low:high, head * head_dim : (head + 1) * head_dim] * BF16(scale)
            k = proj[:high, span + head * head_dim : span + (head + 1) * head_dim]
            v = proj[:high, 2 * span + head * head_dim : 2 * span + (head + 1) * head_dim]
            own = jnp.where(below, dot_back(q, k[low:]), masked_score)
            peak = jnp.max(own, -1, keepdims=True)
            if block:
                past = dot_back(q, k[:low])
                peak = jnp.maximum(peak, jnp.max(past, -1, keepdims=True))
            own = jnp.exp(own - peak)
            total = jnp.sum(own, -1, keepdims=True)
            mix = dot_rows(own.astype(BF16), v[low:])
            if block:
                past = jnp.exp(past - peak)
                total = total + jnp.sum(past, -1, keepdims=True)
                mix = mix + dot_rows(past.astype(BF16), v[:low])
            mixed.append(mix / total)
            stat = jnp.where(lane == head, peak + jnp.log(total), stat)
        stats[low:high, :] = stat
        value = jnp.concatenate(mixed, axis=1)
        mixed_out[low:high, :] = value
        att[block] = fold_heads(value.astype(BF16))


def ffn_forward(
    pos, att, tokens, vectors, wide_gains, weights,
    hidden, acts, middle, unit_four, slope, scale_four,
    w_out, w_up, up, sems,
):
    rows, width = tokens.shape
    copies = [
        pltpu.make_async_copy(weights.at[:, pl.ds(0, width)], w_out, sems.at[0]),
        pltpu.make_async_copy(weights.at[:, pl.ds(width, w_up.shape[1])], w_up, sems.at[1]),
    ]
    run_copies(copies)
    attended = jnp.concatenate([unfold_heads(att[j]) for j in range(4)], axis=1).astype(F32)
    unit, _ = row_stats(attended)
    inner_low = (unit * vectors[2:3, :] + vectors[3:4, :]).astype(BF16)
    acts[:, width:] = inner_low
    copies[0].wait()
    mid = tokens[...].astype(F32) + dot_rows(inner_low, w_out[...])
    middle[...] = mid
    unit, _ = row_stats(mid)
    low = (unit * vectors[4:5, :] + vectors[5:6, :]).astype(BF16)
    acts[:, :width] = low
    copies[1].wait()
    up[...] = dot_rows(low, w_up[...])
    step = 64
    gain, bias = wide_gains[0:1, :], wide_gains[1:2, :]

    def chunk(i, carry):
        at = pl.ds(pl.multiple_of(i * step, step), step)
        value = up[at, :]
        gate = 0.5 * (1.0 + lax.erf(value * (2.0**-0.5)))
        slope[at, :] = (gate + value * jnp.exp(-0.5 * value * value) * (0.5 / math.pi) ** 0.5).astype(
            BF16
        )
        unit, scale = row_stats(value * gate)
        unit_four[at, :] = unit.astype(BF16)
        hidden[at, :] = (unit * gain + bias).astype(BF16)
        scale_four[at, :] = jnp.broadcast_to(scale, (step, 128))
        return carry

    lax.fori_loop(0, rows // step, chunk, 0, unroll=True)


def down_copies(pos, stacks, target, sems):
    rows = stacks[0].shape[1]
    plane = 2 * (pos[0] % 2) + pos[1] // 2
    copies = []
    for other in range(2):
        for mask in range(4):
            for z in range(4):
                slot = 2 * (4 * z + (plane ^ mask)) + (pos[1] % 2 ^ other)
                copies.append(
                    pltpu.make_async_copy(
                        stacks[other * 4 + mask].at[z],
                        target.at[pl.ds(pl.multiple_of(slot * rows, rows), rows)],
                        sems.at[len(copies)],
                    )
                )
    return copies


def fold(value):
    total = value[:, :128]
    for start in range(128, value.shape[1], 128):
        total = total + value[:, start : start + 128]
    return total


def ffn_backward(
    pos, att, cot, vectors, wide_gains, middle, hidden_far, unit_four, slope, scale_four, weights,
    s0, s1, s2, s3, s4, s5, s6, s7,
    output, grads, d_middle, d0, d1, d2, d3, vector_grads, wide_grads,
    w_down, w_out, w_up, hidden, units, slopes, d_hidden, sems,
):
    rows, width = cot.shape
    wide = w_up.shape[1]
    copies = down_copies(pos, (s0, s1, s2, s3, s4, s5, s6, s7), w_down, sems)
    later = []
    for source, target in (
        (unit_four, units),
        (hidden_far, hidden),
        (slope, slopes),
        (weights.at[:, pl.ds(width, wide)], w_up),
        (weights.at[:, pl.ds(0, width)], w_out),
    ):
        later.append(pltpu.make_async_copy(source, target, sems.at[len(copies) + len(later)]))
    by_z = [copies[q::4] for q in range(4)]
    run_copies(by_z[0] + later[:1] + by_z[1] + later[1:2] + by_z[2] + by_z[3] + later[2:])

    def first_grad(q):
        wait_copies(by_z[q] + later[: 2 if q == 0 else 0])
        return dot_back(cot[...], w_down[q * width : (q + 1) * width, :])

    def fold_rows(value):
        total = value[:8]
        for start in range(8, rows, 8):
            total = total + value[start : start + 8]
        return jnp.sum(total, 0, keepdims=True)

    current = first_grad(0)
    first = jnp.zeros((rows, 128), F32)
    second = jnp.zeros((rows, 128), F32)
    out = middle[...]
    for q in range(4):
        at = slice(q * width, (q + 1) * width)
        if q < 3:
            following = first_grad(q + 1)
        out = out + dot_rows(hidden[:, at], w_down[at, :])
        d_hidden[:, at] = current
        unit = units[:, at].astype(F32)
        part = current * unit
        wide_grads[0:1, at] = fold_rows(part)
        wide_grads[1:2, at] = fold_rows(current)
        gain = wide_gains[0:1, at]
        first = first + fold(current * gain)
        second = second + fold(part * gain)
        current = following
    output[...] = out.astype(BF16)
    first = jnp.sum(first, -1, keepdims=True) * (1.0 / wide)
    second = jnp.sum(second, -1, keepdims=True) * (1.0 / wide)
    scale = scale_four[:, 0:1]
    wait_copies(later[2:])

    def second_grad(q):
        at = slice(q * width, (q + 1) * width)
        grad = d_hidden[:, at] * wide_gains[0:1, at] - first - units[:, at].astype(F32) * second
        grad = (scale * grad * slopes[:, at].astype(F32)).astype(BF16)
        grads[:, at] = grad
        return grad

    d_normed = 0.0
    for q in range(4):
        d_normed = d_normed + dot_back(second_grad(q), w_up[:, q * width : (q + 1) * width])
    unit, scale = row_stats(middle[...])
    gain_three = jnp.sum(d_normed * unit, 0, keepdims=True)
    bias_three = jnp.sum(d_normed, 0, keepdims=True)
    d_mid = cot[...].astype(F32) + norm_back(d_normed * vectors[4:5, :], unit, scale)
    d_middle[...] = d_mid
    d_mid_low = d_mid.astype(BF16)
    grads[:, wide:] = d_mid_low
    d_inner = dot_back(d_mid_low, w_out[...])
    attended = jnp.concatenate([unfold_heads(att[j]) for j in range(4)], axis=1).astype(F32)
    unit, scale = row_stats(attended)
    gain_two = jnp.sum(d_inner * unit, 0, keepdims=True)
    bias_two = jnp.sum(d_inner, 0, keepdims=True)
    vector_grads[...] = jnp.concatenate(
        [gain_two, bias_two, gain_three, bias_three, jnp.zeros((4, width), F32)], axis=0
    )
    back = norm_back(d_inner * vectors[2:3, :], unit, scale).astype(BF16)
    span = width // 4
    parts = [back[:, j * span : (j + 1) * span] for j in range(4)]
    for k, target in enumerate((d0, d1, d2, d3)):
        value = parts[k]
        for j in range(4):
            if j != k:
                value = jnp.where((pos[1] ^ k) == j, parts[j], value)
        target[...] = fold_heads(value)


def piece_copies(pos, held, targets, sems, zs):
    chip = pos[0] * 2 + pos[1] // 2
    copies = []
    for start, masks, target in targets:
        for i, plane in enumerate(masks):
            for z in zs:
                slot = ((chip ^ plane) & 3) + 4 * z
                copies.append(
                    pltpu.make_async_copy(
                        held.at[slot, :, pl.ds(start, target.shape[3])],
                        target.at[i, z],
                        sems.at[len(copies)],
                    )
                )
    return copies


def down_grads(pos, hidden, cot, mine_far, theirs_far, mine, theirs, sems):
    rows = mine.shape[2]
    plane = 2 * (pos[0] % 2) + pos[1] // 2
    first = pos[1] % 2 == 0
    copies = []
    for pair in range(hidden.shape[1] // (4 * rows)):
        value = dot_outer(hidden[:, 4 * rows * pair : 4 * rows * (pair + 1)], cot[...]).astype(BF16)
        for i in range(2):
            chip = 2 * pair + i
            low, high = value[2 * i * rows : (2 * i + 1) * rows], value[(2 * i + 1) * rows : (2 * i + 2) * rows]
            mine[chip // 4, (chip % 4) ^ plane] = jnp.where(first, low, high)
            theirs[chip // 4, (chip % 4) ^ plane] = jnp.where(first, high, low)
        if pair % 2:
            z = pair // 2
            for k, (source, target) in enumerate(((mine, mine_far), (theirs, theirs_far))):
                copies.append(pltpu.make_async_copy(source.at[z], target.at[z], sems.at[k, z]))
                copies[-1].start()
    wait_copies(copies)


def up_grads(
    pos, acts, acts_other, g0, g1, down_mine, down_got,
    keep_a, send_a, keep_b, send_b, down_grad,
    held, left, right, chosen, down, out_sems, sems,
):
    rows = held.shape[1]
    core = pos[1] % 2
    width = acts.shape[1] // 2
    wide = 4 * width
    copies = []

    def load(source, target):
        copies.append(pltpu.make_async_copy(source, target, sems.at[len(copies)]))
        copies[-1].start()

    for i, source in enumerate((acts, acts_other)):
        load(source, left.at[i])
    for i, source in enumerate((g0, g1)):
        load(source, right.at[i])
    for i, source in enumerate((down_mine, down_got)):
        load(source, down.at[i])
    row = lax.broadcasted_iota(jnp.int32, (width, width // 2), 0)
    column = lax.broadcasted_iota(jnp.int32, (width, width // 2), 1)
    take = (row // rows == 2 * (column // rows) + core) & (row % rows == column % rows)
    take = take.astype(BF16)
    wait_copies(copies[:2])
    for i in range(2):
        for part in range(2):
            at = slice(part * width // 2, (part + 1) * width // 2)
            chosen[i, :, at] = dot_rows(
                left[i, :, part * width : (part + 1) * width], take
            ).astype(BF16)
    cut = keep_a.shape[3]
    pieces = ((0, (0, 1), keep_a), (0, (2, 3), send_a), (cut, (0, 2), keep_b), (cut, (1, 3), send_b))
    tile = 384
    wait_copies(copies[2:4])
    outs = []
    for c in range(0, wide + width, tile):
        from_up = c >= width
        source = c - width if from_up else wide + c
        first = 0 if from_up else width // 2
        value = 0.0
        for i in range(2):
            value = value + dot_outer(
                chosen[i, :, first : first + width // 2], right[i, :, source : source + tile]
            )
        for chip in range(16):
            held[chip, :, c : c + tile] = value[chip * rows : (chip + 1) * rows].astype(BF16)
        if c + tile == cut or c + tile == wide + width:
            part = len(outs)
            outs.append(
                piece_copies(pos, held, pieces[2 * part : 2 * part + 2], out_sems.at[part], range(4))
            )
            run_copies(outs[-1])
    wait_copies(copies[4:])
    for z in range(down.shape[1]):
        down[0, z] = down[0, z] + down[1, z]
    outs.append([pltpu.make_async_copy(down.at[0], down_grad, sems.at[0])])
    run_copies(outs[-1])
    for group in outs:
        wait_copies(group)


def gather_wide(grads, width):
    quarter = width // 32
    run = 4 * quarter
    place = lax.broadcasted_iota(jnp.int32, (run, 4 * run), 1)
    row = lax.broadcasted_iota(jnp.int32, (run, 4 * run), 0)
    lane = lax.broadcasted_iota(jnp.int32, (run, 128), 1)
    rows = jnp.concatenate([grads, jnp.zeros((126, grads.shape[1]), F32)], axis=0).astype(BF16)
    pieces = []
    for m in range(8):
        piece = jnp.zeros((run, 128), F32)
        for c in range(4):
            want = (row // quarter) * run + c * quarter + row % quarter
            put = (place == want).astype(BF16)
            got = dot_back(put, rows[:, m * 4 * run : (m + 1) * 4 * run])
            for v in range(2):
                piece = piece + jnp.where(lane == 6 + 4 * v + c, got[:, v : v + 1], 0.0)
        pieces.append(piece)
    return jnp.concatenate(pieces, axis=0)


def attention_backward(
    pos, d0, d1, d2, d3, normed_far, units_far, proj, weight_far, mixed, stats, vector_grads,
    wide_grads,
    own, own_far, other, p0, p1,
    d_out, d_proj, tt, held, d_normed, normed, units, weight, load_sems, sems,
):
    rows, width = d0.shape[0] * 2 // 3, normed.shape[1]
    loads = [
        pltpu.make_async_copy(source, target, load_sems.at[i])
        for i, (source, target) in enumerate(
            ((weight_far, weight), (units_far, units), (normed_far, normed))
        )
    ]
    run_copies(loads)
    head_dim = width // HEADS
    span = d_out.shape[1]
    heads = span // head_dim
    dp, blk = pos[0], pos[1]
    for k, source in enumerate((d0, d1, d2, d3)):
        d_out[pl.ds(pl.multiple_of((blk ^ k) * rows, rows), rows), :] = unfold_heads(source[...])
    scale = head_dim ** (-0.5)
    below = lax.broadcasted_iota(jnp.int32, (rows, rows), 1) <= lax.broadcasted_iota(
        jnp.int32, (rows, rows), 0
    )
    for head in range(heads):
        at_q = slice(head * head_dim, (head + 1) * head_dim)
        at_k = slice(span + head * head_dim, span + (head + 1) * head_dim)
        at_v = slice(2 * span + head * head_dim, 2 * span + (head + 1) * head_dim)
        tt[...] = jnp.zeros_like(tt)
        for block in range(4):
            low, high = block * rows, (block + 1) * rows
            q = proj[low:high, at_q] * BF16(scale)
            d = d_out[low:high, at_q]
            log_total = stats[low:high, head : head + 1]
            delta = jnp.sum(d.astype(F32) * mixed[low:high, at_q], -1, keepdims=True)
            d_query = 0.0
            for start, end in [(low, high)] + ([(0, low)] if block else []):
                score = dot_back(q, proj[start:end, at_k])
                if start == low:
                    score = jnp.where(below, score, masked_score)
                score = jnp.exp(score - log_total)
                grad = dot_back(d, proj[start:end, at_v])
                d_score = (score * (grad - delta)).astype(BF16)
                d_query = d_query + dot_rows(d_score, proj[start:end, at_k])
                tt[0, :, start:end] += dot_outer(q, d_score)
                tt[1, :, start:end] += dot_outer(d, score.astype(BF16))
            d_proj[low:high, at_q] = (d_query * scale).astype(BF16)
        d_proj[:, at_k] = jnp.transpose(tt[0]).astype(BF16)
        d_proj[:, at_v] = jnp.transpose(tt[1]).astype(BF16)
    columns = weight.shape[1]
    vector_sums = []
    wait_copies(loads[:2])
    for j in range(4):
        at = slice(j * rows, (j + 1) * rows)
        grad = dot_back(d_proj[at, :], weight[:, : 3 * span])
        unit = units[at, :].astype(F32)
        vector_sums.append((jnp.sum(grad * unit, 0, keepdims=True), jnp.sum(grad, 0, keepdims=True)))
        d_normed[j ^ blk] = grad.astype(BF16)
    copies = [
        pltpu.make_async_copy(d_normed.at[k], target, sems.at[8 + k])
        for k, target in enumerate((own, other.at[0], own_far, other.at[1]))
    ]
    run_copies(copies)
    loads[2].wait()
    sums = [sum(v[i] for v in vector_sums) for i in range(2)]
    turned = jnp.transpose(
        jnp.concatenate(
            sums + [vector_grads[0:4, :], jnp.zeros((128 - 6, width), F32)], axis=0
        )
    ) + gather_wide(wide_grads[...], width)
    slot_rows = held.shape[1]
    for r in range(0, width, 2 * slot_rows):
        value = dot_outer(normed[:, r : r + 2 * slot_rows], d_proj[...])
        value = jnp.concatenate(
            [value, turned[r : r + 2 * slot_rows, : columns - 3 * span]], axis=1
        ).astype(BF16)
        held[r // slot_rows] = value[:slot_rows]
        held[r // slot_rows + 1] = value[slot_rows:]
    pieces = []
    for x, target in enumerate((p0, p1)):
        for z in range(4):
            slot = ((dp ^ x) & 1) + 2 * z
            pieces.append(pltpu.make_async_copy(held.at[slot], target.at[z], sems.at[x * 4 + z]))
    run_copies(pieces)
    wait_copies(copies + pieces)


def local_kernel(kernel, outs, ins, scratch=(), us=2, in_any=(), out_any=(), after=(), passed=(), mib=16):
    here = pl.BlockSpec(memory_space=pltpu.VMEM)
    far = pl.BlockSpec(memory_space=pl.ANY)
    specs = [pl.BlockSpec(memory_space=pltpu.SMEM)]
    specs += [far if i in in_any else here for i in range(1, len(ins))]
    specs += [far] * (len(after) + len(passed))
    unread = len(ins) + len(after) + len(passed)
    ends = unread + len(outs)

    def run(*refs):
        kernel(*refs[: len(ins)], *refs[unread:ends], *refs[ends + len(passed) :])

    return pl.pallas_call(
        run,
        out_shape=[*outs, *(shape_of(v.dtype, *v.shape) for v in passed)],
        in_specs=specs,
        out_specs=[far if i in out_any else here for i in range(len(outs))] + [far] * len(passed),
        input_output_aliases={
            len(ins) + len(after) + i: len(outs) + i for i in range(len(passed))
        },
        scratch_shapes=list(scratch),
        compiler_params=pltpu.CompilerParams(vmem_limit_bytes=mib * 1024 * 1024),
        cost_estimate=pl.CostEstimate(
            flops=int(us * 1.15e9) // 100, bytes_accessed=int(us * 3.6e6) // 100, transcendentals=0
        ),
    )(*ins, *after, *passed)


def shape_of(dtype, *shape):
    return jax.ShapeDtypeStruct(shape, dtype)


def z_exchange(own):
    return [own] + [swap(own, mask) for mask in Z_MASKS[1:]]


def pack_weights(
    pos, w_qkv, w_out, w_up, gains, wide_gains, packed, slices
):
    rows, width = w_out.shape
    span = width // 4
    packed[:, :width] = w_out[...]
    packed[:, width:] = w_up[...]
    wide = wide_gains[...].astype(F32)
    lines = [gains[...].astype(F32)] + [
        wide[i : i + 1, c * rows : (c + 1) * rows] for i in range(2) for c in range(4)
    ]
    square = jnp.concatenate(lines + [jnp.zeros((128 - 14, rows), F32)], axis=0)
    square = jnp.concatenate([square, jnp.zeros((128, 128 - rows), F32)], axis=1)
    ends = jnp.transpose(square)[:rows, : slices.shape[2] - 3 * span].astype(BF16)
    for j in range(4):
        parts = [w_qkv[:, p * width + j * span : p * width + (j + 1) * span] for p in range(3)]
        slices[j] = jnp.concatenate(parts + [ends], axis=1)

def stack_z(pos, b0, b1, b2, b3, target):
    for k, part in enumerate((b0, b1, b2, b3)):
        target[(pos[0] // 2) ^ k] = part[...]


def nothing(pos):
    pass


def sum_first(pos, keep_a, got_a, keep_b, got_b, own_a, send_a, own_b, send_b):
    for keep, got, own, send in ((keep_a, got_a, own_a, send_a), (keep_b, got_b, own_b, send_b)):
        own[...] = keep[0].astype(F32) + got[0].astype(F32)
        send[...] = (keep[1].astype(F32) + got[1].astype(F32)).astype(BF16)


def sum_second(pos, own_a, got_a, own_b, got_b, total):
    cut = own_a.shape[2]
    total[:, :, :cut] = (own_a[...] + got_a[...].astype(F32)).astype(BF16)
    total[:, :, cut:] = (own_b[...] + got_b[...].astype(F32)).astype(BF16)


def sum_two(pos, p0, p1, z0, z1, z2, z3):
    for k, target in enumerate((z0, z1, z2, z3)):
        at = (pos[0] // 2) ^ k
        target[...] = (p0[at].astype(F32) + p1[at].astype(F32)).astype(target.dtype)


def join_heads(pos, parts, grad, e0, e1, e2, e3, e4, e5, e6, e7):
    width = grad.shape[1] // 3
    span = width // 4
    rows = grad.shape[0]
    for j in range(4):
        for p in range(3):
            grad[:, p * width + j * span : p * width + (j + 1) * span] = parts[
                j, :, p * span : (p + 1) * span
            ]
    tail = (3 * span // 128) * 128
    last = (parts[0] + parts[1]) + (parts[2] + parts[3])
    square = jnp.concatenate([last[:, tail:], jnp.zeros((128 - rows, 128), F32)], axis=0)
    ends = jnp.transpose(square)[3 * span - tail : 3 * span - tail + 16]
    for i, target in enumerate((e0, e1, e2, e3, e4, e5)):
        target[...] = ends[i : i + 1, :rows]
    for i, target in enumerate((e6, e7)):
        first = 6 + 4 * i
        target[...] = jnp.concatenate(
            [ends[first + c : first + c + 1, :rows] for c in range(4)], axis=1
        )


def far_pair(pos, own, core_part, target):
    target[...] = (own[...].astype(F32) + core_part[1].astype(F32)).astype(BF16)


def sum_four(pos, p0, p1, p2, p3, total):
    total[...] = (p0[...].astype(F32) + p1[...].astype(F32)) + (
        p2[...].astype(F32) + p3[...].astype(F32)
    )


def input_back(pos, own, core_part, far, tokens, d_middle, vectors, input_grad):
    grad = own[...].astype(F32) + core_part[0].astype(F32) + far[...].astype(F32)
    unit, scale = row_stats(tokens[...].astype(F32))
    input_grad[...] = (d_middle[...] + norm_back(grad * vectors[0:1, :], unit, scale)).astype(BF16)


def groups_of(fixed):
    numbers = range(lax.axis_size("dp") * lax.axis_size("blk"))
    return [[i for i in numbers if i & fixed == j] for j in numbers if j & fixed == j]


def fast_body(
    tokens, cotangent, doc_lengths, w_qkv, w_out, w_up, w_down,
    ln1_gain, ln1_bias, ln2_gain, ln2_bias, ln3_gain, ln3_bias, ln4_gain, ln4_bias,
):
    rows, width = tokens.shape
    shard = w_qkv.shape[0]
    ff = w_up.shape[1]
    head_dim = width // HEADS
    span = width // 4
    group = rows * 4
    columns = -(-(3 * span + 16) // 128) * 128
    slot_rows = 4 * shard
    both = ("dp", "blk")
    along_z = groups_of(CORE + Y_LINK + X_LINK)
    in_plane = groups_of(CORE + 3 * Z_LINK)
    dp, blk = lax.axis_index("dp"), lax.axis_index("blk")
    pos = jnp.stack([dp, blk]).astype(jnp.int32)

    def gather(value, groups):
        return lax.all_gather(value, both, axis=0, axis_index_groups=groups)

    def scatter(value, groups):
        return lax.psum_scatter(
            value, both, scatter_dimension=0, axis_index_groups=groups, tiled=False
        )

    norms = [ln1_gain, ln1_bias, ln2_gain, ln2_bias, ln3_gain, ln3_bias]
    gains = jnp.stack(norms)
    wide_gains = jnp.stack([ln4_gain, ln4_bias])
    packed, slices = local_kernel(
        pack_weights,
        [shape_of(BF16, shard, width + ff), shape_of(BF16, 4, shard, columns)],
        [pos, w_qkv, w_out, w_up, gains, wide_gains],
        mib=56,
    )
    weights = lax.all_gather(packed, both, axis=0, tiled=True)

    token_y = swap(tokens, Y_LINK)

    slices = lax.all_to_all(slices, "blk", 0, 0).reshape(slot_rows, columns)
    down_own, slices = local_kernel(
        stack_z,
        [shape_of(BF16, 4, *w_down.shape)],
        [pos, w_down] + [swap(w_down, mask) for mask in Z_MASKS[1:]],
        after=(token_y,),
        passed=(slices,),
    )
    slices, down_own, down_x, down_y = local_kernel(
        stack_z,
        [shape_of(BF16, 4, slot_rows, columns)],
        [pos, slices] + [swap(slices, mask) for mask in Z_MASKS[1:]],
        passed=(down_own, swap(down_own, X_LINK), swap(down_own, Y_LINK)),
    )
    down_parts = [down_own, down_y, down_x, swap(down_x, Y_LINK)]
    token_core, token_both = swap(tokens, CORE), swap(token_y, CORE)
    slices_x = swap(slices, X_LINK)

    tokens_group = [tokens, token_core, token_y, token_both]
    packed_rows = rows * 3 // 2
    normed, units, proj, weight, vectors, wide, att, mixed, stats = local_kernel(
        attention_forward,
        [
            shape_of(BF16, group, width),
            shape_of(BF16, group, width),
            shape_of(BF16, group, columns),
            shape_of(BF16, width, columns),
            shape_of(F32, 8, width),
            shape_of(F32, 2, ff),
            shape_of(BF16, 4, packed_rows, 128),
            shape_of(F32, group, span),
            shape_of(F32, group, 128),
        ],
        [pos, *tokens_group, slices, slices_x],
        us=11,
        mib=56,
    )
    att = lax.all_to_all(att, "blk", 0, 0)
    down_all = down_parts + [swap(value, CORE) for value in down_parts]
    hidden, acts, middle, unit_four, slope, scale_four = local_kernel(
        ffn_forward,
        [
            shape_of(BF16, rows, ff),
            shape_of(BF16, rows, 2 * width),
            shape_of(F32, rows, width),
            shape_of(BF16, rows, ff),
            shape_of(BF16, rows, ff),
            shape_of(F32, rows, 128),
        ],
        [pos, att, tokens, vectors, wide, weights],
        [
            pltpu.VMEM((width, width), BF16),
            pltpu.VMEM((width, ff), BF16),
            pltpu.VMEM((rows, ff), F32),
            pltpu.SemaphoreType.DMA((2,)),
        ],
        in_any=(5,),
        us=12,
        mib=56,
    )
    down_mine, down_theirs = local_kernel(
        down_grads,
        [shape_of(BF16, 4, 4, *w_down.shape)] * 2,
        [pos, hidden, cotangent],
        [pltpu.VMEM((4, 4, *w_down.shape), BF16)] * 2 + [pltpu.SemaphoreType.DMA((2, 4))],
        out_any=(0, 1),
        us=5,
        mib=56,
    )
    acts_other = swap(acts, CORE)
    output, grads, d_middle, d0, d1, d2, d3, vector_grads, wide_grads, down_theirs = local_kernel(
        ffn_backward,
        [
            shape_of(BF16, rows, width),
            shape_of(BF16, rows, ff + width),
            shape_of(F32, rows, width),
            *[shape_of(BF16, packed_rows, 128)] * 4,
            shape_of(F32, 8, width),
            shape_of(F32, 2, ff),
        ],
        [
            pos, att, cotangent, vectors, wide, middle, hidden, unit_four, slope, scale_four,
            weights, *down_all,
        ],
        [
            pltpu.VMEM((ff, width), BF16),
            pltpu.VMEM((width, width), BF16),
            pltpu.VMEM((width, ff), BF16),
            pltpu.VMEM((rows, ff), BF16),
            pltpu.VMEM((rows, ff), BF16),
            pltpu.VMEM((rows, ff), BF16),
            pltpu.VMEM((rows, ff), F32),
            pltpu.SemaphoreType.DMA((37,)),
        ],
        in_any=(6, 7, 8, *range(10, 19)),
        us=15,
        after=(down_mine, acts_other),
        passed=(down_theirs,),
        mib=56,
    )
    d_att = [d0] + [swap(value, k) for k, value in ((1, d1), (2, d2), (3, d3))]
    grads_other, down_got = swap(grads, CORE), swap(down_theirs, CORE)
    a_columns = -(-(width + ff) // (2 * 384)) * 384
    piece_a = (4, shard, a_columns)
    piece_b = (4, shard, width + ff - a_columns)
    keep_a, send_a, keep_b, send_b, down_grad = local_kernel(
        up_grads,
        [shape_of(BF16, 2, *piece_a)] * 2
        + [shape_of(BF16, 2, *piece_b)] * 2
        + [shape_of(BF16, *down_mine.shape)],
        [pos, acts, acts_other, grads, grads_other, down_mine, down_got],
        [
            pltpu.VMEM((16, shard, width + ff), BF16),
            pltpu.VMEM((2, rows, 2 * width), BF16),
            pltpu.VMEM((2, rows, width + ff), BF16),
            pltpu.VMEM((2, rows, width), BF16),
            pltpu.VMEM((2, *down_mine.shape), BF16),
            pltpu.SemaphoreType.DMA((2, 16)),
            pltpu.SemaphoreType.DMA((6,)),
        ],
        in_any=range(1, 7),
        out_any=range(5),
        after=d_att[1:],
        mib=56,
    )
    down_first = scatter(down_grad, along_z)
    got_a, got_b = swap(send_a, X_LINK), swap(send_b, Y_LINK)

    def total_of(pieces):
        return sum(piece.astype(F32) for piece in pieces)

    own_part, own_far, other_part, p0, p1 = local_kernel(
        attention_backward,
        [shape_of(BF16, rows, width)] * 2
        + [shape_of(BF16, 2, rows, width)]
        + [shape_of(BF16, 4, slot_rows, columns)] * 2,
        [
            pos, *d_att, normed, units, proj, weight, mixed, stats, vector_grads, wide_grads
        ],
        [
            pltpu.VMEM((group, span), BF16),
            pltpu.VMEM((group, 3 * span), BF16),
            pltpu.VMEM((2, head_dim, group), F32),
            pltpu.VMEM((8, slot_rows, columns), BF16),
            pltpu.VMEM((4, rows, width), BF16),
            pltpu.VMEM((group, width), BF16),
            pltpu.VMEM((group, width), BF16),
            pltpu.VMEM((width, columns), BF16),
            pltpu.SemaphoreType.DMA((3,)),
            pltpu.SemaphoreType.DMA((12,)),
        ],
        in_any=(5, 6, 8),
        out_any=range(5),
        after=(keep_a,),
        us=20,
        mib=56,
    )
    own_a, send_a, own_b, send_b = local_kernel(
        sum_first,
        [
            shape_of(F32, *piece_a),
            shape_of(BF16, *piece_a),
            shape_of(F32, *piece_b),
            shape_of(BF16, *piece_b),
        ],
        [pos, keep_a, got_a, keep_b, got_b],
        after=(own_part,),
    )
    (other_part,) = local_kernel(
        nothing, [], [pos], after=(send_a,), passed=(other_part,), mib=56
    )
    got_a, got_b = swap(send_a, Y_LINK), swap(send_b, X_LINK)
    core_part = swap(other_part, CORE)
    (pair_far,) = local_kernel(
        far_pair,
        [shape_of(BF16, rows, width)],
        [pos, own_far, core_part],
    )
    far_part = swap(pair_far, Y_LINK)
    up_total, p1 = local_kernel(
        sum_second,
        [shape_of(BF16, 4, shard, width + ff)],
        [pos, own_a, got_a, own_b, got_b],
        after=(pair_far,),
        passed=(p1,),
    )
    up_sum = scatter(up_total, along_z).astype(F32)
    grad_out, grad_up = up_sum[:, :width], up_sum[:, width:]
    *head_z, down_first = local_kernel(
        sum_two,
        [shape_of(F32 if z == 0 else BF16, slot_rows, columns) for z in range(4)],
        [pos, p0, swap(p1, X_LINK)],
        passed=(down_first,),
        mib=56,
    )
    (input_grad,) = local_kernel(
        input_back,
        [shape_of(BF16, rows, width)],
        [pos, own_part, core_part, far_part, tokens, d_middle, vectors],
        after=(head_z[0],),
    )
    head_z = [head_z[0]] + [swap(head_z[z], Z_MASKS[z]) for z in range(1, 4)]
    down_plane = [down_first[0]] + [
        swap(down_first[k], PLANE_MASKS[k]) for k in range(1, 4)
    ]
    (grad_down,) = local_kernel(
        sum_four, [shape_of(F32, *w_down.shape)], [pos, *down_plane]
    )
    (head_sum,) = local_kernel(
        sum_four, [shape_of(F32, slot_rows, columns)], [pos, *head_z], after=(input_grad,)
    )
    head_parts = head_sum.reshape(4, shard, columns)
    head_parts = lax.all_to_all(head_parts, "blk", 0, 0)
    grad_qkv, *ends = local_kernel(
        join_heads,
        [shape_of(F32, shard, 3 * width)]
        + [shape_of(F32, 1, shard)] * 6
        + [shape_of(F32, 1, 4 * shard)] * 2,
        [pos, head_parts],
    )
    ends = [value.reshape(-1) for value in ends]
    return (output, input_grad, grad_qkv, grad_out, grad_up, grad_down, *ends)


def layer(*arrays):
    one_document = arrays[2].shape[1] == 1
    if lax.axis_size("dp") == 8 and lax.axis_size("blk") == 4 and one_document:
        return fast_body(*arrays)
    return general_body(*arrays)


def solution(mesh):
    placed = (
        P(("dp", "blk"), None),
        P(("dp", "blk"), None),
        P("dp", None),
        P(("dp", "blk"), None),
        P(("dp", "blk"), None),
        P(("dp", "blk"), None),
        P(("dp", "blk"), None),
        P(("dp", "blk")),
        P(("dp", "blk")),
        P(("dp", "blk")),
        P(("dp", "blk")),
        P(("dp", "blk")),
        P(("dp", "blk")),
        P(("dp", "blk")),
        P(("dp", "blk")),
    )
    return jax.shard_map(
        layer,
        mesh=mesh,
        in_specs=placed,
        out_specs=(
            P(("dp", "blk"), None),
            P(("dp", "blk"), None),
            P(("dp", "blk"), None),
            P(("dp", "blk"), None),
            P(("dp", "blk"), None),
            P(("dp", "blk"), None),
            P(("dp", "blk")),
            P(("dp", "blk")),
            P(("dp", "blk")),
            P(("dp", "blk")),
            P(("dp", "blk")),
            P(("dp", "blk")),
            P(("dp", "blk")),
            P(("dp", "blk")),
        ),
        check_vma=False,
    )
```
